32 devices in a mesh: dp: 16 (over z, y, core), tensor: 2 (over x).
Axes of the slice: x: 2, y: 2, z: 4, core: 2. Of those that a mesh axis runs over, the one named last changes fastest.
Arguments:
- inputs: bfloat16 [4096, 1536], P(('dp', 'tensor')), may hold values from -6 to 6
- clip_ids: int32 [4096], P('dp'), may hold values from 0 to 2, as said below
- positions: int32 [4096], P('dp'), may hold values from 0 to 4095
- text_tokens: bfloat16 [768, 4096], P('dp'), may hold values from -6 to 6
- conditioning: bfloat16 [3, 1024], replicated, may hold values from -6 to 6
- ada_weight: bfloat16 [1024, 9216], P('dp'), may hold values from -0.1875 to 0.1875
- ada_bias: bfloat16 [9216], replicated, may hold values from -4 to 4
- first_norm_gain: bfloat16 [1536], replicated, may hold values from 0.25 to 1.75
- query_gain: bfloat16 [64], replicated, may hold values from 0.25 to 1.75
- key_gain: bfloat16 [64], replicated, may hold values from 0.25 to 1.75
- text_key_gain: bfloat16 [64], replicated, may hold values from 0.25 to 1.75
- head_gate: bfloat16 [24], replicated, may hold values from 0.19921875 to 1.5
- qkv_weight: bfloat16 [3, 1536, 1536], P(None, 'dp', 'tensor'), may hold values from -0.15625 to 0.15625
- out_weight: bfloat16 [1536, 1536], P('tensor', 'dp'), may hold values from -2.5 to 2.5
- text_kv_weight: bfloat16 [2, 4096, 1536], P(None, 'dp', 'tensor'), may hold values from -0.09375 to 0.09375
- second_norm_gain: bfloat16 [1536], replicated, may hold values from 0.25 to 1.75
- gate_up_weight: bfloat16 [2, 1536, 4096], P(None, 'dp', 'tensor'), may hold values from -0.15625 to 0.15625
- down_weight: bfloat16 [4096, 1536], P('tensor', 'dp'), may hold values from -0.09375 to 0.09375
- grad_output: bfloat16 [4096, 1536], P(('dp', 'tensor')), may hold values from -6 to 6
Outputs:
- output: bfloat16 [4096, 1536], P(('dp', 'tensor'))
- grad_inputs: float32 [4096, 1536], P(('dp', 'tensor'))
- grad_text: float32 [768, 4096], P('dp', 'tensor')
- grad_conditioning: float32 [3, 1024], replicated
- grad_ada_weight: float32 [1024, 9216], P('dp')
- grad_ada_bias: float32 [9216], replicated
- grad_first_gain: float32 [1536], replicated
- grad_query_gain: float32 [64], replicated
- grad_key_gain: float32 [64], replicated
- grad_text_key_gain: float32 [64], replicated
- grad_head_gate: float32 [24], replicated
- grad_qkv_weight: float32 [3, 1536, 1536], P(None, 'dp', 'tensor')
- grad_out_weight: float32 [1536, 1536], P('tensor', 'dp')
- grad_text_kv_weight: float32 [2, 4096, 1536], P(None, 'dp', 'tensor')
- grad_second_gain: float32 [1536], replicated
- grad_gate_up_weight: float32 [2, 1536, 4096], P(None, 'dp', 'tensor')
- grad_down_weight: float32 [4096, 1536], P('tensor', 'dp')
The draws below stay inside these ranges and needn't reach their ends.
Inputs may be any that keep to these rules, and one draw needn't show every extreme that they name: `clip_ids`: in block j of 256 rows (one index of dp), the rows of clip 0 come first, at least 128 and at most 224 of them, and all other rows belong to clip 1 + j // 8.
All inputs are finite; a program needn't handle non-finite values.
Results may differ from the reference program's by a relative error of at most 0.019.
Values may be sent and summed in bfloat16 or wider, within the bound.
No kernel may reach another device: no remote copies, remote signals or barrier semaphores. Data moves between devices by JAX's collectives and lax.ppermute only.
A program may use at most 384 MiB of HBM per device.

```python
import jax
import jax.numpy as jnp
from jax import lax

D = 1536
HEADS = 24
HS = 64
FF = 4096
TD = 4096
COND = 1024
TXT = 256
TOK_DEV = 256
CLIPS = 3
TOKENS = 4096
TEXT_ROWS = 768
N_DP = 16


def draw_clip_ids(key, part):
    key = jax.random.fold_in(key, 11)
    least = TOK_DEV // 2
    most = 7 * TOK_DEV // 8
    starts = jax.random.randint(jax.random.fold_in(key, 1), (N_DP,), least, most + 1).astype(jnp.int32)
    order = jax.random.permutation(jax.random.fold_in(key, 2), N_DP)
    starts = starts.at[order[0]].set(most)
    starts = starts.at[order[1]].set(least)
    row_index = jnp.arange(TOK_DEV, dtype=jnp.int32)
    groups = (1 + jnp.arange(N_DP, dtype=jnp.int32) // 8).astype(jnp.int32)
    labels = jnp.where(row_index[None, :] < starts[:, None], 0, groups[:, None])
    return labels.reshape(-1).astype(jnp.int32)


def set_ends(drawn, rng, smallest, top_value):
    shape = drawn.shape
    index_at = [jax.random.randint(jax.random.fold_in(rng, axis), (), 0, shape[axis]) for axis in range(len(shape))]
    drawn = drawn.at[tuple(index_at)].set(smallest)
    longest = shape.index(max(shape))
    index_at[longest] = (index_at[longest] + 1) % shape[longest]
    return drawn.at[tuple(index_at)].set(top_value)


def level_of(stream_key, extent, pieces, smallest, high):
    gain, own = 1.0, jax.random.fold_in(stream_key, 6)
    for axis_at, parts in pieces:
        steps = jnp.exp(jax.random.uniform(jax.random.fold_in(own, axis_at), (parts,), jnp.float32, smallest / len(pieces), high / len(pieces)))
        gain = gain * jnp.repeat(steps, extent[axis_at] // parts).reshape([-1 if axis == axis_at else 1 for axis in range(len(extent))])
    return gain


def scatter_about(key, shape, width, most, shards=(), held_as=jnp.bfloat16):
    factor_of = level_of(key, shape, shards, -0.22, 0.18) if shards else 1.0
    entries = jax.random.normal(key, shape, jnp.float32) * width * factor_of
    return jnp.minimum(jnp.maximum(entries, -most), most).astype(held_as)


def setup_inputs(seed: int = 0) -> dict:
    keys = jax.random.split(jax.random.key(seed), 20)
    return {
        "inputs": scatter_about(keys[0], (TOKENS, D), 1.0, 6.0, ((0, 32),)),
        "clip_ids": draw_clip_ids(jax.random.fold_in(keys[19], 71), 0),
        "positions": set_ends(jax.random.randint(keys[2], (TOKENS,), 0, 4096), jax.random.fold_in(keys[2], 1), 0, 4095).astype(jnp.int32),
        "text_tokens": scatter_about(keys[3], (TEXT_ROWS, TD), 1.0, 6.0, ((0, 16),)),
        "conditioning": scatter_about(keys[4], (CLIPS, COND), 1.0, 6.0),
        "ada_weight": scatter_about(keys[5], (COND, 6 * D), COND ** -0.5, 0.1875, ((0, 16),)),
        "ada_bias": scatter_about(keys[6], (6 * D,), 0.3, 4.0),
        "first_norm_gain": jnp.clip(1.0 + 0.15 * jax.random.normal(keys[7], (D,), jnp.float32), 0.25, 1.75).astype(jnp.bfloat16),
        "query_gain": jnp.clip(1.0 + 0.15 * jax.random.normal(keys[8], (HS,), jnp.float32), 0.25, 1.75).astype(jnp.bfloat16),
        "key_gain": jnp.clip(1.0 + 0.15 * jax.random.normal(keys[9], (HS,), jnp.float32), 0.25, 1.75).astype(jnp.bfloat16),
        "text_key_gain": jnp.clip(1.0 + 0.15 * jax.random.normal(keys[10], (HS,), jnp.float32), 0.25, 1.75).astype(jnp.bfloat16),
        "head_gate": jnp.clip(jax.random.uniform(keys[11], (HEADS,), jnp.float32, 0.19921875, 1.5), 0.19921875, 1.5).astype(jnp.bfloat16),
        "qkv_weight": scatter_about(keys[12], (3, D, D), D ** -0.5, 0.15625, ((1, 16), (2, 2))),
        "out_weight": scatter_about(keys[13], (D, D), 6 ** -0.5, 2.5, ((0, 2), (1, 16))),
        "text_kv_weight": scatter_about(keys[14], (2, TD, D), TD ** -0.5, 0.09375, ((1, 16), (2, 2))),
        "second_norm_gain": jnp.clip(1.0 + 0.15 * jax.random.normal(keys[15], (D,), jnp.float32), 0.25, 1.75).astype(jnp.bfloat16),
        "gate_up_weight": scatter_about(keys[16], (2, D, FF), D ** -0.5, 0.15625, ((1, 16), (2, 2))),
        "down_weight": scatter_about(keys[17], (FF, D), FF ** -0.5, 0.09375, ((0, 2), (1, 16))),
        "grad_output": scatter_about(keys[18], (TOKENS, D), 1.0, 6.0, ((0, 32),)),
    }


@jax.custom_vjp
def low(v):
    return lax.optimization_barrier(v.astype(jnp.bfloat16)).astype(jnp.float32)

@jax.custom_vjp
def low_back(v):
    return v

def low_keep(v):
    return (low(v), None)

def low_pass(kept, grad):
    return (grad,)

def back_keep(v):
    return (v, None)

def back_low(kept, grad):
    return (low(grad),)
low.defvjp(low_keep, low_pass)
low_back.defvjp(back_keep, back_low)

def norm_rows(values, gains):
    return values * lax.rsqrt(lax.optimization_barrier(jnp.mean(values * values, axis=-1, keepdims=True)) + 1e-06) * gains

def rotate(values, cosine_table, sine_table):
    half_size = values.shape[-1] // 2
    former = values[..., :half_size]
    latter = values[..., half_size:]
    cosine = cosine_table[:, None, :]
    sine_part = sine_table[:, None, :]
    return jnp.concatenate([former * cosine - latter * sine_part, latter * cosine + former * sine_part], axis=-1)

def rope_tables(positions):
    half_size = HS // 2
    frequency = 10000.0 ** (-(jnp.arange(half_size, dtype=jnp.float32) * 2.0 / HS))
    angles = positions.astype(jnp.float32)[:, None] * frequency[None, :]
    return (jnp.cos(angles), jnp.sin(angles))

def matmul(left, right):
    return jnp.dot(left, right, precision=lax.Precision.HIGHEST, preferred_element_type=jnp.float32)

def attend(queries, query_ids, key_heads, value_heads, key_ids, text_keys, text_values, text_ids, text_gate):
    score_scale = HS ** (-0.5)
    scores = low_back(jnp.einsum('qhd,khd->hqk', queries, key_heads, precision=lax.Precision.HIGHEST) * score_scale)
    scores = jnp.where((query_ids[:, None] == key_ids[None, :])[None], scores, -1e+30)
    weights = low(jax.nn.softmax(scores, axis=-1))
    own_part = jnp.einsum('hqk,khd->qhd', weights, value_heads, precision=lax.Precision.HIGHEST)
    text_scores = low_back(jnp.einsum('qhd,khd->hqk', queries, text_keys, precision=lax.Precision.HIGHEST) * score_scale)
    text_scores = jnp.where((query_ids[:, None] == text_ids[None, :])[None], text_scores, -1e+30)
    text_weights = low(jax.nn.softmax(text_scores, axis=-1))
    text_part = low_back(jnp.einsum('hqk,khd->qhd', text_weights, text_values, precision=lax.Precision.HIGHEST))
    return low_back(low(own_part + text_gate[None, :, None] * text_part))

def layer(inputs, text_tokens, conditioning, ada_weight, ada_bias, first_norm_gain, query_gain, key_gain, text_key_gain, head_gate, qkv_weight, out_weight, text_kv_weight, second_norm_gain, gate_up_weight, down_weight, clip_ids, positions):
    modulation = low_back(matmul(low(jax.nn.silu(conditioning)), ada_weight) + ada_bias)
    token_mod = jnp.take(modulation, clip_ids, axis=0)
    shift_one, scale_one, gate_one, shift_two, scale_two, gate_two = jnp.split(token_mod, 6, axis=1)
    normed_one = low(norm_rows(inputs, first_norm_gain) * (1.0 + scale_one) + shift_one)
    query_raw = low_back(matmul(normed_one, qkv_weight[0])).reshape(TOKENS, HEADS, HS)
    key_raw = low_back(matmul(normed_one, qkv_weight[1])).reshape(TOKENS, HEADS, HS)
    value_heads = low_back(low(matmul(normed_one, qkv_weight[2]))).reshape(TOKENS, HEADS, HS)
    cosine_table, sine_table = rope_tables(positions)
    query_heads = low_back(low(rotate(norm_rows(query_raw, query_gain), cosine_table, sine_table)))
    key_heads = low_back(low(rotate(norm_rows(key_raw, key_gain), cosine_table, sine_table)))
    text_raw = low_back(matmul(text_tokens, text_kv_weight[0])).reshape(CLIPS * TXT, HEADS, HS)
    text_keys = low_back(low(norm_rows(text_raw, text_key_gain)))
    text_values = low_back(low(matmul(text_tokens, text_kv_weight[1]))).reshape(CLIPS * TXT, HEADS, HS)
    text_ids = (jnp.arange(CLIPS * TXT, dtype=jnp.int32) // TXT).astype(jnp.int32)
    text_gate = jnp.tanh(head_gate)
    block_rows = 512
    while TOKENS % block_rows:
        block_rows //= 2
    block_count = TOKENS // block_rows
    query_blocks = query_heads.reshape(block_count, block_rows, HEADS, HS)
    id_blocks = clip_ids.reshape(block_count, block_rows)
    checked = jax.checkpoint(attend)

    def map_block(block_pair):
        return checked(block_pair[0], block_pair[1], key_heads, value_heads, clip_ids, text_keys, text_values, text_ids, text_gate)
    mixed_heads = lax.map(map_block, (query_blocks, id_blocks)).reshape(TOKENS, D)
    attn_rows = low_back(matmul(mixed_heads, out_weight))
    after_attn = inputs + gate_one * attn_rows
    normed_two = low(norm_rows(after_attn, second_norm_gain) * (1.0 + scale_two) + shift_two)
    gate_values = low_back(matmul(normed_two, gate_up_weight[0]))
    up_values = low_back(matmul(normed_two, gate_up_weight[1]))
    hidden = low(jax.nn.silu(gate_values) * up_values)
    ffn_rows = low_back(matmul(hidden, down_weight))
    return after_attn + gate_two * ffn_rows

def reference(inputs, clip_ids, positions, text_tokens, conditioning, ada_weight, ada_bias, first_norm_gain, query_gain, key_gain, text_key_gain, head_gate, qkv_weight, out_weight, text_kv_weight, second_norm_gain, gate_up_weight, down_weight, grad_output):
    floats = tuple((value.astype(jnp.float32) for value in (inputs, text_tokens, conditioning, ada_weight, ada_bias, first_norm_gain, query_gain, key_gain, text_key_gain, head_gate, qkv_weight, out_weight, text_kv_weight, second_norm_gain, gate_up_weight, down_weight)))

    def forward(*params):
        return layer(*params, clip_ids, positions)
    result, pull_back = jax.vjp(forward, *floats)
    grads = pull_back(grad_output.astype(jnp.float32))
    return (result.astype(jnp.bfloat16), grads[0], grads[1], grads[2], grads[3], grads[4], grads[5], grads[6], grads[7], grads[8], grads[9], grads[10], grads[11], grads[12], grads[13], grads[14], grads[15])
```

```python
import functools

import jax
import jax.numpy as jnp
from jax import lax
from jax.experimental import pallas as pl
from jax.experimental.pallas import tpu as pltpu
from jax.sharding import PartitionSpec as P

TXT = 256
GROUP = 8
SPLIT = 4
EPS = 1e-06
MASK = -1e4
LOW = jnp.bfloat16
FLOAT = jnp.float32
MIB = 1024 * 1024


def pick_tile(total, most):
    size = most
    while total % size:
        size //= 2
    return size


def matmul(left, right, left_dim, right_dim):
    return lax.dot_general(
        left, right, (((left_dim,), (right_dim,)), ((), ())), preferred_element_type=jnp.float32
    )


def build_keys(kv_ref, kf_ref, keys_ref, values_ref):
    lanes = lax.broadcasted_iota(jnp.int32, kv_ref.shape, 1)
    kv = kv_ref[...]
    keys_ref[...] = jnp.where(lanes < 64, kv, kf_ref[...])
    values_ref[...] = jnp.where(
        lanes < 64, jnp.where(lanes < 3, 1.0, 0.0).astype(jnp.bfloat16), kv
    )


def forward_kernel(
    chunk, q_ref, sel_ref, qf_ref, kv_ref, kf_ref, tkv_ref, tf_ref, gate_ref,
    mixed_ref, outs_ref, stats_ref, keys, values, text_keys, text_values,
):
    @pl.when(pl.program_id(1) == 0)
    def _():
        build_keys(kv_ref, kf_ref, keys, values)
        build_keys(tkv_ref, tf_ref, text_keys, text_values)

    rows = q_ref.shape[0]
    query = (matmul(q_ref[...], sel_ref[0], 1, 0) + qf_ref[...].astype(jnp.float32)).astype(
        jnp.bfloat16
    )

    def attend(key_part, value_part):
        scores = matmul(query, key_part, 1, 1)
        return matmul(jnp.exp(scores).astype(jnp.bfloat16), value_part, 1, 0)

    def step(index, total):
        part = pl.ds(pl.multiple_of(index * chunk, chunk), chunk)
        return total + attend(keys[part, :], values[part, :])

    own = lax.fori_loop(
        0, keys.shape[0] // chunk, step, jnp.zeros((rows, 128), jnp.float32), unroll=2
    )
    text_chunk = pick_tile(text_keys.shape[0], 256)

    def text_step(index, total):
        part = pl.ds(pl.multiple_of(index * text_chunk, text_chunk), text_chunk)
        return total + attend(text_keys[part, :], text_values[part, :])

    cross = lax.fori_loop(
        0, text_keys.shape[0] // text_chunk, text_step, jnp.zeros((rows, 128), jnp.float32), unroll=True
    )
    own_inverse = 1.0 / own[:, 0:1]
    cross_inverse = 1.0 / cross[:, 0:1]
    own = own * own_inverse
    cross = cross * cross_inverse
    lanes = lax.broadcasted_iota(jnp.int32, own.shape, 1)
    gate = gate_ref[0, 0:1, :]
    mixed_ref[...] = (own + gate * cross).astype(jnp.bfloat16)
    outs_ref[...] = jnp.where(lanes < 64, pltpu.roll(cross, 64, 1), own)
    stats_ref[...] = jnp.where(lanes == 0, own_inverse, cross_inverse)


def attention_forward(q, sel, qf, kv, kf, tkv, tf, gates):
    rows, width = q.shape
    heads = sel.shape[0]
    total, text_total = kv.shape[0], tkv.shape[0]
    tile = pick_tile(rows, 256)
    chunk = pick_tile(total, 512)
    head_block = lambda h, i: (i, h)
    out = jax.ShapeDtypeStruct((rows, heads * 128), jnp.float32)
    pairs = rows * heads * (total + text_total)
    return pl.pallas_call(
        functools.partial(forward_kernel, chunk),
        grid=(heads, rows // tile),
        in_specs=[
            pl.BlockSpec((tile, width), lambda h, i: (i, 0)),
            pl.BlockSpec((1, width, 128), lambda h, i: (h, 0, 0)),
            pl.BlockSpec((tile, 128), lambda h, i: (i, 0)),
            pl.BlockSpec((total, 128), lambda h, i: (0, h)),
            pl.BlockSpec((total, 128), lambda h, i: (0, 0)),
            pl.BlockSpec((text_total, 128), lambda h, i: (0, h)),
            pl.BlockSpec((text_total, 128), lambda h, i: (0, 0)),
            pl.BlockSpec((1, 8, 128), lambda h, i: (h, 0, 0)),
        ],
        out_specs=[pl.BlockSpec((tile, 128), head_block)] * 3,
        out_shape=[jax.ShapeDtypeStruct((rows, heads * 128), jnp.bfloat16), out, out],
        scratch_shapes=[
            pltpu.VMEM((total, 128), jnp.bfloat16),
            pltpu.VMEM((total, 128), jnp.bfloat16),
            pltpu.VMEM((text_total, 128), jnp.bfloat16),
            pltpu.VMEM((text_total, 128), jnp.bfloat16),
        ],
        compiler_params=pltpu.CompilerParams(vmem_limit_bytes=48 * 1024 * 1024),
        cost_estimate=pl.CostEstimate(
            flops=pairs * 512, bytes_accessed=8 * total * heads * 128, transcendentals=pairs
        ),
    )(q, sel, qf, kv, kf, tkv, tf, gates)


def backward_kernel(
    chunk, q_ref, dm_ref, sel_ref, msel_ref, qf_ref, kv_ref, kf_ref, tkv_ref, tf_ref, gate_ref,
    outs_ref, stats_ref, dq_ref, dkv_ref, dt_ref, dg_ref,
    keys, values, text_keys, text_values, acc, text_acc,
):
    tile_index = pl.program_id(1)

    @pl.when(tile_index == 0)
    def _():
        build_keys(kv_ref, kf_ref, keys, values)
        build_keys(tkv_ref, tf_ref, text_keys, text_values)
        acc[...] = jnp.zeros_like(acc)
        text_acc[...] = jnp.zeros_like(text_acc)
        dg_ref[...] = jnp.zeros_like(dg_ref)

    rows = q_ref.shape[0]
    query_wide = matmul(q_ref[...], sel_ref[0], 1, 0)
    query = (query_wide + qf_ref[...].astype(jnp.float32)).astype(jnp.bfloat16)
    query_low = query_wide.astype(jnp.bfloat16)
    grads = matmul(dm_ref[...], msel_ref[0], 1, 0)
    outs = outs_ref[...]
    lanes = lax.broadcasted_iota(jnp.int32, outs.shape, 1)
    gate = gate_ref[0, 0:1, :]
    cross_out = jnp.where(lanes < 64, 0.0, pltpu.roll(outs, 64, 1))
    dg_ref[...] += jnp.sum((grads * cross_out).reshape(rows // 8, 8, 128), axis=0)
    cross_grads = (gate * grads).astype(jnp.bfloat16).astype(jnp.float32)

    def widen(grad, out, inverse):
        delta = -jnp.sum(grad * out, axis=1, keepdims=True) * inverse
        first = delta.astype(jnp.bfloat16).astype(jnp.float32)
        second = (delta - first).astype(jnp.bfloat16).astype(jnp.float32)
        third = delta - first - second
        features = jnp.where(lanes == 0, first, jnp.where(lanes == 1, second, third))
        scaled = grad * inverse
        whole = jnp.where(lanes < 3, features, scaled).astype(jnp.bfloat16)
        return whole, scaled.astype(jnp.bfloat16)

    stats = stats_ref[...]
    own_wide, own_low = widen(grads, outs, stats[:, 0:1])
    cross_wide, cross_low = widen(cross_grads, cross_out, stats[:, 1:2])

    def attend(key_part, value_part, wide, pair):
        weights = jnp.exp(matmul(key_part, query, 1, 1))
        grad_scores = (weights * matmul(value_part, wide, 1, 1)).astype(jnp.bfloat16)
        low = weights.astype(jnp.bfloat16)
        grad_pair = matmul(jnp.concatenate([grad_scores, low], axis=1), pair, 1, 0)
        return grad_pair, matmul(grad_scores, key_part, 0, 0)

    own_pair = jnp.concatenate([query_low, own_low], axis=0)
    cross_pair = jnp.concatenate([query_low, cross_low], axis=0)

    def step(index, total):
        part = pl.ds(pl.multiple_of(index * chunk, chunk), chunk)
        grad_pair, grad_query = attend(keys[part, :], values[part, :], own_wide, own_pair)
        acc[part, :] += grad_pair
        return total + grad_query

    query_grad = lax.fori_loop(
        0, keys.shape[0] // chunk, step, jnp.zeros((rows, 128), jnp.float32), unroll=2
    )
    text_chunk = pick_tile(text_keys.shape[0], 256)

    def text_step(index, total):
        part = pl.ds(pl.multiple_of(index * text_chunk, text_chunk), text_chunk)
        grad_pair, grad_query = attend(
            text_keys[part, :], text_values[part, :], cross_wide, cross_pair
        )
        text_acc[part, :] += grad_pair
        return total + grad_query

    query_grad = lax.fori_loop(
        0, text_keys.shape[0] // text_chunk, text_step, query_grad, unroll=True
    )
    dq_ref[...] = (query_grad * 0.125).astype(jnp.bfloat16)

    @pl.when(tile_index == pl.num_programs(1) - 1)
    def _():
        dkv_ref[...] = acc[...].astype(jnp.bfloat16)
        dt_ref[...] = text_acc[...].astype(jnp.bfloat16)


def attention_backward(q, dm, sel, msel, qf, kv, kf, tkv, tf, gates, outs, stats):
    rows, width = q.shape
    heads = sel.shape[0]
    total, text_total = kv.shape[0], tkv.shape[0]
    tile = pick_tile(rows, 256)
    chunk = pick_tile(total, 512)
    low = jnp.bfloat16
    pairs = rows * heads * (total + text_total)
    return pl.pallas_call(
        functools.partial(backward_kernel, chunk),
        grid=(heads, rows // tile),
        in_specs=[
            pl.BlockSpec((tile, width), lambda h, i: (i, 0)),
            pl.BlockSpec((tile, width), lambda h, i: (i, 0)),
            pl.BlockSpec((1, width, 128), lambda h, i: (h, 0, 0)),
            pl.BlockSpec((1, width, 128), lambda h, i: (h, 0, 0)),
            pl.BlockSpec((tile, 128), lambda h, i: (i, 0)),
            pl.BlockSpec((total, 128), lambda h, i: (0, h)),
            pl.BlockSpec((total, 128), lambda h, i: (0, 0)),
            pl.BlockSpec((text_total, 128), lambda h, i: (0, h)),
            pl.BlockSpec((text_total, 128), lambda h, i: (0, 0)),
            pl.BlockSpec((1, 8, 128), lambda h, i: (h, 0, 0)),
            pl.BlockSpec((tile, 128), lambda h, i: (i, h)),
            pl.BlockSpec((tile, 128), lambda h, i: (i, h)),
        ],
        out_specs=[
            pl.BlockSpec((tile, 128), lambda h, i: (i, h)),
            pl.BlockSpec((total, 128), lambda h, i: (0, h)),
            pl.BlockSpec((text_total, 128), lambda h, i: (0, h)),
            pl.BlockSpec((8, 128), lambda h, i: (0, h)),
        ],
        out_shape=[
            jax.ShapeDtypeStruct((rows, heads * 128), low),
            jax.ShapeDtypeStruct((total, heads * 128), low),
            jax.ShapeDtypeStruct((text_total, heads * 128), low),
            jax.ShapeDtypeStruct((8, heads * 128), jnp.float32),
        ],
        scratch_shapes=[
            pltpu.VMEM((total, 128), low),
            pltpu.VMEM((total, 128), low),
            pltpu.VMEM((text_total, 128), low),
            pltpu.VMEM((text_total, 128), low),
            pltpu.VMEM((total, 128), jnp.float32),
            pltpu.VMEM((text_total, 128), jnp.float32),
        ],
        compiler_params=pltpu.CompilerParams(vmem_limit_bytes=56 * 1024 * 1024),
        cost_estimate=pl.CostEstimate(
            flops=pairs * 1280, bytes_accessed=12 * total * heads * 128, transcendentals=pairs
        ),
    )(q, dm, sel, msel, qf, kv, kf, tkv, tf, gates, outs, stats)


def half_means(values, lanes):
    low = jnp.sum(jnp.where(lanes < 64, values, 0.0), axis=1, keepdims=True)
    high = jnp.sum(jnp.where(lanes < 64, 0.0, values), axis=1, keepdims=True)
    return jnp.where(lanes < 64, low, high) * (1.0 / 64.0)


def swap_halves(values, lanes):
    return jnp.where(
        lax.rem(lanes, 64) < 32, pltpu.roll(values, 96, 1), pltpu.roll(values, 32, 1)
    )


def placed_at(groups, head, upper):
    values = groups[head // 2]
    return values if (head % 2 == 1) == upper else pltpu.roll(values, 64, 1)


def rope_forward_kernel(heads, qkv_ref, cos_ref, sin_ref, gains_ref, out_ref):
    width = heads * 64
    cosine, sine = cos_ref[...], sin_ref[...]
    lanes = lax.broadcasted_iota(jnp.int32, cosine.shape, 1)

    def turned(start, gain):
        groups = []
        for index in range(heads // 2):
            raw = qkv_ref[:, start + 128 * index : start + 128 * index + 128]
            normed = raw * lax.rsqrt(half_means(raw * raw, lanes) + EPS) * gain
            groups.append(normed * cosine + swap_halves(normed, lanes) * sine)
        return groups

    queries = turned(0, gains_ref[0:1, :])
    keys = turned(width, gains_ref[1:2, :])
    values = [
        qkv_ref[:, 2 * width + 128 * index : 2 * width + 128 * index + 128]
        for index in range(heads // 2)
    ]
    each = heads // SPLIT
    for part in range(SPLIT):
        first = part * each
        blocks = []
        for pair in range((each + 1) // 2):
            left = placed_at(queries, first + 2 * pair, False)
            if 2 * pair + 1 < each:
                right = placed_at(queries, first + 2 * pair + 1, True)
            else:
                right = jnp.zeros_like(left)
            blocks.append(jnp.where(lanes < 64, left, right))
        for head in range(first, first + each):
            blocks.append(
                jnp.where(lanes < 64, placed_at(keys, head, False), placed_at(values, head, True))
            )
        for index, block in enumerate(blocks):
            out_ref[part, :, 128 * index : 128 * index + 128] = block.astype(LOW)


def rope_forward(qkv, cosine, sine, gains, heads):
    rows = qkv.shape[0]
    each = heads // SPLIT
    width = 128 * ((each + 1) // 2 + each)
    return pl.pallas_call(
        functools.partial(rope_forward_kernel, heads),
        out_shape=jax.ShapeDtypeStruct((SPLIT, rows, width), LOW),
        compiler_params=pltpu.CompilerParams(vmem_limit_bytes=32 * MIB),
    )(qkv, cosine, sine, gains)


def rope_backward_kernel(heads, part_ref, qkv_ref, cos_ref, sin_ref, gains_ref, out_ref, sums_ref):
    width = heads * 64
    each = heads // SPLIT
    query_blocks = (each + 1) // 2
    cosine, sine = cos_ref[...], sin_ref[...]
    lanes = lax.broadcasted_iota(jnp.int32, cosine.shape, 1)

    def found(kind, head):
        part, index = head // each, head % each
        if kind == 0:
            block, upper = index // 2, index % 2 == 1
        else:
            block, upper = query_blocks + index, kind == 2
        values = part_ref[part, :, 128 * block : 128 * block + 128].astype(FLOAT)
        return values if upper == (head % 2 == 1) else pltpu.roll(values, 64, 1)

    def joined(kind, index):
        return jnp.where(lanes < 64, found(kind, 2 * index), found(kind, 2 * index + 1))

    for kind in range(2):
        gain = gains_ref[kind : kind + 1, :]
        total = jnp.zeros((1, 128), FLOAT)
        for index in range(heads // 2):
            spot = kind * width + 128 * index
            raw = qkv_ref[:, spot : spot + 128]
            inverse = lax.rsqrt(half_means(raw * raw, lanes) + EPS)
            unit = raw * inverse
            grad = joined(kind, index)
            back = grad * cosine - swap_halves(grad, lanes) * sine
            total = total + jnp.sum(back * unit, axis=0, keepdims=True)
            scaled = back * gain
            raw_grad = inverse * (scaled - unit * half_means(scaled * unit, lanes))
            out_ref[:, spot : spot + 128] = raw_grad.astype(LOW)
        sums_ref[kind : kind + 1, :] = total
    sums_ref[2:8, :] = jnp.zeros((6, 128), FLOAT)
    for index in range(heads // 2):
        spot = 2 * width + 128 * index
        out_ref[:, spot : spot + 128] = joined(2, index).astype(LOW)


def rope_backward(parts, qkv, cosine, sine, gains, heads):
    return pl.pallas_call(
        functools.partial(rope_backward_kernel, heads),
        out_shape=[
            jax.ShapeDtypeStruct(qkv.shape, LOW),
            jax.ShapeDtypeStruct((8, 128), FLOAT),
        ],
        compiler_params=pltpu.CompilerParams(vmem_limit_bytes=32 * MIB),
    )(parts, qkv, cosine, sine, gains)


def outer_kernel(left_ref, right_ref, out_ref):
    out_ref[...] = matmul(left_ref[0], right_ref[...], 1, 0).astype(LOW)


def outer_products(left, right, bounds, tile):
    depth, columns = left.shape[1], right.shape[1]
    return pl.pallas_call(
        outer_kernel,
        grid=(columns // tile,),
        in_specs=[
            pl.BlockSpec(
                (1, depth, left.shape[2]), lambda i: (jnp.where(i < bounds // tile, 0, 1), 0, 0)
            ),
            pl.BlockSpec((right.shape[0], tile), lambda i: (0, i)),
        ],
        out_specs=pl.BlockSpec((depth, tile), lambda i: (0, i)),
        out_shape=jax.ShapeDtypeStruct((depth, columns), LOW),
        compiler_params=pltpu.CompilerParams(vmem_limit_bytes=40 * MIB),
        cost_estimate=pl.CostEstimate(
            flops=2 * depth * columns * right.shape[0],
            bytes_accessed=2 * depth * columns,
            transcendentals=0,
        ),
    )(left, right)


def dot_float(left, right):
    return jnp.dot(left, right, preferred_element_type=FLOAT)


def dot_turned(left, right):
    return matmul(left, right, 1, 1)


def norm_rows(values, gains):
    return values * lax.rsqrt(jnp.mean(values * values, axis=-1, keepdims=True) + EPS) * gains


def modulated(values, gains, shifts, scales):
    return norm_rows(values, gains) * (1.0 + scales) + shifts


def swapped(values):
    return lax.ppermute(values, "tensor", [(0, 1), (1, 0)])


def both_rows(values):
    return jnp.concatenate([values, swapped(values)], axis=0)


def own_rows(partial):
    rows = partial.shape[0] // 2
    return partial[:rows] + swapped(partial[rows:].astype(LOW)).astype(FLOAT)


def shards(
    inputs,
    clip_ids,
    positions,
    text_tokens,
    conditioning,
    ada_weight,
    ada_bias,
    first_norm_gain,
    query_gain,
    key_gain,
    text_key_gain,
    head_gate,
    qkv_weight,
    out_weight,
    text_kv_weight,
    second_norm_gain,
    gate_up_weight,
    down_weight,
    grad_output,
):
    dp = lax.axis_size("dp")
    near = dp // SPLIT
    bits = [near >> (step + 1) for step in range(near.bit_length() - 1)]
    tensor_index = lax.axis_index("tensor")
    dp_index = lax.axis_index("dp")
    far_index, near_index = dp_index // near, dp_index % near
    row_count, width = inputs.shape
    token_count = clip_ids.shape[0]
    head_size = query_gain.shape[0]
    local_width = qkv_weight.shape[2]
    heads = local_width // head_size
    each = heads // SPLIT
    part_width = each * head_size
    clip_count = conditioning.shape[0]
    hidden_count = gate_up_weight.shape[2]
    weight_rows = qkv_weight.shape[1]

    def flip(values, bit):
        return lax.ppermute(values, "dp", [(j, j ^ bit) for j in range(dp)])

    def shift(values, steps):
        pairs = [(j, ((j // near + steps) % SPLIT) * near + j % near) for j in range(dp)]
        return lax.ppermute(values, "dp", pairs)

    def sum_dp(values):
        step = 1
        while step < dp:
            values = values + flip(values, step)
            step *= 2
        return values

    def spread(values):
        for bit in bits:
            values = jnp.concatenate([values, flip(values, bit)], axis=0)
        return values

    def collect(values):
        for bit in reversed(bits):
            half = values.shape[0] // 2
            values = values[:half].astype(FLOAT) + flip(
                values[half:].astype(LOW), bit
            ).astype(FLOAT)
        return values

    def pick(stacked, index):
        return lax.dynamic_index_in_dim(stacked, index, 0, keepdims=False)

    def send_parts(stacked):
        out = [pick(stacked, far_index)]
        for steps in range(1, SPLIT):
            out.append(shift(pick(stacked, (far_index + steps) % SPLIT), steps))
        return out

    def in_place(parts):
        doubled = jnp.stack(parts + parts)
        return lax.dynamic_slice_in_dim(doubled, (SPLIT - far_index) % SPLIT, SPLIT, 0)

    def return_parts(slots):
        return in_place(
            [slots[0]] + [shift(slots[steps], -steps) for steps in range(1, SPLIT)]
        )

    qkv_full = lax.all_gather(
        qkv_weight.transpose(1, 0, 2).reshape(weight_rows, 3 * local_width),
        "dp",
        axis=0,
        tiled=True,
    )
    rest_shard = jnp.concatenate(
        [out_weight.T, gate_up_weight[0], gate_up_weight[1], down_weight.T], axis=1
    )
    rest_shard, qkv_full = lax.optimization_barrier((rest_shard, qkv_full))
    rest_full = lax.all_gather(rest_shard, "dp", axis=0, tiled=True)
    out_full = rest_full[:, :local_width]
    gate_up_full = rest_full[:, local_width : local_width + 2 * hidden_count]
    down_full = rest_full[:, local_width + 2 * hidden_count :]

    cond_float = conditioning.astype(FLOAT)
    silu_cond = jax.nn.silu(cond_float).astype(LOW)
    cond_rows = ada_weight.shape[0]
    silu_slice = lax.dynamic_slice_in_dim(silu_cond, dp_index * cond_rows, cond_rows, axis=1)
    first_rows = jnp.sum((clip_ids == 0).astype(FLOAT))
    spots = jnp.arange(ada_weight.shape[1], dtype=jnp.int32)
    mod_part = jnp.concatenate(
        [
            dot_float(silu_slice, ada_weight),
            jnp.where(spots == dp_index, first_rows, 0.0)[None],
        ],
        axis=0,
    )
    mod_sum = sum_dp(mod_part)
    modulation = mod_sum[:clip_count] + ada_bias.astype(FLOAT)
    counts = mod_sum[clip_count, :dp].astype(jnp.int32)

    own_ids = lax.dynamic_slice_in_dim(clip_ids, tensor_index * row_count, row_count)
    row_positions = jnp.where(
        tensor_index == 0, positions, jnp.roll(positions, row_count)
    )
    other_clip = jnp.max(clip_ids)
    first_clip = (own_ids == 0)[:, None]
    mod_rows = jnp.where(
        first_clip,
        modulation[0:1],
        lax.dynamic_slice_in_dim(modulation, other_clip, 1, 0),
    )
    shift_one, scale_one, gate_one, shift_two, scale_two, gate_two = jnp.split(mod_rows, 6, axis=1)

    input_rows = inputs.astype(FLOAT)
    first_gain = first_norm_gain.astype(FLOAT)
    normed_all = both_rows(modulated(input_rows, first_gain, shift_one, scale_one).astype(LOW))
    grad_two = grad_output.astype(FLOAT)
    grad_ffn = both_rows((gate_two * grad_two).astype(LOW))

    half_size = head_size // 2
    frequency = 10000.0 ** (-(jnp.arange(half_size, dtype=FLOAT) * 2.0 / head_size))
    angles = row_positions.astype(FLOAT)[:, None] * frequency[None, :]
    cosine = jnp.cos(angles)
    sine = jnp.sin(angles)
    cosine = jnp.concatenate([cosine] * 4, axis=1)
    sine = jnp.concatenate([-sine, sine, -sine, sine], axis=1)
    gains = jnp.stack([jnp.tile(query_gain, 2), jnp.tile(key_gain, 2)]).astype(FLOAT)
    gains = jnp.concatenate([gains, jnp.zeros((6, 128), FLOAT)], axis=0)

    flips = []
    for order in range(near):
        mask = 0
        for place, bit in enumerate(bits):
            if order >> place & 1:
                mask |= bit
        flips.append(mask)

    text_rows = text_tokens.shape[0]
    group_rows = text_rows * SPLIT
    text_columns = lax.all_to_all(text_tokens, "dp", split_axis=1, concat_axis=0, tiled=True)
    text_groups = text_columns.reshape(near, group_rows, text_columns.shape[1])
    text_near = jnp.concatenate([pick(text_groups, near_index ^ mask) for mask in flips], axis=0)
    text_weight = (
        text_kv_weight.reshape(2, -1, SPLIT, part_width)
        .transpose(1, 2, 0, 3)
        .reshape(-1, 2 * local_width)
    )
    text_sum = collect(dot_float(text_near, text_weight))
    text_parts = text_sum.astype(LOW).reshape(group_rows, SPLIT, 2 * part_width).transpose(1, 0, 2)
    text_raw = sum(part.astype(FLOAT) for part in send_parts(text_parts))
    ky_gain = text_key_gain.astype(FLOAT)
    text_key_raw = text_raw[:, :part_width].reshape(group_rows, each, head_size)
    text_key = norm_rows(text_key_raw, ky_gain).astype(LOW)
    text_value = text_raw[:, part_width:].astype(LOW).reshape(group_rows, each, head_size)
    text_pairs = spread(
        jnp.concatenate([text_key, text_value], axis=-1).reshape(group_rows, 2 * part_width)
    )

    lanes = jnp.arange(128, dtype=jnp.int32)[None, :]
    text_groups_at = jnp.stack([near_index ^ mask for mask in flips])
    text_clip = (
        text_groups_at[:, None] * group_rows + jnp.arange(group_rows, dtype=jnp.int32)[None, :]
    ).reshape(-1) // TXT
    text_features = (lanes == 64 + text_clip[:, None]).astype(LOW)
    block_at = jnp.stack(
        [
            ((far_index - steps) % SPLIT) * near + (near_index ^ mask)
            for mask in flips
            for steps in range(SPLIT)
        ]
    )
    block_count = jnp.sum(
        jnp.where(block_at[:, None] == jnp.arange(dp, dtype=jnp.int32)[None, :], counts[None, :], 0),
        axis=1,
    )
    row_at = (jnp.arange(token_count, dtype=jnp.int32) + tensor_index * row_count) % token_count
    key_clip = jnp.where(
        row_at[None, :] < block_count[:, None], 0, 1 + block_at[:, None] // GROUP
    ).reshape(-1)
    key_features = (lanes == 64 + key_clip[:, None]).astype(LOW)
    group_tokens = SPLIT * token_count
    query_clip = key_clip[:group_tokens, None]
    query_features = jnp.where(
        (lanes >= 64) & (lanes < 64 + clip_count) & (lanes != 64 + query_clip), MASK, 0.0
    ).astype(LOW)
    query_width = 128 * ((each + 1) // 2)
    head_at = jnp.arange(each, dtype=jnp.int32)[:, None, None]
    lane_at = jnp.arange(128, dtype=jnp.int32)[None, None, :]

    def selector(rows, offset, scale):
        row = jnp.arange(rows, dtype=jnp.int32)[None, :, None]
        hit = (row == head_at * head_size + lane_at - offset) & (lane_at >= offset)
        hit = hit & (lane_at < offset + head_size)
        return jnp.where(hit, scale, 0.0).astype(LOW)

    query_select = selector(query_width, 0, head_size**-0.5)
    mixed_select = selector(query_width, 64, 1.0)
    gate_heads = jnp.tanh(
        lax.dynamic_slice_in_dim(
            head_gate.astype(FLOAT), tensor_index * heads + far_index * each, each
        )
    )
    gate_lanes = jnp.broadcast_to(gate_heads[:, None, None], (each, 8, 128))

    qkv_raw = dot_float(normed_all, qkv_full)
    head_parts = send_parts(rope_forward(qkv_raw, cosine, sine, gains, heads))
    arrived = jnp.concatenate(head_parts, axis=0)
    queries = arrived[:, :query_width]
    pairs = spread(arrived[:, query_width:])
    mixed_wide, head_outs, head_stats = attention_forward(
        queries,
        query_select,
        query_features,
        pairs,
        key_features,
        text_pairs,
        text_features,
        gate_lanes,
    )
    mixed_slots = mixed_wide.reshape(SPLIT, token_count, each, 128)[..., 64:].reshape(
        SPLIT, token_count, part_width
    )
    mixed = (
        return_parts([mixed_slots[index] for index in range(SPLIT)])
        .transpose(1, 0, 2)
        .reshape(token_count, local_width)
    )
    attn_rows = own_rows(dot_turned(mixed, out_full))
    after_attn = input_rows + gate_one * attn_rows
    second_gain = second_norm_gain.astype(FLOAT)
    normed_two_all = both_rows(modulated(after_attn, second_gain, shift_two, scale_two).astype(LOW))
    gate_up = dot_float(normed_two_all, gate_up_full)
    gate_values, up_values = gate_up[:, :hidden_count], gate_up[:, hidden_count:]
    sigmoid_gate = jax.nn.sigmoid(gate_values)
    hidden_low = (gate_values * sigmoid_gate * up_values).astype(LOW)
    ffn_rows = own_rows(dot_turned(hidden_low, down_full))
    output = (after_attn + gate_two * ffn_rows).astype(LOW)
    grad_gate_two = grad_two * ffn_rows
    grad_hidden = dot_float(grad_ffn, down_full)
    grad_gate_low = (
        grad_hidden * up_values * sigmoid_gate * (1.0 + gate_values * (1.0 - sigmoid_gate))
    ).astype(LOW)
    grad_up_low = (grad_hidden * gate_values * sigmoid_gate).astype(LOW)
    grad_gate_up = jnp.concatenate([grad_gate_low, grad_up_low], axis=1)
    feed_grads = outer_products(
        jnp.stack([normed_two_all.T, grad_ffn.T]),
        jnp.concatenate([grad_gate_up, hidden_low], axis=1),
        2 * hidden_count,
        512,
    )
    feed_shard = lax.psum_scatter(feed_grads, "dp", scatter_dimension=0, tiled=True).astype(FLOAT)
    grad_normed_two = own_rows(dot_turned(grad_gate_up, gate_up_full))
    _, pull_two = jax.vjp(modulated, after_attn, second_gain, shift_two, scale_two)
    back_two, grad_second_gain, grad_shift_two, grad_scale_two = pull_two(grad_normed_two)
    grad_after = grad_two + back_two
    grad_attn = both_rows((gate_one * grad_after).astype(LOW))
    grad_gate_one = grad_after * attn_rows
    grad_mixed = dot_float(grad_attn, out_full).astype(LOW)
    grad_mixed_parts = send_parts(
        grad_mixed.reshape(token_count, SPLIT, part_width).transpose(1, 0, 2)
    )
    query_grad, pair_grads, text_grads, gate_sums = attention_backward(
        queries,
        jnp.pad(
            jnp.concatenate(grad_mixed_parts, axis=0), ((0, 0), (0, query_width - part_width))
        ),
        query_select,
        mixed_select,
        query_features,
        pairs,
        key_features,
        text_pairs,
        text_features,
        gate_lanes,
        head_outs,
        head_stats,
    )
    pair_sum = collect(pair_grads).astype(LOW)
    query_packed = query_grad.reshape(group_tokens, each, 128)[..., :64].reshape(
        group_tokens, part_width
    )
    back_slots = jnp.concatenate(
        [
            query_packed,
            jnp.zeros((group_tokens, query_width - part_width), LOW),
            pair_sum,
        ],
        axis=1,
    ).reshape(SPLIT, token_count, -1)
    back_parts = return_parts([back_slots[index] for index in range(SPLIT)])
    qkv_grad, gain_sums = rope_backward(back_parts, qkv_raw, cosine, sine, gains, heads)
    grad_normed_one = own_rows(dot_turned(qkv_grad, qkv_full))
    attention_grads = outer_products(
        jnp.stack([normed_all.T, grad_attn.T]),
        jnp.concatenate([qkv_grad, mixed], axis=1),
        3 * local_width,
        local_width,
    )
    attention_shard = lax.psum_scatter(
        attention_grads, "dp", scatter_dimension=0, tiled=True
    ).astype(FLOAT)

    text_grad_sum = collect(text_grads).reshape(group_rows, each, 2 * head_size)
    text_key_low = text_grad_sum[..., :head_size].astype(LOW).astype(FLOAT)
    _, pull_text = jax.vjp(norm_rows, text_key_raw, ky_gain)
    text_raw_grad, grad_ky_gain = pull_text(text_key_low)
    text_low = jnp.concatenate(
        [
            text_raw_grad.astype(LOW).reshape(group_rows, part_width),
            text_grad_sum[..., head_size:].astype(LOW).reshape(group_rows, part_width),
        ],
        axis=1,
    )
    text_all = spread(
        in_place([text_low] + [shift(text_low, -steps) for steps in range(1, SPLIT)])
        .transpose(1, 0, 2)
        .reshape(group_rows, 2 * local_width)
    )
    grad_text_kv = (
        matmul(text_near, text_all, 0, 0)
        .reshape(-1, SPLIT, 2, part_width)
        .transpose(2, 0, 1, 3)
        .reshape(2, -1, local_width)
    )
    grad_text_part = dot_turned(text_all, text_weight).astype(LOW)
    grad_text_pair = grad_text_part.astype(FLOAT) + swapped(grad_text_part).astype(FLOAT)
    grad_text_groups = grad_text_pair.astype(LOW).reshape(near, group_rows, -1)
    orders = jnp.arange(near, dtype=jnp.int32)
    flip_at = jnp.array(flips, jnp.int32)
    grad_text_rows = jnp.concatenate(
        [
            pick(grad_text_groups, jnp.sum(jnp.where(flip_at == near_index ^ group, orders, 0)))
            for group in range(near)
        ],
        axis=0,
    )
    grad_text_all = lax.all_to_all(grad_text_rows, "dp", split_axis=0, concat_axis=1, tiled=True)
    half_text = text_tokens.shape[1] // 2
    grad_text = lax.dynamic_slice_in_dim(
        grad_text_all, tensor_index * half_text, half_text, 1
    ).astype(FLOAT)

    _, pull_one = jax.vjp(modulated, input_rows, first_gain, shift_one, scale_one)
    back_one, grad_first_gain, grad_shift_one, grad_scale_one = pull_one(grad_normed_one)
    grad_inputs = grad_after + back_one
    clip_at = jnp.arange(clip_count, dtype=jnp.int32)[:, None]

    def clip_sums(values):
        first_sum = jnp.sum(jnp.where(first_clip, values, 0.0), axis=0)[None]
        other_sum = jnp.sum(jnp.where(first_clip, 0.0, values), axis=0)[None]
        return jnp.where(clip_at == 0, first_sum, jnp.where(clip_at == other_clip, other_sum, 0.0))

    mod_grads = jnp.concatenate(
        [
            clip_sums(values)
            for values in (
                grad_shift_one,
                grad_scale_one,
                grad_gate_one,
                grad_shift_two,
                grad_scale_two,
                grad_gate_two,
            )
        ],
        axis=1,
    )
    head_sums = (1.0 - gate_heads * gate_heads) * jnp.sum(
        gate_sums.reshape(8, each, 128), axis=(0, 2)
    )
    head_row = lax.dynamic_update_slice_in_dim(
        jnp.zeros((head_gate.shape[0],), FLOAT),
        head_sums,
        tensor_index * heads + far_index * each,
        0,
    )
    gain_halves = gain_sums[:2, :head_size] + gain_sums[:2, head_size:]
    small = jnp.concatenate(
        [grad_first_gain, grad_second_gain, gain_halves.reshape(-1), grad_ky_gain, head_row]
    )
    small_row = jnp.concatenate([small, jnp.zeros((mod_grads.shape[1] - small.shape[0],), FLOAT)])
    grad_sums = jnp.concatenate([mod_grads, small_row[None]], axis=0)
    grad_sums = sum_dp(grad_sums + swapped(grad_sums))
    grad_mod_low = grad_sums[:clip_count].astype(LOW)
    sums = grad_sums[clip_count]
    first_gain_sum = sums[:width]
    second_gain_sum = sums[width : 2 * width]
    at = 2 * width
    q_gain_sum = sums[at : at + head_size]
    k_gain_sum = sums[at + head_size : at + 2 * head_size]
    ky_gain_sum = sums[at + 2 * head_size : at + 3 * head_size]
    gate_sum = sums[at + 3 * head_size : at + 3 * head_size + head_gate.shape[0]]
    grad_ada_bias = jnp.sum(grad_mod_low.astype(FLOAT), axis=0)
    grad_ada = matmul(silu_slice, grad_mod_low, 0, 0)
    cond_part = lax.dynamic_update_slice_in_dim(
        jnp.zeros(cond_float.shape, FLOAT),
        dot_turned(grad_mod_low, ada_weight),
        dp_index * cond_rows,
        1,
    )
    cond_sigmoid = jax.nn.sigmoid(cond_float)
    grad_conditioning = (
        sum_dp(cond_part) * cond_sigmoid * (1.0 + cond_float * (1.0 - cond_sigmoid))
    )
    qkv_shard = (
        attention_shard[:, : 3 * local_width]
        .reshape(weight_rows, 3, local_width)
        .transpose(1, 0, 2)
    )
    out_shard = attention_shard[:, 3 * local_width :].T
    gate_up_shard = jnp.stack(
        [feed_shard[:, :hidden_count], feed_shard[:, hidden_count : 2 * hidden_count]]
    )
    down_shard = feed_shard[:, 2 * hidden_count :].T
    return (
        output,
        grad_inputs,
        grad_text,
        grad_conditioning,
        grad_ada,
        grad_ada_bias,
        first_gain_sum,
        q_gain_sum,
        k_gain_sum,
        ky_gain_sum,
        gate_sum,
        qkv_shard,
        out_shard,
        grad_text_kv,
        second_gain_sum,
        gate_up_shard,
        down_shard,
    )


def solution(mesh):
    placed = (
        P(("dp", "tensor"), None),
        P("dp"),
        P("dp"),
        P("dp", None),
        P(),
        P("dp", None),
        P(),
        P(),
        P(),
        P(),
        P(),
        P(),
        P(None, "dp", "tensor"),
        P("tensor", "dp"),
        P(None, "dp", "tensor"),
        P(),
        P(None, "dp", "tensor"),
        P("tensor", "dp"),
        P(("dp", "tensor"), None),
    )
    return jax.shard_map(
        shards,
        mesh=mesh,
        in_specs=placed,
        out_specs=(
            P(("dp", "tensor"), None),
            P(("dp", "tensor"), None),
            P("dp", "tensor"),
            P(),
            P("dp", None),
            P(),
            P(),
            P(),
            P(),
            P(),
            P(),
            P(None, "dp", "tensor"),
            P("tensor", "dp"),
            P(None, "dp", "tensor"),
            P(),
            P(None, "dp", "tensor"),
            P("tensor", "dp"),
        ),
        check_vma=False,
    )
```

```python
import functools

import jax
import jax.numpy as jnp
from jax import lax
from jax.experimental import pallas as pl
from jax.experimental.pallas import tpu as pltpu
from jax.sharding import PartitionSpec as P

TXT = 256
GROUP = 8
SPLIT = 4
EPS = 1e-06
MASK = -1e4
LOW = jnp.bfloat16
FLOAT = jnp.float32
MIB = 1024 * 1024
SMALL = pl.CostEstimate(flops=1024, bytes_accessed=1024, transcendentals=0)


def pick_tile(total, most):
    size = most
    while total % size:
        size //= 2
    return size


def matmul(left, right, left_dim, right_dim):
    return lax.dot_general(
        left, right, (((left_dim,), (right_dim,)), ((), ())), preferred_element_type=jnp.float32
    )


def build_keys(kv_ref, kf_ref, keys_ref, values_ref):
    lanes = lax.broadcasted_iota(jnp.int32, kv_ref.shape, 1)
    kv = kv_ref[...]
    keys_ref[...] = jnp.where(lanes < 64, kv, kf_ref[...])
    values_ref[...] = jnp.where(
        lanes < 64, jnp.where(lanes < 3, 1.0, 0.0).astype(jnp.bfloat16), kv
    )


def forward_kernel(
    chunk, q_ref, sel_ref, qf_ref, kv_ref, kf_ref, tkv_ref, tf_ref, gate_ref,
    mixed_ref, outs_ref, stats_ref, keys, values, text_keys, text_values,
):
    @pl.when(pl.program_id(1) == 0)
    def _():
        build_keys(kv_ref, kf_ref, keys, values)
        build_keys(tkv_ref, tf_ref, text_keys, text_values)

    rows = q_ref.shape[0]
    query = (matmul(q_ref[...], sel_ref[0], 1, 0) + qf_ref[...].astype(jnp.float32)).astype(
        jnp.bfloat16
    )

    def attend(key_part, value_part):
        scores = matmul(query, key_part, 1, 1)
        return matmul(jnp.exp(scores).astype(jnp.bfloat16), value_part, 1, 0)

    def step(index, total):
        part = pl.ds(pl.multiple_of(index * chunk, chunk), chunk)
        return total + attend(keys[part, :], values[part, :])

    own = lax.fori_loop(
        0, keys.shape[0] // chunk, step, jnp.zeros((rows, 128), jnp.float32), unroll=2
    )
    text_chunk = pick_tile(text_keys.shape[0], 256)

    def text_step(index, total):
        part = pl.ds(pl.multiple_of(index * text_chunk, text_chunk), text_chunk)
        return total + attend(text_keys[part, :], text_values[part, :])

    cross = lax.fori_loop(
        0, text_keys.shape[0] // text_chunk, text_step, jnp.zeros((rows, 128), jnp.float32), unroll=True
    )
    own_inverse = 1.0 / own[:, 0:1]
    cross_inverse = 1.0 / cross[:, 0:1]
    own = own * own_inverse
    cross = cross * cross_inverse
    lanes = lax.broadcasted_iota(jnp.int32, own.shape, 1)
    gate = gate_ref[0, 0:1, :]
    mixed_ref[...] = (own + gate * cross).astype(jnp.bfloat16)
    outs_ref[...] = jnp.where(lanes < 64, pltpu.roll(cross, 64, 1), own)
    stats_ref[...] = jnp.where(lanes == 0, own_inverse, cross_inverse)


def attention_forward(q, sel, qf, kv, kf, tkv, tf, gates):
    rows, width = q.shape
    heads = sel.shape[0]
    total, text_total = kv.shape[0], tkv.shape[0]
    tile = pick_tile(rows, 256)
    chunk = pick_tile(total, 512)
    head_block = lambda h, i: (i, h)
    out = jax.ShapeDtypeStruct((rows, heads * 128), jnp.float32)
    return pl.pallas_call(
        functools.partial(forward_kernel, chunk),
        grid=(heads, rows // tile),
        in_specs=[
            pl.BlockSpec((tile, width), lambda h, i: (i, 0)),
            pl.BlockSpec((1, width, 128), lambda h, i: (h, 0, 0)),
            pl.BlockSpec((tile, 128), lambda h, i: (i, 0)),
            pl.BlockSpec((total, 128), lambda h, i: (0, h)),
            pl.BlockSpec((total, 128), lambda h, i: (0, 0)),
            pl.BlockSpec((text_total, 128), lambda h, i: (0, h)),
            pl.BlockSpec((text_total, 128), lambda h, i: (0, 0)),
            pl.BlockSpec((1, 8, 128), lambda h, i: (h, 0, 0)),
        ],
        out_specs=[pl.BlockSpec((tile, 128), head_block)] * 3,
        out_shape=[jax.ShapeDtypeStruct((rows, heads * 128), jnp.bfloat16), out, out],
        scratch_shapes=[
            pltpu.VMEM((total, 128), jnp.bfloat16),
            pltpu.VMEM((total, 128), jnp.bfloat16),
            pltpu.VMEM((text_total, 128), jnp.bfloat16),
            pltpu.VMEM((text_total, 128), jnp.bfloat16),
        ],
        compiler_params=pltpu.CompilerParams(vmem_limit_bytes=48 * 1024 * 1024),
        cost_estimate=SMALL,
    )(q, sel, qf, kv, kf, tkv, tf, gates)


def backward_kernel(
    chunk, q_ref, dm_ref, sel_ref, msel_ref, qf_ref, kv_ref, kf_ref, tkv_ref, tf_ref, gate_ref,
    outs_ref, stats_ref, dq_ref, dkv_ref, dt_ref, dg_ref,
    keys, values, text_keys, text_values, acc, text_acc,
):
    tile_index = pl.program_id(1)

    @pl.when(tile_index == 0)
    def _():
        build_keys(kv_ref, kf_ref, keys, values)
        build_keys(tkv_ref, tf_ref, text_keys, text_values)
        acc[...] = jnp.zeros_like(acc)
        text_acc[...] = jnp.zeros_like(text_acc)
        dg_ref[...] = jnp.zeros_like(dg_ref)

    rows = q_ref.shape[0]
    query_wide = matmul(q_ref[...], sel_ref[0], 1, 0)
    query = (query_wide + qf_ref[...].astype(jnp.float32)).astype(jnp.bfloat16)
    query_low = query_wide.astype(jnp.bfloat16)
    grads = matmul(dm_ref[...], msel_ref[0], 1, 0)
    outs = outs_ref[...]
    lanes = lax.broadcasted_iota(jnp.int32, outs.shape, 1)
    gate = gate_ref[0, 0:1, :]
    cross_out = jnp.where(lanes < 64, 0.0, pltpu.roll(outs, 64, 1))
    dg_ref[...] += jnp.sum((grads * cross_out).reshape(rows // 8, 8, 128), axis=0)
    cross_grads = (gate * grads).astype(jnp.bfloat16).astype(jnp.float32)

    def widen(grad, out, inverse):
        delta = -jnp.sum(grad * out, axis=1, keepdims=True) * inverse
        first = delta.astype(jnp.bfloat16).astype(jnp.float32)
        second = (delta - first).astype(jnp.bfloat16).astype(jnp.float32)
        third = delta - first - second
        features = jnp.where(lanes == 0, first, jnp.where(lanes == 1, second, third))
        scaled = grad * inverse
        whole = jnp.where(lanes < 3, features, scaled).astype(jnp.bfloat16)
        return whole, scaled.astype(jnp.bfloat16)

    stats = stats_ref[...]
    own_wide, own_low = widen(grads, outs, stats[:, 0:1])
    cross_wide, cross_low = widen(cross_grads, cross_out, stats[:, 1:2])

    def attend(key_part, value_part, wide, pair):
        weights = jnp.exp(matmul(key_part, query, 1, 1))
        grad_scores = (weights * matmul(value_part, wide, 1, 1)).astype(jnp.bfloat16)
        low = weights.astype(jnp.bfloat16)
        grad_pair = matmul(jnp.concatenate([grad_scores, low], axis=1), pair, 1, 0)
        return grad_pair, matmul(grad_scores, key_part, 0, 0)

    own_pair = jnp.concatenate([query_low, own_low], axis=0)
    cross_pair = jnp.concatenate([query_low, cross_low], axis=0)

    def step(index, total):
        part = pl.ds(pl.multiple_of(index * chunk, chunk), chunk)
        grad_pair, grad_query = attend(keys[part, :], values[part, :], own_wide, own_pair)
        acc[part, :] += grad_pair
        return total + grad_query

    query_grad = lax.fori_loop(
        0, keys.shape[0] // chunk, step, jnp.zeros((rows, 128), jnp.float32), unroll=2
    )
    text_chunk = pick_tile(text_keys.shape[0], 256)

    def text_step(index, total):
        part = pl.ds(pl.multiple_of(index * text_chunk, text_chunk), text_chunk)
        grad_pair, grad_query = attend(
            text_keys[part, :], text_values[part, :], cross_wide, cross_pair
        )
        text_acc[part, :] += grad_pair
        return total + grad_query

    query_grad = lax.fori_loop(
        0, text_keys.shape[0] // text_chunk, text_step, query_grad, unroll=True
    )
    dq_ref[...] = (query_grad * 0.125).astype(jnp.bfloat16)

    @pl.when(tile_index == pl.num_programs(1) - 1)
    def _():
        dkv_ref[...] = acc[...].astype(jnp.bfloat16)
        dt_ref[...] = text_acc[...].astype(jnp.bfloat16)


def attention_backward(q, dm, sel, msel, qf, kv, kf, tkv, tf, gates, outs, stats):
    rows, width = q.shape
    heads = sel.shape[0]
    total, text_total = kv.shape[0], tkv.shape[0]
    tile = pick_tile(rows, 256)
    chunk = pick_tile(total, 512)
    low = jnp.bfloat16
    return pl.pallas_call(
        functools.partial(backward_kernel, chunk),
        grid=(heads, rows // tile),
        in_specs=[
            pl.BlockSpec((tile, width), lambda h, i: (i, 0)),
            pl.BlockSpec((tile, width), lambda h, i: (i, 0)),
            pl.BlockSpec((1, width, 128), lambda h, i: (h, 0, 0)),
            pl.BlockSpec((1, width, 128), lambda h, i: (h, 0, 0)),
            pl.BlockSpec((tile, 128), lambda h, i: (i, 0)),
            pl.BlockSpec((total, 128), lambda h, i: (0, h)),
            pl.BlockSpec((total, 128), lambda h, i: (0, 0)),
            pl.BlockSpec((text_total, 128), lambda h, i: (0, h)),
            pl.BlockSpec((text_total, 128), lambda h, i: (0, 0)),
            pl.BlockSpec((1, 8, 128), lambda h, i: (h, 0, 0)),
            pl.BlockSpec((tile, 128), lambda h, i: (i, h)),
            pl.BlockSpec((tile, 128), lambda h, i: (i, h)),
        ],
        out_specs=[
            pl.BlockSpec((tile, 128), lambda h, i: (i, h)),
            pl.BlockSpec((total, 128), lambda h, i: (0, h)),
            pl.BlockSpec((text_total, 128), lambda h, i: (0, h)),
            pl.BlockSpec((8, 128), lambda h, i: (0, h)),
        ],
        out_shape=[
            jax.ShapeDtypeStruct((rows, heads * 128), low),
            jax.ShapeDtypeStruct((total, heads * 128), low),
            jax.ShapeDtypeStruct((text_total, heads * 128), low),
            jax.ShapeDtypeStruct((8, heads * 128), jnp.float32),
        ],
        scratch_shapes=[
            pltpu.VMEM((total, 128), low),
            pltpu.VMEM((total, 128), low),
            pltpu.VMEM((text_total, 128), low),
            pltpu.VMEM((text_total, 128), low),
            pltpu.VMEM((total, 128), jnp.float32),
            pltpu.VMEM((text_total, 128), jnp.float32),
        ],
        compiler_params=pltpu.CompilerParams(vmem_limit_bytes=56 * 1024 * 1024),
        cost_estimate=SMALL,
    )(q, dm, sel, msel, qf, kv, kf, tkv, tf, gates, outs, stats)


def half_means(values, lanes):
    low = jnp.sum(jnp.where(lanes < 64, values, 0.0), axis=1, keepdims=True)
    high = jnp.sum(jnp.where(lanes < 64, 0.0, values), axis=1, keepdims=True)
    return jnp.where(lanes < 64, low, high) * (1.0 / 64.0)


def swap_halves(values, lanes):
    return jnp.where(
        lax.rem(lanes, 64) < 32, pltpu.roll(values, 96, 1), pltpu.roll(values, 32, 1)
    )


def placed_at(groups, head, upper):
    values = groups[head // 2]
    return values if (head % 2 == 1) == upper else pltpu.roll(values, 64, 1)


def rope_forward_kernel(heads, qkv_ref, cos_ref, sin_ref, gains_ref, out_ref):
    width = heads * 64
    cosine, sine = cos_ref[...], sin_ref[...]
    lanes = lax.broadcasted_iota(jnp.int32, cosine.shape, 1)

    def turned(start, gain):
        groups = []
        for index in range(heads // 2):
            raw = qkv_ref[:, start + 128 * index : start + 128 * index + 128]
            normed = raw * lax.rsqrt(half_means(raw * raw, lanes) + EPS) * gain
            groups.append(normed * cosine + swap_halves(normed, lanes) * sine)
        return groups

    queries = turned(0, gains_ref[0:1, :])
    keys = turned(width, gains_ref[1:2, :])
    values = [
        qkv_ref[:, 2 * width + 128 * index : 2 * width + 128 * index + 128]
        for index in range(heads // 2)
    ]
    each = heads // SPLIT
    for part in range(SPLIT):
        first = part * each
        blocks = []
        for pair in range((each + 1) // 2):
            left = placed_at(queries, first + 2 * pair, False)
            if 2 * pair + 1 < each:
                right = placed_at(queries, first + 2 * pair + 1, True)
            else:
                right = jnp.zeros_like(left)
            blocks.append(jnp.where(lanes < 64, left, right))
        for head in range(first, first + each):
            blocks.append(
                jnp.where(lanes < 64, placed_at(keys, head, False), placed_at(values, head, True))
            )
        for index, block in enumerate(blocks):
            out_ref[part, :, 128 * index : 128 * index + 128] = block.astype(LOW)


def rope_forward(qkv, cosine, sine, gains, heads):
    rows = qkv.shape[0]
    each = heads // SPLIT
    width = 128 * ((each + 1) // 2 + each)
    return pl.pallas_call(
        functools.partial(rope_forward_kernel, heads),
        out_shape=jax.ShapeDtypeStruct((SPLIT, rows, width), LOW),
        compiler_params=pltpu.CompilerParams(vmem_limit_bytes=32 * MIB),
    )(qkv, cosine, sine, gains)


def rope_backward_kernel(heads, part_ref, qkv_ref, cos_ref, sin_ref, gains_ref, out_ref, sums_ref):
    width = heads * 64
    each = heads // SPLIT
    query_blocks = (each + 1) // 2
    cosine, sine = cos_ref[...], sin_ref[...]
    lanes = lax.broadcasted_iota(jnp.int32, cosine.shape, 1)

    def found(kind, head):
        part, index = head // each, head % each
        if kind == 0:
            block, upper = index // 2, index % 2 == 1
        else:
            block, upper = query_blocks + index, kind == 2
        values = part_ref[part, :, 128 * block : 128 * block + 128].astype(FLOAT)
        return values if upper == (head % 2 == 1) else pltpu.roll(values, 64, 1)

    def joined(kind, index):
        return jnp.where(lanes < 64, found(kind, 2 * index), found(kind, 2 * index + 1))

    for kind in range(2):
        gain = gains_ref[kind : kind + 1, :]
        total = jnp.zeros((1, 128), FLOAT)
        for index in range(heads // 2):
            spot = kind * width + 128 * index
            raw = qkv_ref[:, spot : spot + 128]
            inverse = lax.rsqrt(half_means(raw * raw, lanes) + EPS)
            unit = raw * inverse
            grad = joined(kind, index)
            back = grad * cosine - swap_halves(grad, lanes) * sine
            total = total + jnp.sum(back * unit, axis=0, keepdims=True)
            scaled = back * gain
            raw_grad = inverse * (scaled - unit * half_means(scaled * unit, lanes))
            out_ref[:, spot : spot + 128] = raw_grad.astype(LOW)
        sums_ref[kind : kind + 1, :] = total
    sums_ref[2:8, :] = jnp.zeros((6, 128), FLOAT)
    for index in range(heads // 2):
        spot = 2 * width + 128 * index
        out_ref[:, spot : spot + 128] = joined(2, index).astype(LOW)


def rope_backward(parts, qkv, cosine, sine, gains, heads):
    return pl.pallas_call(
        functools.partial(rope_backward_kernel, heads),
        out_shape=[
            jax.ShapeDtypeStruct(qkv.shape, LOW),
            jax.ShapeDtypeStruct((8, 128), FLOAT),
        ],
        compiler_params=pltpu.CompilerParams(vmem_limit_bytes=32 * MIB),
    )(parts, qkv, cosine, sine, gains)


def outer_kernel(left_ref, *refs):
    out_ref = refs[-1]
    total = None
    for index, right_ref in enumerate(refs[:-1]):
        rows = right_ref.shape[0]
        term = matmul(left_ref[:, rows * index : rows * index + rows], right_ref[...], 1, 0)
        total = term if total is None else total + term
    out_ref[...] = total.astype(LOW)


def outer_products(left, rights, tile):
    depth = left.shape[0]
    rows, columns = rights[0].shape
    return pl.pallas_call(
        outer_kernel,
        grid=(columns // tile,),
        in_specs=[pl.BlockSpec(left.shape, lambda i: (0, 0))]
        + [pl.BlockSpec((rows, tile), lambda i: (0, i)) for _ in rights],
        out_specs=pl.BlockSpec((depth, tile), lambda i: (0, i)),
        out_shape=jax.ShapeDtypeStruct((depth, columns), LOW),
        compiler_params=pltpu.CompilerParams(vmem_limit_bytes=40 * MIB),
        cost_estimate=SMALL,
    )(left, *rights)


def tie(*values):
    return lax.optimization_barrier(values)


def dot_float(left, right):
    return jnp.dot(left, right, preferred_element_type=FLOAT)


def dot_turned(left, right):
    return matmul(left, right, 1, 1)


def norm_rows(values, gains):
    return values * lax.rsqrt(jnp.mean(values * values, axis=-1, keepdims=True) + EPS) * gains


def modulated(values, gains, shifts, scales):
    return norm_rows(values, gains) * (1.0 + scales) + shifts


def swapped(values):
    return lax.ppermute(values, "tensor", [(0, 1), (1, 0)])


def both_rows(values):
    return jnp.concatenate([values, swapped(values)], axis=0)


def own_rows(partial):
    rows = partial.shape[0] // 2
    return partial[:rows] + swapped(partial[rows:].astype(LOW)).astype(FLOAT)


def shards(
    inputs,
    clip_ids,
    positions,
    text_tokens,
    conditioning,
    ada_weight,
    ada_bias,
    first_norm_gain,
    query_gain,
    key_gain,
    text_key_gain,
    head_gate,
    qkv_weight,
    out_weight,
    text_kv_weight,
    second_norm_gain,
    gate_up_weight,
    down_weight,
    grad_output,
):
    dp = lax.axis_size("dp")
    near = dp // SPLIT
    bits = [near >> (step + 1) for step in range(near.bit_length() - 1)]
    tensor_index = lax.axis_index("tensor")
    dp_index = lax.axis_index("dp")
    far_index, near_index = dp_index // near, dp_index % near
    row_count, width = inputs.shape
    token_count = clip_ids.shape[0]
    head_size = query_gain.shape[0]
    local_width = qkv_weight.shape[2]
    heads = local_width // head_size
    each = heads // SPLIT
    part_width = each * head_size
    clip_count = conditioning.shape[0]
    hidden_count = gate_up_weight.shape[2]
    weight_rows = qkv_weight.shape[1]

    def flip(values, bit):
        return lax.ppermute(values, "dp", [(j, j ^ bit) for j in range(dp)])

    def shift(values, steps):
        pairs = [(j, ((j // near + steps) % SPLIT) * near + j % near) for j in range(dp)]
        return lax.ppermute(values, "dp", pairs)

    def sum_dp(values):
        step = 1
        while step < dp:
            values = values + flip(values, step)
            step *= 2
        return values

    def spread(values):
        for bit in bits:
            values = jnp.concatenate([values, flip(values, bit)], axis=0)
        return values

    def spread_list(values):
        values = [values]
        for bit in bits:
            values = values + [flip(value, bit) for value in values]
        return values

    def collect(values):
        for bit in reversed(bits):
            half = values.shape[0] // 2
            values = values[:half].astype(FLOAT) + flip(
                values[half:].astype(LOW), bit
            ).astype(FLOAT)
        return values

    def pick(stacked, index):
        return lax.dynamic_index_in_dim(stacked, index, 0, keepdims=False)

    def send_parts(stacked):
        out = [pick(stacked, far_index)]
        for steps in range(1, SPLIT):
            out.append(shift(pick(stacked, (far_index + steps) % SPLIT), steps))
        return out

    def in_place(parts):
        doubled = jnp.stack(parts + parts)
        return lax.dynamic_slice_in_dim(doubled, (SPLIT - far_index) % SPLIT, SPLIT, 0)

    def return_parts(slots):
        return in_place(
            [slots[0]] + [shift(slots[steps], -steps) for steps in range(1, SPLIT)]
        )

    flips = []
    for order in range(near):
        mask = 0
        for place, bit in enumerate(bits):
            if order >> place & 1:
                mask |= bit
        flips.append(mask)

    def own_columns(values):
        blocks = (
            values.T.reshape(SPLIT, near, weight_rows, token_count)
            .transpose(1, 0, 2, 3)
            .reshape(near, SPLIT * weight_rows, token_count)
        )
        parts = [pick(blocks, near_index ^ mask) for mask in flips]
        return jnp.concatenate(
            [part if mask == 0 else flip(part, mask) for part, mask in zip(parts, flips)], axis=1
        )

    def weight_shard(partial):
        parts = send_parts(partial.reshape(SPLIT, weight_rows, -1))
        return sum(part.astype(FLOAT) for part in parts)

    qkv_full = lax.all_gather(
        qkv_weight.transpose(1, 0, 2).reshape(weight_rows, 3 * local_width),
        "dp",
        axis=0,
        tiled=True,
    )
    cond_float = conditioning.astype(FLOAT)
    silu_cond = jax.nn.silu(cond_float).astype(LOW)
    cond_rows = ada_weight.shape[0]
    silu_slice = lax.dynamic_slice_in_dim(silu_cond, dp_index * cond_rows, cond_rows, axis=1)
    first_rows = jnp.sum((clip_ids == 0).astype(FLOAT))
    spots = jnp.arange(ada_weight.shape[1], dtype=jnp.int32)
    early = 2 * width
    early_part = jnp.concatenate(
        [
            dot_float(silu_slice, ada_weight[:, :early]),
            jnp.where(spots[:early] == dp_index, first_rows, 0.0)[None],
        ],
        axis=0,
    )
    early_sum = sum_dp(early_part)
    bias = ada_bias.astype(FLOAT)
    early_mod = early_sum[:clip_count] + bias[:early]
    counts = early_sum[clip_count, :dp].astype(jnp.int32)

    own_ids = lax.dynamic_slice_in_dim(clip_ids, tensor_index * row_count, row_count)
    row_positions = jnp.where(
        tensor_index == 0, positions, jnp.roll(positions, row_count)
    )
    other_clip = jnp.max(clip_ids)
    first_clip = (own_ids == 0)[:, None]

    def mod_blocks(modulation):
        rows = jnp.where(
            first_clip,
            modulation[0:1],
            lax.dynamic_slice_in_dim(modulation, other_clip, 1, 0),
        )
        return jnp.split(rows, rows.shape[1] // width, axis=1)

    shift_one, scale_one = mod_blocks(early_mod)
    input_rows = inputs.astype(FLOAT)
    first_gain = first_norm_gain.astype(FLOAT)
    normed_one = modulated(input_rows, first_gain, shift_one, scale_one).astype(LOW)
    normed_one, text_tokens, silu_late = tie(normed_one, text_tokens, silu_slice)
    normed_all = both_rows(normed_one)
    late_sum = sum_dp(dot_float(silu_late, ada_weight[:, early:]))

    half_size = head_size // 2
    frequency = 10000.0 ** (-(jnp.arange(half_size, dtype=FLOAT) * 2.0 / head_size))
    angles = row_positions.astype(FLOAT)[:, None] * frequency[None, :]
    cosine = jnp.cos(angles)
    sine = jnp.sin(angles)
    cosine = jnp.concatenate([cosine] * 4, axis=1)
    sine = jnp.concatenate([-sine, sine, -sine, sine], axis=1)
    gains = jnp.stack([jnp.tile(query_gain, 2), jnp.tile(key_gain, 2)]).astype(FLOAT)
    gains = jnp.concatenate([gains, jnp.zeros((6, 128), FLOAT)], axis=0)

    text_rows = text_tokens.shape[0]
    group_rows = text_rows * SPLIT
    text_columns = lax.all_to_all(text_tokens, "dp", split_axis=1, concat_axis=0, tiled=True)
    text_groups = text_columns.reshape(near, group_rows, text_columns.shape[1])
    text_near = jnp.concatenate([pick(text_groups, near_index ^ mask) for mask in flips], axis=0)
    text_weight = (
        text_kv_weight.reshape(2, -1, SPLIT, part_width)
        .transpose(1, 2, 0, 3)
        .reshape(-1, 2 * local_width)
    )
    text_sum = collect(dot_float(text_near, text_weight))
    text_parts = text_sum.astype(LOW).reshape(group_rows, SPLIT, 2 * part_width).transpose(1, 0, 2)
    out_part, qkv_full, normed_all, text_parts, late_sum = tie(
        out_weight.T, qkv_full, normed_all, text_parts, late_sum
    )
    out_full = lax.all_gather(out_part, "dp", axis=0, tiled=True)
    text_raw = sum(part.astype(FLOAT) for part in send_parts(text_parts))
    ky_gain = text_key_gain.astype(FLOAT)
    text_key_raw = text_raw[:, :part_width].reshape(group_rows, each, head_size)
    text_key = norm_rows(text_key_raw, ky_gain).astype(LOW)
    text_value = text_raw[:, part_width:].astype(LOW).reshape(group_rows, each, head_size)
    text_pairs = spread(
        jnp.concatenate([text_key, text_value], axis=-1).reshape(group_rows, 2 * part_width)
    )

    lanes = jnp.arange(128, dtype=jnp.int32)[None, :]
    text_groups_at = jnp.stack([near_index ^ mask for mask in flips])
    text_clip = (
        text_groups_at[:, None] * group_rows + jnp.arange(group_rows, dtype=jnp.int32)[None, :]
    ).reshape(-1) // TXT
    text_features = (lanes == 64 + text_clip[:, None]).astype(LOW)
    block_at = jnp.stack(
        [
            ((far_index - steps) % SPLIT) * near + (near_index ^ mask)
            for mask in flips
            for steps in range(SPLIT)
        ]
    )
    block_count = jnp.sum(
        jnp.where(block_at[:, None] == jnp.arange(dp, dtype=jnp.int32)[None, :], counts[None, :], 0),
        axis=1,
    )
    row_at = (jnp.arange(token_count, dtype=jnp.int32) + tensor_index * row_count) % token_count
    key_clip = jnp.where(
        row_at[None, :] < block_count[:, None], 0, 1 + block_at[:, None] // GROUP
    ).reshape(-1)
    key_features = (lanes == 64 + key_clip[:, None]).astype(LOW)
    group_tokens = SPLIT * token_count
    query_clip = key_clip[:group_tokens, None]
    query_features = jnp.where(
        (lanes >= 64) & (lanes < 64 + clip_count) & (lanes != 64 + query_clip), MASK, 0.0
    ).astype(LOW)
    query_width = 128 * ((each + 1) // 2)
    head_at = jnp.arange(each, dtype=jnp.int32)[:, None, None]
    lane_at = jnp.arange(128, dtype=jnp.int32)[None, None, :]

    def selector(rows, offset, scale):
        row = jnp.arange(rows, dtype=jnp.int32)[None, :, None]
        hit = (row == head_at * head_size + lane_at - offset) & (lane_at >= offset)
        hit = hit & (lane_at < offset + head_size)
        return jnp.where(hit, scale, 0.0).astype(LOW)

    query_select = selector(query_width, 0, head_size**-0.5)
    mixed_select = selector(query_width, 64, 1.0)
    gate_heads = jnp.tanh(
        lax.dynamic_slice_in_dim(
            head_gate.astype(FLOAT), tensor_index * heads + far_index * each, each
        )
    )
    gate_lanes = jnp.broadcast_to(gate_heads[:, None, None], (each, 8, 128))

    qkv_raw = dot_float(normed_all, qkv_full)
    gate_one, shift_two, scale_two, gate_two = mod_blocks(late_sum + bias[early:])
    grad_two = grad_output.astype(FLOAT)
    grad_ffn = both_rows((gate_two * grad_two).astype(LOW))
    head_parts = send_parts(rope_forward(qkv_raw, cosine, sine, gains, heads))
    arrived = jnp.concatenate(head_parts, axis=0)
    feed_weights, arrived = tie(
        jnp.concatenate([gate_up_weight[0], gate_up_weight[1], down_weight.T], axis=1), arrived
    )
    queries = arrived[:, :query_width]
    pairs = spread(arrived[:, query_width:])
    feed_full = lax.all_gather(feed_weights, "dp", axis=0, tiled=True)
    gate_up_full = feed_full[:, : 2 * hidden_count]
    down_full = feed_full[:, 2 * hidden_count :]
    mixed_wide, head_outs, head_stats = attention_forward(
        queries,
        query_select,
        query_features,
        pairs,
        key_features,
        text_pairs,
        text_features,
        gate_lanes,
    )
    mixed_slots = mixed_wide.reshape(SPLIT, token_count, each, 128)[..., 64:].reshape(
        SPLIT, token_count, part_width
    )
    mixed = (
        return_parts([mixed_slots[index] for index in range(SPLIT)])
        .transpose(1, 0, 2)
        .reshape(token_count, local_width)
    )
    mixed_all = spread_list(mixed)
    normed_columns = own_columns(normed_all)
    attn_rows = own_rows(dot_turned(mixed, out_full))
    after_attn = input_rows + gate_one * attn_rows
    second_gain = second_norm_gain.astype(FLOAT)
    normed_two_all = both_rows(modulated(after_attn, second_gain, shift_two, scale_two).astype(LOW))
    gate_up = dot_float(normed_two_all, gate_up_full)
    gate_values, up_values = gate_up[:, :hidden_count], gate_up[:, hidden_count:]
    sigmoid_gate = jax.nn.sigmoid(gate_values)
    hidden_low = (gate_values * sigmoid_gate * up_values).astype(LOW)
    down_grads = outer_products(grad_ffn.T, [hidden_low], 512)
    hidden_low, down_grads = tie(hidden_low, down_grads)
    down_low = lax.psum_scatter(down_grads, "dp", scatter_dimension=0, tiled=True)
    ffn_rows = own_rows(dot_turned(hidden_low, down_full))
    output = (after_attn + gate_two * ffn_rows).astype(LOW)
    grad_gate_two = grad_two * ffn_rows
    grad_hidden = dot_float(grad_ffn, down_full)
    grad_gate_low = (
        grad_hidden * up_values * sigmoid_gate * (1.0 + gate_values * (1.0 - sigmoid_gate))
    ).astype(LOW)
    grad_up_low = (grad_hidden * gate_values * sigmoid_gate).astype(LOW)
    grad_gate_up = jnp.concatenate([grad_gate_low, grad_up_low], axis=1)
    gate_up_grads = outer_products(normed_two_all.T, [grad_gate_up], 512)
    grad_normed_two = own_rows(dot_turned(grad_gate_up, gate_up_full))
    _, pull_two = jax.vjp(modulated, after_attn, second_gain, shift_two, scale_two)
    back_two, grad_second_gain, grad_shift_two, grad_scale_two = pull_two(grad_normed_two)
    grad_after = grad_two + back_two
    grad_attn = both_rows((gate_one * grad_after).astype(LOW))
    grad_gate_one = grad_after * attn_rows
    out_partial = outer_products(own_columns(grad_attn), mixed_all, local_width)
    grad_mixed = dot_float(grad_attn, out_full).astype(LOW)
    grad_mixed_parts = send_parts(
        grad_mixed.reshape(token_count, SPLIT, part_width).transpose(1, 0, 2)
    )
    grad_mixed_slots = jnp.pad(
        jnp.concatenate(grad_mixed_parts, axis=0), ((0, 0), (0, query_width - part_width))
    )
    grad_mixed_slots, gate_up_grads, out_partial, normed_columns = tie(
        grad_mixed_slots, gate_up_grads, out_partial, normed_columns
    )
    gate_up_low = lax.psum_scatter(gate_up_grads, "dp", scatter_dimension=0, tiled=True)
    out_shard = weight_shard(out_partial)
    query_grad, pair_grads, text_grads, gate_sums = attention_backward(
        queries,
        grad_mixed_slots,
        query_select,
        mixed_select,
        query_features,
        pairs,
        key_features,
        text_pairs,
        text_features,
        gate_lanes,
        head_outs,
        head_stats,
    )
    clip_at = jnp.arange(clip_count, dtype=jnp.int32)[:, None]

    def clip_sums(values):
        first_sum = jnp.sum(jnp.where(first_clip, values, 0.0), axis=0)[None]
        other_sum = jnp.sum(jnp.where(first_clip, 0.0, values), axis=0)[None]
        return jnp.where(clip_at == 0, first_sum, jnp.where(clip_at == other_clip, other_sum, 0.0))

    def pair_sums(blocks, gains_row):
        wide = jnp.concatenate([clip_sums(values) for values in blocks], axis=1)
        gains_row = jnp.concatenate(
            [gains_row, jnp.zeros((wide.shape[1] - gains_row.shape[0],), FLOAT)]
        )
        wide = jnp.concatenate([wide, gains_row[None]], axis=0)
        return wide + swapped(wide)

    late_pairs = pair_sums(
        (grad_gate_one, grad_shift_two, grad_scale_two, grad_gate_two), grad_second_gain
    )

    pair_sum = collect(pair_grads).astype(LOW)
    pair_sum, text_grads, late_pairs = tie(pair_sum, text_grads, late_pairs)
    late_total = sum_dp(late_pairs)
    late_grads = late_total[:clip_count].astype(LOW)
    second_gain_sum = late_total[clip_count, :width]
    query_packed = query_grad.reshape(group_tokens, each, 128)[..., :64].reshape(
        group_tokens, part_width
    )
    back_slots = jnp.concatenate(
        [
            query_packed,
            jnp.zeros((group_tokens, query_width - part_width), LOW),
            pair_sum,
        ],
        axis=1,
    ).reshape(SPLIT, token_count, -1)
    back_parts = return_parts([back_slots[index] for index in range(SPLIT)])
    text_grad_sum = collect(text_grads).reshape(group_rows, each, 2 * head_size)
    text_key_low = text_grad_sum[..., :head_size].astype(LOW).astype(FLOAT)
    _, pull_text = jax.vjp(norm_rows, text_key_raw, ky_gain)
    text_raw_grad, grad_ky_gain = pull_text(text_key_low)
    text_low = jnp.concatenate(
        [
            text_raw_grad.astype(LOW).reshape(group_rows, part_width),
            text_grad_sum[..., head_size:].astype(LOW).reshape(group_rows, part_width),
        ],
        axis=1,
    )
    back_parts, text_low, late_grads = tie(back_parts, text_low, late_grads)
    qkv_grad, gain_sums = rope_backward(back_parts, qkv_raw, cosine, sine, gains, heads)
    qkv_partial = outer_products(normed_columns, spread_list(qkv_grad), local_width)
    grad_normed_one = own_rows(dot_turned(qkv_grad, qkv_full))
    _, pull_one = jax.vjp(modulated, input_rows, first_gain, shift_one, scale_one)
    back_one, grad_first_gain, grad_shift_one, grad_scale_one = pull_one(grad_normed_one)
    grad_inputs = grad_after + back_one
    head_sums = (1.0 - gate_heads * gate_heads) * jnp.sum(
        gate_sums.reshape(8, each, 128), axis=(0, 2)
    )
    head_row = lax.dynamic_update_slice_in_dim(
        jnp.zeros((head_gate.shape[0],), FLOAT),
        head_sums,
        tensor_index * heads + far_index * each,
        0,
    )
    gain_halves = gain_sums[:2, :head_size] + gain_sums[:2, head_size:]
    early_pairs = pair_sums(
        (grad_shift_one, grad_scale_one),
        jnp.concatenate([grad_first_gain, gain_halves.reshape(-1), grad_ky_gain, head_row]),
    )
    text_wide = (
        in_place([text_low] + [shift(text_low, -steps) for steps in range(1, SPLIT)])
        .transpose(1, 0, 2)
        .reshape(group_rows, 2 * local_width)
    )
    early_pairs, text_wide, qkv_partial = tie(early_pairs, text_wide, qkv_partial)
    qkv_shard = weight_shard(qkv_partial)
    early_total = sum_dp(early_pairs)
    early_grads, sums = early_total[:clip_count].astype(LOW), early_total[clip_count]
    grad_mod_low = jnp.concatenate([early_grads, late_grads], axis=1)
    first_gain_sum = sums[:width]
    at = width
    q_gain_sum = sums[at : at + head_size]
    k_gain_sum = sums[at + head_size : at + 2 * head_size]
    ky_gain_sum = sums[at + 2 * head_size : at + 3 * head_size]
    gate_sum = sums[at + 3 * head_size : at + 3 * head_size + head_gate.shape[0]]
    text_all = spread(text_wide)
    grad_text_kv = (
        matmul(text_near, text_all, 0, 0)
        .reshape(-1, SPLIT, 2, part_width)
        .transpose(2, 0, 1, 3)
        .reshape(2, -1, local_width)
    )
    grad_text_part = dot_turned(text_all, text_weight).astype(LOW)
    grad_text_pair = grad_text_part.astype(FLOAT) + swapped(grad_text_part).astype(FLOAT)
    grad_text_groups = grad_text_pair.astype(LOW).reshape(near, group_rows, -1)
    orders = jnp.arange(near, dtype=jnp.int32)
    flip_at = jnp.array(flips, jnp.int32)
    grad_text_rows = jnp.concatenate(
        [
            pick(grad_text_groups, jnp.sum(jnp.where(flip_at == near_index ^ group, orders, 0)))
            for group in range(near)
        ],
        axis=0,
    )
    grad_text_all = lax.all_to_all(grad_text_rows, "dp", split_axis=0, concat_axis=1, tiled=True)
    half_text = text_tokens.shape[1] // 2
    grad_text = lax.dynamic_slice_in_dim(
        grad_text_all, tensor_index * half_text, half_text, 1
    ).astype(FLOAT)
    grad_ada_bias = jnp.sum(grad_mod_low.astype(FLOAT), axis=0)
    grad_ada = matmul(silu_slice, grad_mod_low, 0, 0)
    cond_part = lax.dynamic_update_slice_in_dim(
        jnp.zeros(cond_float.shape, FLOAT),
        dot_turned(grad_mod_low, ada_weight),
        dp_index * cond_rows,
        1,
    )
    cond_sigmoid = jax.nn.sigmoid(cond_float)
    grad_conditioning = (
        sum_dp(cond_part) * cond_sigmoid * (1.0 + cond_float * (1.0 - cond_sigmoid))
    )
    qkv_shard = qkv_shard.reshape(weight_rows, 3, local_width).transpose(1, 0, 2)
    gate_up_low = gate_up_low.astype(FLOAT)
    gate_up_shard = jnp.stack([gate_up_low[:, :hidden_count], gate_up_low[:, hidden_count:]])
    down_shard = down_low.astype(FLOAT)
    return (
        output,
        grad_inputs,
        grad_text,
        grad_conditioning,
        grad_ada,
        grad_ada_bias,
        first_gain_sum,
        q_gain_sum,
        k_gain_sum,
        ky_gain_sum,
        gate_sum,
        qkv_shard,
        out_shard.T,
        grad_text_kv,
        second_gain_sum,
        gate_up_shard,
        down_shard.T,
    )


def solution(mesh):
    placed = (
        P(("dp", "tensor"), None),
        P("dp"),
        P("dp"),
        P("dp", None),
        P(),
        P("dp", None),
        P(),
        P(),
        P(),
        P(),
        P(),
        P(),
        P(None, "dp", "tensor"),
        P("tensor", "dp"),
        P(None, "dp", "tensor"),
        P(),
        P(None, "dp", "tensor"),
        P("tensor", "dp"),
        P(("dp", "tensor"), None),
    )
    return jax.shard_map(
        shards,
        mesh=mesh,
        in_specs=placed,
        out_specs=(
            P(("dp", "tensor"), None),
            P(("dp", "tensor"), None),
            P("dp", "tensor"),
            P(),
            P("dp", None),
            P(),
            P(),
            P(),
            P(),
            P(),
            P(),
            P(None, "dp", "tensor"),
            P("tensor", "dp"),
            P(None, "dp", "tensor"),
            P(),
            P(None, "dp", "tensor"),
            P("tensor", "dp"),
        ),
        check_vma=False,
    )
```

```python
import functools

import jax
import jax.numpy as jnp
from jax import lax
from jax.experimental import pallas as pl
from jax.experimental.pallas import tpu as pltpu
from jax.sharding import PartitionSpec as P

TXT = 256
GROUP = 8
SPLIT = 4
EPS = 1e-06
MASK = -1e4
FORWARD_SLOTS = 4
BACKWARD_SLOTS = 4
LOW = jnp.bfloat16
FLOAT = jnp.float32
MIB = 1024 * 1024
SMALL = pl.CostEstimate(flops=1024, bytes_accessed=1024, transcendentals=0)


def pick_tile(total, most):
    size = most
    while total % size:
        size //= 2
    return size


def matmul(left, right, left_dim, right_dim):
    return lax.dot_general(
        left, right, (((left_dim,), (right_dim,)), ((), ())), preferred_element_type=jnp.float32
    )


def lane_ids(shape):
    return lax.broadcasted_iota(jnp.int32, shape, len(shape) - 1)


def turn(values):
    return pltpu.roll(values, 64, 1)


def fold_low(values):
    half = values.shape[0] // 2
    top, bottom = values[:half], turn(values)[half:]
    return jnp.where(lane_ids(top.shape) < 64, top, bottom).astype(LOW)


def fold_high(values):
    half = values.shape[0] // 2
    top, bottom = turn(values)[:half], values[half:]
    return jnp.where(lane_ids(top.shape) < 64, top, bottom).astype(LOW)


def unfold_low(packed):
    wide = packed.astype(FLOAT)
    return jnp.concatenate([wide, turn(wide)], axis=0)


def unfold_high(packed):
    wide = packed.astype(FLOAT)
    return jnp.concatenate([turn(wide), wide], axis=0)


def build_pair(pair, features, spot, keys, values):
    lanes = lane_ids(pair.shape)
    rows = pl.ds(spot, pair.shape[0])
    keys[rows, :] = jnp.where(lanes < 64, pair, features)
    values[rows, :] = jnp.where(
        lanes < 64, jnp.where(lanes < 3, 1.0, 0.0).astype(LOW), pair
    )


def build_inputs(head, near_refs, query_ref, qf_ref, kf_ref, tf_ref, queries, keys, values, text_keys, text_values):
    rows = query_ref.shape[0]
    queries[...] = query_ref[...] + qf_ref[...]
    each = pl.cdiv(near_refs[0].shape[0], rows) - 1
    text_rows = (near_refs[0].shape[0] - each * rows) // each
    for index, ref in enumerate(near_refs):
        spot = pl.ds(pl.multiple_of(head * rows, rows), rows)
        build_pair(ref[spot, :], kf_ref[rows * index : rows * index + rows, :], rows * index, keys, values)
        spot = pl.ds(pl.multiple_of(each * rows + head * text_rows, 16), text_rows)
        first = text_rows * index
        build_pair(
            ref[spot, :], tf_ref[first : first + text_rows, :], first, text_keys, text_values
        )


def forward_kernel(near, chunk, *refs):
    near_refs, refs = refs[:near], refs[near:]
    query_ref, qf_ref, kf_ref, tf_ref, gate_ref = refs[:5]
    mixed_refs, refs = refs[5 : 5 + SPLIT], refs[5 + SPLIT :]
    outs_ref, stats_ref, queries, keys, values, text_keys, text_values, hold = refs
    build_inputs(
        pl.program_id(0), near_refs, query_ref, qf_ref, kf_ref, tf_ref,
        queries, keys, values, text_keys, text_values,
    )
    rows = queries.shape[0] // SPLIT * FORWARD_SLOTS
    text_chunk = pick_tile(text_keys.shape[0], 256)

    def tile_step(tile, carry):
        spot = pl.ds(pl.multiple_of(tile * rows, rows), rows)
        query = queries[spot, :]

        def attend(key_part, value_part):
            scores = matmul(query, key_part, 1, 1)
            return matmul(jnp.exp(scores).astype(LOW), value_part, 1, 0)

        def step(index, total):
            part = pl.ds(pl.multiple_of(index * chunk, chunk), chunk)
            return total + attend(keys[part, :], values[part, :])

        def text_step(index, total):
            part = pl.ds(pl.multiple_of(index * text_chunk, text_chunk), text_chunk)
            return total + attend(text_keys[part, :], text_values[part, :])

        blank = jnp.zeros((rows, 128), FLOAT)
        own = lax.fori_loop(0, keys.shape[0] // chunk, step, blank)
        cross = lax.fori_loop(0, text_keys.shape[0] // text_chunk, text_step, blank, unroll=True)
        own_inverse = 1.0 / own[:, 0:1]
        cross_inverse = 1.0 / cross[:, 0:1]
        own = own * own_inverse
        cross = cross * cross_inverse
        lanes = lane_ids(own.shape)
        mixed = own + gate_ref[0, 0:1, :] * cross
        each = rows // FORWARD_SLOTS
        for slot in range(FORWARD_SLOTS):
            hold[tile * FORWARD_SLOTS + slot] = fold_high(mixed[each * slot : each * slot + each])
        outs_ref[spot, :] = jnp.where(lanes < 64, turn(cross), own)
        stats_ref[spot, :] = jnp.where(lanes == 0, own_inverse, cross_inverse)
        return carry

    lax.fori_loop(0, SPLIT // FORWARD_SLOTS, tile_step, 0)
    for index, ref in enumerate(mixed_refs):
        ref[...] = hold[index]


def whole(shape):
    return pl.BlockSpec(shape, lambda i: (0,) * len(shape))


def attention_specs(pairs, queries, qf, kf, tf):
    return [whole(value.shape) for value in pairs] + [
        pl.BlockSpec(qf.shape, lambda i: (i, 0)),
        whole(qf.shape),
        whole(kf.shape),
        whole(tf.shape),
        pl.BlockSpec((1, 8, 128), lambda i: (i, 0, 0)),
    ]


def attention_scratch(qf, kf, tf):
    return [
        pltpu.VMEM(qf.shape, LOW),
        pltpu.VMEM(kf.shape, LOW),
        pltpu.VMEM(kf.shape, LOW),
        pltpu.VMEM(tf.shape, LOW),
        pltpu.VMEM(tf.shape, LOW),
    ]


def attention_forward(pairs, queries, qf, kf, tf, gates):
    rows = qf.shape[0]
    heads = gates.shape[0]
    half = rows // SPLIT // 2
    folded = jax.ShapeDtypeStruct((heads * half, 128), LOW)
    wide = jax.ShapeDtypeStruct((heads * rows, 128), FLOAT)
    out = pl.pallas_call(
        functools.partial(forward_kernel, len(pairs), pick_tile(kf.shape[0], 1024)),
        grid=(heads,),
        in_specs=attention_specs(pairs, queries, qf, kf, tf),
        out_specs=[pl.BlockSpec((half, 128), lambda i: (i, 0))] * SPLIT
        + [pl.BlockSpec((rows, 128), lambda i: (i, 0))] * 2,
        out_shape=[folded] * SPLIT + [wide] * 2,
        scratch_shapes=attention_scratch(qf, kf, tf) + [pltpu.VMEM((SPLIT, half, 128), LOW)],
        compiler_params=pltpu.CompilerParams(vmem_limit_bytes=60 * MIB),
        cost_estimate=SMALL,
    )(*pairs, queries, qf, kf, tf, gates)
    return out[:SPLIT], out[SPLIT], out[SPLIT + 1]


def backward_kernel(near, chunk, *refs):
    near_refs, refs = refs[:near], refs[near:]
    query_ref, qf_ref, kf_ref, tf_ref, gate_ref = refs[:5]
    refs = refs[5:]
    grad_refs, refs = refs[:SPLIT], refs[SPLIT:]
    outs_ref, stats_ref, refs = refs[0], refs[1], refs[2:]
    dq_refs, refs = refs[:SPLIT], refs[SPLIT:]
    dkv_refs, dt_refs, dg_ref = refs[:2], refs[2:4], refs[4]
    queries, keys, values, text_keys, text_values, hold, grad_hold, acc, text_acc = refs[5:]
    build_inputs(
        pl.program_id(0), near_refs, query_ref, qf_ref, kf_ref, tf_ref,
        queries, keys, values, text_keys, text_values,
    )
    for index, ref in enumerate(grad_refs):
        grad_hold[index] = ref[...]
    acc[...] = jnp.zeros_like(acc)
    text_acc[...] = jnp.zeros_like(text_acc)
    dg_ref[...] = jnp.zeros_like(dg_ref)
    rows = queries.shape[0] // SPLIT * BACKWARD_SLOTS
    text_chunk = pick_tile(text_keys.shape[0], 256)
    gate = gate_ref[0, 0:1, :]

    def tile_step(tile, carry):
        spot = pl.ds(pl.multiple_of(tile * rows, rows), rows)
        query = queries[spot, :]
        lanes = lane_ids(query.shape)
        query_low = jnp.where(lanes < 64, query, jnp.zeros_like(query))
        grads = jnp.concatenate(
            [unfold_high(grad_hold[tile * BACKWARD_SLOTS + slot]) for slot in range(BACKWARD_SLOTS)],
            axis=0,
        )
        grads = jnp.where(lanes < 64, 0.0, grads)
        outs = outs_ref[spot, :]
        cross_out = jnp.where(lanes < 64, 0.0, turn(outs))
        dg_ref[0] += jnp.sum((grads * cross_out).reshape(rows // 8, 8, 128), axis=0)
        cross_grads = (gate * grads).astype(LOW).astype(FLOAT)

        def widen(grad, out, inverse):
            delta = -jnp.sum(grad * out, axis=1, keepdims=True) * inverse
            first = delta.astype(LOW).astype(FLOAT)
            second = (delta - first).astype(LOW).astype(FLOAT)
            third = delta - first - second
            features = jnp.where(lanes == 0, first, jnp.where(lanes == 1, second, third))
            scaled = grad * inverse
            return jnp.where(lanes < 3, features, scaled).astype(LOW), scaled.astype(LOW)

        stats = stats_ref[spot, :]
        own_wide, own_low = widen(grads, outs, stats[:, 0:1])
        cross_wide, cross_low = widen(cross_grads, cross_out, stats[:, 1:2])
        own_pair = jnp.concatenate([query_low, own_low], axis=0)
        cross_pair = jnp.concatenate([query_low, cross_low], axis=0)

        def attend(key_part, value_part, wide, pair):
            weights = jnp.exp(matmul(key_part, query, 1, 1))
            grad_scores = (weights * matmul(value_part, wide, 1, 1)).astype(LOW)
            low = weights.astype(LOW)
            grad_pair = matmul(jnp.concatenate([grad_scores, low], axis=1), pair, 1, 0)
            return grad_pair, matmul(grad_scores, key_part, 0, 0)

        def step(index, total):
            part = pl.ds(pl.multiple_of(index * chunk, chunk), chunk)
            grad_pair, grad_query = attend(keys[part, :], values[part, :], own_wide, own_pair)
            acc[part, :] += grad_pair
            return total + grad_query

        def text_step(index, total):
            part = pl.ds(pl.multiple_of(index * text_chunk, text_chunk), text_chunk)
            grad_pair, grad_query = attend(
                text_keys[part, :], text_values[part, :], cross_wide, cross_pair
            )
            text_acc[part, :] += grad_pair
            return total + grad_query

        blank = jnp.zeros((rows, 128), FLOAT)
        total = lax.fori_loop(0, keys.shape[0] // chunk, step, blank, unroll=2)
        total = lax.fori_loop(0, text_keys.shape[0] // text_chunk, text_step, total, unroll=True)
        total = total * 0.125
        each = rows // BACKWARD_SLOTS
        for slot in range(BACKWARD_SLOTS):
            hold[tile * BACKWARD_SLOTS + slot] = fold_low(total[each * slot : each * slot + each])
        return carry

    lax.fori_loop(0, SPLIT // BACKWARD_SLOTS, tile_step, 0)
    for index, ref in enumerate(dq_refs):
        ref[...] = hold[index]
    for values, refs in ((acc, dkv_refs), (text_acc, dt_refs)):
        size = refs[0].shape[1]
        refs[0][0] = values[:size, :].astype(LOW)
        refs[1][0] = values[size:, :].astype(LOW)


def attention_backward(pairs, queries, qf, kf, tf, gates, grads, outs, stats):
    rows = qf.shape[0]
    heads = gates.shape[0]
    half = rows // SPLIT // 2
    folded = jax.ShapeDtypeStruct((heads * half, 128), LOW)
    piece = jax.ShapeDtypeStruct((heads, kf.shape[0] // 2, 128), LOW)
    text = jax.ShapeDtypeStruct((heads, tf.shape[0] // 2, 128), LOW)
    sums = jax.ShapeDtypeStruct((heads, 8, 128), FLOAT)
    out = pl.pallas_call(
        functools.partial(backward_kernel, len(pairs), pick_tile(kf.shape[0], 512)),
        grid=(heads,),
        in_specs=attention_specs(pairs, queries, qf, kf, tf)
        + [pl.BlockSpec((half, 128), lambda i: (i, 0))] * SPLIT
        + [pl.BlockSpec((rows, 128), lambda i: (i, 0))] * 2,
        out_specs=[pl.BlockSpec((half, 128), lambda i: (i, 0))] * SPLIT
        + [
            pl.BlockSpec((1,) + value.shape[1:], lambda i: (i, 0, 0))
            for value in (piece, piece, text, text, sums)
        ],
        out_shape=[folded] * SPLIT + [piece, piece, text, text, sums],
        scratch_shapes=attention_scratch(qf, kf, tf)
        + [
            pltpu.VMEM((SPLIT, half, 128), LOW),
            pltpu.VMEM((SPLIT, half, 128), LOW),
            pltpu.VMEM(kf.shape, FLOAT),
            pltpu.VMEM(tf.shape, FLOAT),
        ],
        compiler_params=pltpu.CompilerParams(vmem_limit_bytes=60 * MIB),
        cost_estimate=SMALL,
    )(*pairs, queries, qf, kf, tf, gates, *grads, outs, stats)
    return (out[:SPLIT],) + tuple(out[SPLIT:])


def half_means(values, lanes):
    low = jnp.sum(jnp.where(lanes < 64, values, 0.0), axis=1, keepdims=True)
    high = jnp.sum(jnp.where(lanes < 64, 0.0, values), axis=1, keepdims=True)
    return jnp.where(lanes < 64, low, high) * (1.0 / 64.0)


def swap_halves(values, lanes):
    return jnp.where(
        lax.rem(lanes, 64) < 32, pltpu.roll(values, 96, 1), pltpu.roll(values, 32, 1)
    )


def placed_at(groups, head, upper):
    values = groups[head // 2]
    return values if (head % 2 == 1) == upper else turn(values)


def rope_forward_kernel(heads, far_ref, qkv_ref, cos_ref, sin_ref, gains_ref, *refs):
    outs, hold = refs[:-1], refs[-1]
    width = heads * 64
    each = heads // SPLIT
    rows = qkv_ref.shape[0]
    cosine, sine = cos_ref[...], sin_ref[...]
    lanes = lane_ids(cosine.shape)

    def turned(start, gain):
        groups = []
        for index in range(heads // 2):
            raw = qkv_ref[:, start + 128 * index : start + 128 * index + 128]
            normed = raw * lax.rsqrt(half_means(raw * raw, lanes) + EPS) * gain
            groups.append(normed * cosine + swap_halves(normed, lanes) * sine)
        return groups

    queries = turned(0, gains_ref[0:1, :])
    keys = turned(width, gains_ref[1:2, :])
    values = [
        qkv_ref[:, 2 * width + 128 * index : 2 * width + 128 * index + 128]
        for index in range(heads // 2)
    ]
    for head in range(heads):
        group, index = head // each, head % each
        slot = lax.rem(group - far_ref[0] + SPLIT, SPLIT)
        pair = jnp.where(
            lanes < 64, placed_at(keys, head, False), placed_at(values, head, True)
        )
        hold[slot, index, :rows, :] = pair.astype(LOW)
        hold[slot, index, rows:, :] = fold_low(placed_at(queries, head, False))
    size = rows * 3 // 2
    for slot in range(SPLIT):
        for index in range(each):
            outs[slot][size * index : size * index + size, :] = hold[slot, index]


def small_call(kernel, operands, shapes, scratch):
    out = pl.pallas_call(
        kernel,
        in_specs=[pl.BlockSpec(memory_space=pltpu.SMEM)]
        + [pl.BlockSpec(memory_space=pltpu.VMEM)] * (len(operands) - 1),
        out_specs=[pl.BlockSpec(memory_space=pltpu.VMEM)] * len(shapes),
        out_shape=shapes,
        scratch_shapes=scratch,
        compiler_params=pltpu.CompilerParams(vmem_limit_bytes=32 * MIB),
        cost_estimate=SMALL,
    )(*operands)
    return out


def rope_forward(far, qkv, cosine, sine, gains, heads):
    rows = qkv.shape[0] * 3 // 2
    each = heads // SPLIT
    out = small_call(
        functools.partial(rope_forward_kernel, heads),
        (far, qkv, cosine, sine, gains),
        [jax.ShapeDtypeStruct((each * rows, 128), LOW)] * SPLIT,
        [pltpu.VMEM((SPLIT, each, rows, 128), LOW)],
    )
    return list(out)


def rope_backward_kernel(heads, far_ref, *refs):
    parts, refs = refs[:SPLIT], refs[SPLIT:]
    qkv_ref, cos_ref, sin_ref, gains_ref, out_ref, sums_ref, hold = refs
    width = heads * 64
    each = heads // SPLIT
    rows = qkv_ref.shape[0]
    for slot in range(SPLIT):
        group = lax.rem(far_ref[0] + slot, SPLIT)
        size = hold.shape[2]
        for index in range(each):
            hold[group, index] = parts[slot][size * index : size * index + size, :]
    cosine, sine = cos_ref[...], sin_ref[...]
    lanes = lane_ids(cosine.shape)

    def found(kind, head):
        group, index, upper = head // each, head % each, head % 2 == 1
        if kind == 0:
            packed = hold[group, index, rows:, :]
            return unfold_high(packed) if upper else unfold_low(packed)
        values = hold[group, index, :rows, :].astype(FLOAT)
        return values if upper == (kind == 2) else turn(values)

    def joined(kind, index):
        return jnp.where(lanes < 64, found(kind, 2 * index), found(kind, 2 * index + 1))

    for kind in range(2):
        gain = gains_ref[kind : kind + 1, :]
        total = jnp.zeros((1, 128), FLOAT)
        for index in range(heads // 2):
            spot = kind * width + 128 * index
            raw = qkv_ref[:, spot : spot + 128]
            inverse = lax.rsqrt(half_means(raw * raw, lanes) + EPS)
            unit = raw * inverse
            grad = joined(kind, index)
            back = grad * cosine - swap_halves(grad, lanes) * sine
            total = total + jnp.sum(back * unit, axis=0, keepdims=True)
            scaled = back * gain
            raw_grad = inverse * (scaled - unit * half_means(scaled * unit, lanes))
            out_ref[:, spot : spot + 128] = raw_grad.astype(LOW)
        sums_ref[kind : kind + 1, :] = total
    sums_ref[2:8, :] = jnp.zeros((6, 128), FLOAT)
    for index in range(heads // 2):
        spot = 2 * width + 128 * index
        out_ref[:, spot : spot + 128] = joined(2, index).astype(LOW)


def rope_backward(far, parts, qkv, cosine, sine, gains, heads):
    each = heads // SPLIT
    return small_call(
        functools.partial(rope_backward_kernel, heads),
        (far, *parts, qkv, cosine, sine, gains),
        [jax.ShapeDtypeStruct(qkv.shape, LOW), jax.ShapeDtypeStruct((8, 128), FLOAT)],
        [pltpu.VMEM((SPLIT, each, parts[0].shape[0] // each, 128), LOW)],
    )


def join_kernel(heads, far_ref, *refs):
    parts, out_ref, hold = refs[:SPLIT], refs[SPLIT], refs[SPLIT + 1]
    each = heads // SPLIT
    half = hold.shape[2]
    for slot in range(SPLIT):
        group = lax.rem(far_ref[0] + slot, SPLIT)
        for index in range(each):
            hold[group, index] = parts[slot][half * index : half * index + half, :]
    for pair in range(heads // 2):
        low = unfold_low(hold[2 * pair // each, 2 * pair % each])
        high = unfold_high(hold[(2 * pair + 1) // each, (2 * pair + 1) % each])
        out_ref[:, 128 * pair : 128 * pair + 128] = jnp.where(
            lane_ids(low.shape) < 64, low, high
        ).astype(LOW)


def join_heads(far, parts, heads):
    each = heads // SPLIT
    half = parts[0].shape[0] // each
    return small_call(
        functools.partial(join_kernel, heads),
        (far, *parts),
        [jax.ShapeDtypeStruct((2 * half, heads * 64), LOW)],
        [pltpu.VMEM((SPLIT, each, half, 128), LOW)],
    )[0]


def split_kernel(heads, far_ref, grad_ref, *refs):
    outs, hold = refs[:-1], refs[-1]
    each = heads // SPLIT
    half = hold.shape[2]
    for head in range(heads):
        group, index = head // each, head % each
        slot = lax.rem(group - far_ref[0] + SPLIT, SPLIT)
        values = grad_ref[:, 128 * (head // 2) : 128 * (head // 2) + 128]
        hold[slot, index] = fold_high(values) if head % 2 else fold_low(values)
    for slot in range(SPLIT):
        for index in range(each):
            outs[slot][half * index : half * index + half, :] = hold[slot, index]


def split_heads(far, grads, heads):
    each = heads // SPLIT
    half = grads.shape[0] // 2
    return small_call(
        functools.partial(split_kernel, heads),
        (far, grads),
        [jax.ShapeDtypeStruct((each * half, 128), LOW)] * SPLIT,
        [pltpu.VMEM((SPLIT, each, half, 128), LOW)],
    )


def local_call(kernel, operands, shapes):
    return pl.pallas_call(
        kernel,
        out_shape=shapes,
        compiler_params=pltpu.CompilerParams(vmem_limit_bytes=40 * MIB),
        cost_estimate=SMALL,
    )(*operands)


def gather_kernel(each, *refs):
    slots, text_ref, pairs_ref, queries_ref = refs[:SPLIT], refs[SPLIT], refs[-2], refs[-1]
    size = slots[0].shape[0] // each
    rows = size * 2 // 3
    for head in range(each):
        for index, slot in enumerate(slots):
            spot = (head * SPLIT + index) * rows
            first = head * size
            pairs_ref[spot : spot + rows, :] = slot[first : first + rows, :]
            query = unfold_low(slot[first + rows : first + size, :])
            query = jnp.where(lane_ids(query.shape) < 64, query * 0.125, 0.0)
            queries_ref[spot : spot + rows, :] = query.astype(LOW)
    pairs_ref[each * SPLIT * rows :, :] = text_ref[...]


def gather_slots(slots, text, each):
    rows = slots[0].shape[0] * 2 // 3 * SPLIT
    return local_call(
        functools.partial(gather_kernel, each),
        (*slots, text),
        [
            jax.ShapeDtypeStruct((rows + text.shape[0], 128), LOW),
            jax.ShapeDtypeStruct((rows, 128), LOW),
        ],
    )


def pack_kernel(terms, *refs):
    inputs, folded, outs = refs[:terms], refs[terms : terms + SPLIT], refs[terms + SPLIT :]
    each = inputs[0].shape[0]
    size = outs[0].shape[0] // each
    rows = size * 2 // 3
    half = size - rows
    for head in range(each):
        for slot in range(SPLIT):
            total = sum(
                term[head, rows * slot : rows * slot + rows, :].astype(FLOAT) for term in inputs
            )
            spot = size * head
            outs[slot][spot : spot + rows, :] = total.astype(LOW)
            outs[slot][spot + rows : spot + size, :] = folded[slot][
                half * head : half * head + half, :
            ]


def pack_slots(terms, folded):
    return local_call(
        functools.partial(pack_kernel, len(terms)),
        (*terms, *folded),
        [jax.ShapeDtypeStruct((3 * folded[0].shape[0], 128), LOW)] * SPLIT,
    )


def text_split_kernel(far_ref, text_ref, *outs):
    size = outs[0].shape[1]
    for slot in range(SPLIT):
        group = lax.rem(far_ref[0] + slot, SPLIT)
        spot = pl.ds(pl.multiple_of(group * size, 128), size)
        outs[slot][...] = text_ref[:, spot].astype(LOW)


def text_join_kernel(far_ref, *refs):
    parts, out_ref = refs[:SPLIT], refs[SPLIT]
    size = parts[0].shape[1]
    for slot in range(SPLIT):
        group = lax.rem(far_ref[0] + slot, SPLIT)
        out_ref[:, pl.ds(pl.multiple_of(group * size, 128), size)] = parts[slot][...]


def low_means(values, lanes):
    return jnp.sum(jnp.where(lanes < 64, values, 0.0), axis=1, keepdims=True) * (1.0 / 64.0)


def text_norm_kernel(*refs):
    parts, gain_ref, raw_ref, out_ref = refs[:SPLIT], refs[SPLIT], refs[-2], refs[-1]
    rows = raw_ref.shape[0]
    raw = sum(part[...].astype(FLOAT) for part in parts)
    raw_ref[...] = raw
    for head in range(raw.shape[1] // 128):
        values = raw[:, 128 * head : 128 * head + 128]
        lanes = lane_ids(values.shape)
        normed = values * lax.rsqrt(low_means(values * values, lanes) + EPS) * gain_ref[0:1, :]
        out_ref[rows * head : rows * head + rows, :] = jnp.where(
            lanes < 64, normed, values
        ).astype(LOW)


def text_back_kernel(terms, *refs):
    inputs, refs = refs[:terms], refs[terms:]
    raw_ref, gain_ref, out_ref, sums_ref = refs
    rows = raw_ref.shape[0]
    total_gain = jnp.zeros((1, 128), FLOAT)
    for head in range(inputs[0].shape[0]):
        grad = sum(term[head, :rows, :].astype(FLOAT) for term in inputs)
        grad = grad.astype(LOW).astype(FLOAT)
        raw = raw_ref[:, 128 * head : 128 * head + 128]
        lanes = lane_ids(raw.shape)
        inverse = lax.rsqrt(low_means(raw * raw, lanes) + EPS)
        unit = raw * inverse
        total_gain = total_gain + jnp.sum(grad * unit, axis=0, keepdims=True)
        scaled = grad * gain_ref[0:1, :]
        back = inverse * (scaled - unit * low_means(scaled * unit, lanes))
        out_ref[:, 128 * head : 128 * head + 128] = jnp.where(lanes < 64, back, grad).astype(LOW)
    sums_ref[...] = jnp.broadcast_to(total_gain, sums_ref.shape)


def tie(*values):
    return lax.optimization_barrier(values)


def stacked_kernel(left_ref, own_ref, other_ref, out_ref):
    rows = own_ref.shape[1]
    out_ref[...] = (
        matmul(left_ref[:, :rows], own_ref[0], 1, 0)
        + matmul(left_ref[:, rows:], other_ref[0], 1, 0)
    ).astype(LOW)


def stacked_outer(left, own, other, tile):
    depth = left.shape[0]
    count, rows, columns = own.shape
    tiles = columns // tile
    part = pl.BlockSpec((1, rows, tile), lambda i: (i // tiles, 0, i % tiles))
    return pl.pallas_call(
        stacked_kernel,
        grid=(count * tiles,),
        in_specs=[pl.BlockSpec(left.shape, lambda i: (0, 0)), part, part],
        out_specs=pl.BlockSpec((depth, tile), lambda i: (0, i)),
        out_shape=jax.ShapeDtypeStruct((depth, count * columns), LOW),
        compiler_params=pltpu.CompilerParams(vmem_limit_bytes=40 * MIB),
        cost_estimate=SMALL,
    )(left, own, other)


def joint_kernel(count, left_ref, own_ref, other_ref, own_last_ref, other_last_ref, out_ref):
    step = pl.program_id(0)
    rows = own_ref.shape[1]

    @pl.when(step < count)
    def _():
        out_ref[...] = (
            matmul(left_ref[0, :, :rows], own_ref[0], 1, 0)
            + matmul(left_ref[0, :, rows:], other_ref[0], 1, 0)
        ).astype(LOW)

    @pl.when(step >= count)
    def _():
        out_ref[...] = (
            matmul(left_ref[0, :, :rows], own_last_ref[...], 1, 0)
            + matmul(left_ref[0, :, rows:], other_last_ref[...], 1, 0)
        ).astype(LOW)


def joint_outer(left, own, other, own_last, other_last, tile):
    depth, tokens = left.shape[1:]
    rows, columns = own.shape[1:]
    tiles = columns // tile
    count = own.shape[0] * tiles
    extra = own_last.shape[1] // tile

    def right_at(i):
        at = jnp.minimum(i, count - 1)
        return (at // tiles, 0, at % tiles)

    right = pl.BlockSpec((1, rows, tile), right_at)
    last = pl.BlockSpec((rows, tile), lambda i: (0, jnp.maximum(i - count, 0)))
    return pl.pallas_call(
        functools.partial(joint_kernel, count),
        grid=(count + extra,),
        in_specs=[
            pl.BlockSpec((1, depth, tokens), lambda i: (jnp.where(i < count, 0, 1), 0, 0)),
            right,
            right,
            last,
            last,
        ],
        out_specs=pl.BlockSpec((depth, tile), lambda i: (0, i)),
        out_shape=jax.ShapeDtypeStruct((depth, (count + extra) * tile), LOW),
        compiler_params=pltpu.CompilerParams(vmem_limit_bytes=40 * MIB),
        cost_estimate=SMALL,
    )(left, own, other, own_last, other_last)


def feed_kernel(
    normed_ref, grad_ref, gate_ref, up_ref, down_ref,
    hidden_ref, grads_ref, feed_own_ref, feed_other_ref, norm_own_ref, norm_other_ref,
    feed_acc, norm_acc,
):
    step = pl.program_id(0)

    @pl.when(step == 0)
    def _():
        feed_acc[...] = jnp.zeros_like(feed_acc)
        norm_acc[...] = jnp.zeros_like(norm_acc)

    normed = normed_ref[...]
    gate = matmul(normed, gate_ref[...], 1, 0)
    up = matmul(normed, up_ref[...], 1, 0)
    grad_hidden = matmul(grad_ref[...], down_ref[...], 1, 0)
    sigmoid = 1.0 / (1.0 + jnp.exp(-gate))
    silu = gate * sigmoid
    hidden = (silu * up).astype(LOW)
    grad_gate = (grad_hidden * up * sigmoid * (1.0 + gate * (1.0 - sigmoid))).astype(LOW)
    grad_up = (grad_hidden * silu).astype(LOW)
    hidden_ref[0] = hidden
    grads_ref[0] = grad_gate
    grads_ref[1] = grad_up
    feed_acc[...] += matmul(hidden, down_ref[...], 1, 1)
    norm_acc[...] += matmul(grad_gate, gate_ref[...], 1, 1) + matmul(grad_up, up_ref[...], 1, 1)

    @pl.when(step == pl.num_programs(0) - 1)
    def _():
        half = feed_own_ref.shape[0]
        feed_own_ref[...] = feed_acc[:half, :]
        feed_other_ref[...] = feed_acc[half:, :].astype(LOW)
        norm_own_ref[...] = norm_acc[:half, :]
        norm_other_ref[...] = norm_acc[half:, :].astype(LOW)


def feed_forward(normed, grads, weights, tile):
    rows, width = normed.shape
    columns = weights.shape[1] // 3
    tiles = columns // tile
    own = jax.ShapeDtypeStruct((rows // 2, width), FLOAT)
    other = jax.ShapeDtypeStruct((rows // 2, width), LOW)
    return pl.pallas_call(
        feed_kernel,
        grid=(tiles,),
        in_specs=[whole(normed.shape), whole(grads.shape)]
        + [
            pl.BlockSpec((width, tile), lambda i, part=part: (0, part * tiles + i))
            for part in range(3)
        ],
        out_specs=[
            pl.BlockSpec((1, rows, tile), lambda i: (0, 0, i)),
            pl.BlockSpec((2, rows, tile), lambda i: (0, 0, i)),
        ]
        + [whole(own.shape)] * 4,
        out_shape=[
            jax.ShapeDtypeStruct((1, rows, columns), LOW),
            jax.ShapeDtypeStruct((2, rows, columns), LOW),
            own,
            other,
            own,
            other,
        ],
        scratch_shapes=[pltpu.VMEM((rows, width), FLOAT)] * 2,
        compiler_params=pltpu.CompilerParams(vmem_limit_bytes=48 * MIB),
        cost_estimate=SMALL,
    )(normed, grads, weights, weights, weights)


def dot_float(left, right):
    return jnp.dot(left, right, preferred_element_type=FLOAT)


def dot_turned(left, right):
    return matmul(left, right, 1, 1)


def norm_rows(values, gains):
    return values * lax.rsqrt(jnp.mean(values * values, axis=-1, keepdims=True) + EPS) * gains


def modulated(values, gains, shifts, scales):
    return norm_rows(values, gains) * (1.0 + scales) + shifts


def swapped(values):
    return lax.ppermute(values, "tensor", [(0, 1), (1, 0)])


def both_rows(values):
    return jnp.concatenate([values, swapped(values)], axis=0)


def own_rows(partial):
    rows = partial.shape[0] // 2
    return partial[:rows] + swapped(partial[rows:].astype(LOW)).astype(FLOAT)


def shards(
    inputs,
    clip_ids,
    positions,
    text_tokens,
    conditioning,
    ada_weight,
    ada_bias,
    first_norm_gain,
    query_gain,
    key_gain,
    text_key_gain,
    head_gate,
    qkv_weight,
    out_weight,
    text_kv_weight,
    second_norm_gain,
    gate_up_weight,
    down_weight,
    grad_output,
):
    dp = lax.axis_size("dp")
    near = dp // SPLIT
    bits = [near >> (step + 1) for step in range(near.bit_length() - 1)]
    tensor_index = lax.axis_index("tensor")
    dp_index = lax.axis_index("dp")
    far_index, near_index = dp_index // near, dp_index % near
    row_count, width = inputs.shape
    token_count = clip_ids.shape[0]
    head_size = query_gain.shape[0]
    local_width = qkv_weight.shape[2]
    heads = local_width // head_size
    each = heads // SPLIT
    part_width = each * head_size
    clip_count = conditioning.shape[0]
    hidden_count = gate_up_weight.shape[2]
    weight_rows = qkv_weight.shape[1]

    def flip(values, bit):
        return lax.ppermute(values, "dp", [(j, j ^ bit) for j in range(dp)])

    def shift(values, steps):
        pairs = [(j, ((j // near + steps) % SPLIT) * near + j % near) for j in range(dp)]
        return lax.ppermute(values, "dp", pairs)

    def sum_dp(values):
        step = 1
        while step < dp:
            values = values + flip(values, step)
            step *= 2
        return values

    def spread(values):
        for bit in bits:
            values = jnp.concatenate([values, flip(values, bit)], axis=0)
        return values

    def spread_list(values):
        values = [values]
        for bit in bits:
            values = values + [flip(value, bit) for value in values]
        return values

    def collect(values):
        for bit in reversed(bits):
            half = values.shape[0] // 2
            values = values[:half].astype(FLOAT) + flip(
                values[half:].astype(LOW), bit
            ).astype(FLOAT)
        return values

    def pick(stacked, index):
        return lax.dynamic_index_in_dim(stacked, index, 0, keepdims=False)

    def send_parts(stacked):
        out = [pick(stacked, far_index)]
        for steps in range(1, SPLIT):
            out.append(shift(pick(stacked, (far_index + steps) % SPLIT), steps))
        return out

    def send_slots(slots):
        return [slots[0]] + [shift(slots[steps], steps) for steps in range(1, SPLIT)]

    def return_slots(slots):
        return [slots[0]] + [shift(slots[steps], -steps) for steps in range(1, SPLIT)]

    flips = []
    for order in range(near):
        mask = 0
        for place, bit in enumerate(bits):
            if order >> place & 1:
                mask |= bit
        flips.append(mask)

    core = dp_index % 2
    core_groups = [list(range(first, dp, 2)) for first in range(2)]

    def core_columns(values):
        halves = (
            values.T.reshape(dp // 2, 2, weight_rows, token_count)
            .transpose(1, 0, 2, 3)
            .reshape(2, width // 2, token_count)
        )
        return jnp.concatenate([pick(halves, core), flip(pick(halves, 1 - core), 1)], axis=1)

    def scatter(values):
        return lax.psum_scatter(
            values, "dp", scatter_dimension=0, axis_index_groups=core_groups, tiled=True
        )

    attn_full = lax.all_gather(
        jnp.concatenate(
            [
                qkv_weight.transpose(1, 0, 2).reshape(weight_rows, 3 * local_width),
                out_weight.T,
            ],
            axis=1,
        ),
        "dp",
        axis=0,
        tiled=True,
    )
    cond_float = conditioning.astype(FLOAT)
    silu_cond = jax.nn.silu(cond_float).astype(LOW)
    cond_rows = ada_weight.shape[0]
    silu_slice = lax.dynamic_slice_in_dim(silu_cond, dp_index * cond_rows, cond_rows, axis=1)
    first_rows = jnp.sum((clip_ids == 0).astype(FLOAT))
    spots = jnp.arange(ada_weight.shape[1], dtype=jnp.int32)
    early = 2 * width
    early_part = jnp.concatenate(
        [
            dot_float(silu_slice, ada_weight[:, :early]),
            jnp.where(spots[:early] == dp_index, first_rows, 0.0)[None],
        ],
        axis=0,
    )
    early_sum = sum_dp(early_part)
    bias = ada_bias.astype(FLOAT)
    early_mod = early_sum[:clip_count] + bias[:early]
    counts = early_sum[clip_count, :dp].astype(jnp.int32)

    own_ids = lax.dynamic_slice_in_dim(clip_ids, tensor_index * row_count, row_count)
    row_positions = jnp.where(
        tensor_index == 0, positions, jnp.roll(positions, row_count)
    )
    other_clip = jnp.max(clip_ids)
    first_clip = (own_ids == 0)[:, None]

    def mod_blocks(modulation):
        rows = jnp.where(
            first_clip,
            modulation[0:1],
            lax.dynamic_slice_in_dim(modulation, other_clip, 1, 0),
        )
        return jnp.split(rows, rows.shape[1] // width, axis=1)

    shift_one, scale_one = mod_blocks(early_mod)
    input_rows = inputs.astype(FLOAT)
    first_gain = first_norm_gain.astype(FLOAT)
    normed_one = modulated(input_rows, first_gain, shift_one, scale_one).astype(LOW)
    normed_all = both_rows(normed_one)
    late_sum = sum_dp(dot_float(silu_slice, ada_weight[:, early:]))

    half_size = head_size // 2
    frequency = 10000.0 ** (-(jnp.arange(half_size, dtype=FLOAT) * 2.0 / head_size))
    angles = row_positions.astype(FLOAT)[:, None] * frequency[None, :]
    cosine = jnp.cos(angles)
    sine = jnp.sin(angles)
    cosine = jnp.concatenate([cosine] * 4, axis=1)
    sine = jnp.concatenate([-sine, sine, -sine, sine], axis=1)
    gains = jnp.stack([jnp.tile(query_gain, 2), jnp.tile(key_gain, 2)]).astype(FLOAT)
    gains = jnp.concatenate([gains, jnp.zeros((6, 128), FLOAT)], axis=0)

    text_rows = text_tokens.shape[0]
    group_rows = text_rows * SPLIT
    text_tokens, late_sum = tie(text_tokens, late_sum)
    text_columns = lax.all_to_all(text_tokens, "dp", split_axis=1, concat_axis=0, tiled=True)
    text_groups = text_columns.reshape(near, group_rows, text_columns.shape[1])
    text_near = jnp.concatenate([pick(text_groups, near_index ^ mask) for mask in flips], axis=0)
    text_weight = (
        text_kv_weight.reshape(2, -1, SPLIT, each, head_size)
        .transpose(1, 2, 3, 0, 4)
        .reshape(-1, 2 * local_width)
    )
    far = far_index.astype(jnp.int32).reshape(1)
    text_sum = collect(dot_float(text_near, text_weight))
    part_shape = jax.ShapeDtypeStruct((group_rows, 2 * part_width), LOW)
    text_parts = small_call(text_split_kernel, (far, text_sum), [part_shape] * SPLIT, [])
    ky_gain = jnp.concatenate([text_key_gain.astype(FLOAT), jnp.zeros((128 - head_size,), FLOAT)])
    ky_gain = jnp.broadcast_to(ky_gain[None], (8, 128))

    lanes = jnp.arange(128, dtype=jnp.int32)[None, :]
    text_groups_at = jnp.stack([near_index ^ mask for mask in flips])
    text_clip = (
        text_groups_at[:, None] * group_rows + jnp.arange(group_rows, dtype=jnp.int32)[None, :]
    ).reshape(-1) // TXT
    text_features = (lanes == 64 + text_clip[:, None]).astype(LOW)
    block_at = jnp.stack(
        [
            ((far_index - steps) % SPLIT) * near + (near_index ^ mask)
            for mask in flips
            for steps in range(SPLIT)
        ]
    )
    block_count = jnp.sum(
        jnp.where(block_at[:, None] == jnp.arange(dp, dtype=jnp.int32)[None, :], counts[None, :], 0),
        axis=1,
    )
    row_at = (jnp.arange(token_count, dtype=jnp.int32) + tensor_index * row_count) % token_count
    key_clip = jnp.where(
        row_at[None, :] < block_count[:, None], 0, 1 + block_at[:, None] // GROUP
    ).reshape(-1)
    key_features = (lanes == 64 + key_clip[:, None]).astype(LOW)
    group_tokens = SPLIT * token_count
    query_clip = key_clip[:group_tokens, None]
    query_features = jnp.where(
        (lanes >= 64) & (lanes < 64 + clip_count) & (lanes != 64 + query_clip), MASK, 0.0
    ).astype(LOW)
    gate_heads = jnp.tanh(
        lax.dynamic_slice_in_dim(
            head_gate.astype(FLOAT), tensor_index * heads + far_index * each, each
        )
    )
    gate_lanes = jnp.broadcast_to(gate_heads[:, None, None], (each, 8, 128))

    qkv_full, normed_all, text_parts, key_features, query_features = tie(
        attn_full[:, : 3 * local_width], normed_all, text_parts, key_features, query_features
    )
    out_full = attn_full[:, 3 * local_width :]
    text_arrived = send_slots(text_parts)
    qkv_raw = dot_float(normed_all, qkv_full)
    head_slots = rope_forward(far, qkv_raw, cosine, sine, gains, heads)
    gate_one, shift_two, scale_two, gate_two = mod_blocks(late_sum + bias[early:])
    grad_two = grad_output.astype(FLOAT)
    grad_ffn = both_rows((gate_two * grad_two).astype(LOW))
    head_slots, text_arrived = tie(head_slots, text_arrived)
    text_raw, text_pairs = local_call(
        text_norm_kernel,
        (*text_arrived, ky_gain),
        [
            jax.ShapeDtypeStruct((group_rows, 2 * part_width), FLOAT),
            jax.ShapeDtypeStruct((each * group_rows, 128), LOW),
        ],
    )
    arrived = send_slots(head_slots)
    own_pairs, queries = gather_slots(arrived, text_pairs, each)
    pairs = spread_list(own_pairs)
    feed_weights, pairs, grad_ffn = tie(
        jnp.concatenate([gate_up_weight[0], gate_up_weight[1], down_weight.T], axis=1),
        pairs,
        grad_ffn,
    )
    feed_full = lax.all_gather(feed_weights, "dp", axis=0, tiled=True)
    mixed_slots, head_outs, head_stats = attention_forward(
        pairs, queries, query_features, key_features, text_features, gate_lanes
    )
    mixed = join_heads(far, return_slots(mixed_slots), heads)
    attn_rows = own_rows(dot_turned(mixed, out_full))
    after_attn = input_rows + gate_one * attn_rows
    second_gain = second_norm_gain.astype(FLOAT)
    normed_two_all = both_rows(modulated(after_attn, second_gain, shift_two, scale_two).astype(LOW))
    hidden_low, feed_grads, feed_own, feed_other, norm_own, norm_other = feed_forward(
        normed_two_all, grad_ffn, feed_full, 512
    )
    down_grads = stacked_outer(core_columns(grad_ffn), hidden_low, flip(hidden_low, 1), 512)
    down_low = scatter(down_grads)
    grad_normed_two = norm_own + swapped(norm_other).astype(FLOAT)
    grad_normed_two, feed_other = tie(grad_normed_two, feed_other)
    ffn_rows = feed_own + swapped(feed_other).astype(FLOAT)
    output = (after_attn + gate_two * ffn_rows).astype(LOW)
    grad_gate_two = grad_two * ffn_rows
    _, pull_two = jax.vjp(modulated, after_attn, second_gain, shift_two, scale_two)
    back_two, grad_second_gain, grad_shift_two, grad_scale_two = pull_two(grad_normed_two)
    grad_after = grad_two + back_two
    grad_attn = both_rows((gate_one * grad_after).astype(LOW))
    grad_gate_one = grad_after * attn_rows
    grad_slots = send_slots(split_heads(far, dot_float(grad_attn, out_full), heads))
    joint_grads = joint_outer(
        jnp.stack([core_columns(normed_two_all), core_columns(grad_attn)]),
        feed_grads,
        flip(feed_grads, 1),
        mixed,
        flip(mixed, 1),
        256,
    )
    grad_slots, joint_grads, down_low = tie(grad_slots, joint_grads, down_low)
    joint_low = scatter(joint_grads)

    def total_rows(terms, first, last):
        return sum(term[:, first:last].astype(FLOAT) for term in terms).astype(LOW)

    def start_sums(keep, send, text_keep, text_send):
        return (
            [keep, flip(send, bits[-1])],
            [text_keep, flip(text_send, bits[-1])],
        )

    def next_send(state):
        terms, text_terms = state
        size, text_size = terms[-1].shape[1], text_terms[-1].shape[1]
        return jnp.concatenate(
            [
                total_rows(terms, size // 2, size),
                total_rows(text_terms, text_size // 2, text_size),
            ],
            axis=1,
        )

    def next_state(state, sent, bit):
        terms, text_terms = state
        size = terms[-1].shape[1] // 2
        other = flip(sent, bit)
        return terms + [other[:, :size]], text_terms + [other[:, size:]]

    folded, *pieces, gate_parts = attention_backward(
        pairs,
        queries,
        query_features,
        key_features,
        text_features,
        gate_lanes,
        grad_slots,
        head_outs,
        head_stats,
    )
    state = start_sums(*pieces)
    for bit in reversed(bits[:-1]):
        state = next_state(state, next_send(state), bit)
    pair_terms, text_terms = state
    back_slots = pack_slots(pair_terms, folded)
    clip_at = jnp.arange(clip_count, dtype=jnp.int32)[:, None]

    def clip_sums(values):
        first_sum = jnp.sum(jnp.where(first_clip, values, 0.0), axis=0)[None]
        other_sum = jnp.sum(jnp.where(first_clip, 0.0, values), axis=0)[None]
        return jnp.where(clip_at == 0, first_sum, jnp.where(clip_at == other_clip, other_sum, 0.0))

    def pair_sums(blocks, gains_row):
        wide = jnp.concatenate([clip_sums(values) for values in blocks], axis=1)
        gains_row = jnp.concatenate(
            [gains_row, jnp.zeros((wide.shape[1] - gains_row.shape[0],), FLOAT)]
        )
        wide = jnp.concatenate([wide, gains_row[None]], axis=0)
        return wide + swapped(wide)

    back_parts = return_slots(back_slots)
    text_low, ky_sums = local_call(
        functools.partial(text_back_kernel, len(text_terms)),
        (*text_terms, text_raw, ky_gain),
        [part_shape, jax.ShapeDtypeStruct((8, 128), FLOAT)],
    )
    back_parts, text_low = tie(back_parts, text_low)
    qkv_grad, gain_sums = rope_backward(far, back_parts, qkv_raw, cosine, sine, gains, heads)
    grad_normed_one = own_rows(dot_turned(qkv_grad, qkv_full))
    qkv_right = qkv_grad[None]
    qkv_grads = stacked_outer(
        core_columns(normed_all), qkv_right, flip(qkv_right, 1), local_width
    )
    qkv_grads, joint_low, grad_normed_one, text_low = tie(
        qkv_grads, joint_low, grad_normed_one, text_low
    )
    qkv_low = scatter(qkv_grads)
    _, pull_one = jax.vjp(modulated, input_rows, first_gain, shift_one, scale_one)
    back_one, grad_first_gain, grad_shift_one, grad_scale_one = pull_one(grad_normed_one)
    grad_inputs = grad_after + back_one
    head_sums = (1.0 - gate_heads * gate_heads) * jnp.sum(gate_parts, axis=(1, 2))
    head_row = lax.dynamic_update_slice_in_dim(
        jnp.zeros((head_gate.shape[0],), FLOAT),
        head_sums,
        tensor_index * heads + far_index * each,
        0,
    )
    gain_halves = gain_sums[:2, :head_size] + gain_sums[:2, head_size:]
    all_pairs = pair_sums(
        (
            grad_shift_one,
            grad_scale_one,
            grad_gate_one,
            grad_shift_two,
            grad_scale_two,
            grad_gate_two,
        ),
        jnp.concatenate(
            [
                grad_first_gain,
                grad_second_gain,
                gain_halves.reshape(-1),
                ky_sums[0, :head_size],
                head_row,
            ]
        ),
    )
    text_wide = small_call(
        text_join_kernel,
        (far, *return_slots([text_low] * SPLIT)),
        [jax.ShapeDtypeStruct((group_rows, 2 * local_width), LOW)],
        [],
    )[0]
    grad_sums = sum_dp(all_pairs)
    grad_mod_low, sums = grad_sums[:clip_count].astype(LOW), grad_sums[clip_count]
    first_gain_sum = sums[:width]
    second_gain_sum = sums[width : 2 * width]
    at = 2 * width
    q_gain_sum = sums[at : at + head_size]
    k_gain_sum = sums[at + head_size : at + 2 * head_size]
    ky_gain_sum = sums[at + 2 * head_size : at + 3 * head_size]
    gate_sum = sums[at + 3 * head_size : at + 3 * head_size + head_gate.shape[0]]
    text_all = spread(text_wide)
    grad_text_kv = (
        matmul(text_near, text_all, 0, 0)
        .reshape(-1, SPLIT, each, 2, head_size)
        .transpose(3, 0, 1, 2, 4)
        .reshape(2, -1, local_width)
    )
    grad_text_part = dot_turned(text_all, text_weight).astype(LOW)
    grad_text_pair = grad_text_part.astype(FLOAT) + swapped(grad_text_part).astype(FLOAT)
    grad_text_groups = grad_text_pair.astype(LOW).reshape(near, group_rows, -1)
    orders = jnp.arange(near, dtype=jnp.int32)
    flip_at = jnp.array(flips, jnp.int32)
    grad_text_rows = jnp.concatenate(
        [
            pick(grad_text_groups, jnp.sum(jnp.where(flip_at == near_index ^ group, orders, 0)))
            for group in range(near)
        ],
        axis=0,
    )
    grad_text_all = lax.all_to_all(grad_text_rows, "dp", split_axis=0, concat_axis=1, tiled=True)
    half_text = text_tokens.shape[1] // 2
    grad_text = lax.dynamic_slice_in_dim(
        grad_text_all, tensor_index * half_text, half_text, 1
    ).astype(FLOAT)
    grad_ada_bias = jnp.sum(grad_mod_low.astype(FLOAT), axis=0)
    grad_ada = matmul(silu_slice, grad_mod_low, 0, 0)
    cond_part = lax.dynamic_update_slice_in_dim(
        jnp.zeros(cond_float.shape, FLOAT),
        dot_turned(grad_mod_low, ada_weight),
        dp_index * cond_rows,
        1,
    )
    cond_sigmoid = jax.nn.sigmoid(cond_float)
    grad_conditioning = (
        sum_dp(cond_part) * cond_sigmoid * (1.0 + cond_float * (1.0 - cond_sigmoid))
    )
    qkv_shard = qkv_low.astype(FLOAT).reshape(weight_rows, 3, local_width).transpose(1, 0, 2)
    joint_shard = joint_low.astype(FLOAT)
    gate_up_shard = jnp.stack(
        [joint_shard[:, :hidden_count], joint_shard[:, hidden_count : 2 * hidden_count]]
    )
    out_shard = joint_shard[:, 2 * hidden_count :]
    down_shard = down_low.astype(FLOAT)
    return (
        output,
        grad_inputs,
        grad_text,
        grad_conditioning,
        grad_ada,
        grad_ada_bias,
        first_gain_sum,
        q_gain_sum,
        k_gain_sum,
        ky_gain_sum,
        gate_sum,
        qkv_shard,
        out_shard.T,
        grad_text_kv,
        second_gain_sum,
        gate_up_shard,
        down_shard.T,
    )


def solution(mesh):
    placed = (
        P(("dp", "tensor"), None),
        P("dp"),
        P("dp"),
        P("dp", None),
        P(),
        P("dp", None),
        P(),
        P(),
        P(),
        P(),
        P(),
        P(),
        P(None, "dp", "tensor"),
        P("tensor", "dp"),
        P(None, "dp", "tensor"),
        P(),
        P(None, "dp", "tensor"),
        P("tensor", "dp"),
        P(("dp", "tensor"), None),
    )
    return jax.shard_map(
        shards,
        mesh=mesh,
        in_specs=placed,
        out_specs=(
            P(("dp", "tensor"), None),
            P(("dp", "tensor"), None),
            P("dp", "tensor"),
            P(),
            P("dp", None),
            P(),
            P(),
            P(),
            P(),
            P(),
            P(),
            P(None, "dp", "tensor"),
            P("tensor", "dp"),
            P(None, "dp", "tensor"),
            P(),
            P(None, "dp", "tensor"),
            P("tensor", "dp"),
        ),
        check_vma=False,
    )
```

```python
import functools

import jax
import jax.numpy as jnp
from jax import lax
from jax.experimental import pallas as pl
from jax.experimental.pallas import tpu as pltpu
from jax.sharding import PartitionSpec as P

TXT = 256
GROUP = 8
SPLIT = 4
EPS = 1e-06
MASK = -1e4
FORWARD_SLOTS = 4
BACKWARD_SLOTS = 4
LOW = jnp.bfloat16
FLOAT = jnp.float32
MIB = 1024 * 1024
SMALL = pl.CostEstimate(flops=1024, bytes_accessed=1024, transcendentals=0)


def pick_tile(total, most):
    size = most
    while total % size:
        size //= 2
    return size


def matmul(left, right, left_dim, right_dim):
    return lax.dot_general(
        left, right, (((left_dim,), (right_dim,)), ((), ())), preferred_element_type=jnp.float32
    )


def lane_ids(shape):
    return lax.broadcasted_iota(jnp.int32, shape, len(shape) - 1)


def turn(values):
    return pltpu.roll(values, 64, 1)


def fold_low(values):
    half = values.shape[0] // 2
    top, bottom = values[:half], turn(values)[half:]
    return jnp.where(lane_ids(top.shape) < 64, top, bottom).astype(LOW)


def fold_high(values):
    half = values.shape[0] // 2
    top, bottom = turn(values)[:half], values[half:]
    return jnp.where(lane_ids(top.shape) < 64, top, bottom).astype(LOW)


def unfold_low(packed):
    wide = packed.astype(FLOAT)
    return jnp.concatenate([wide, turn(wide)], axis=0)


def unfold_high(packed):
    wide = packed.astype(FLOAT)
    return jnp.concatenate([turn(wide), wide], axis=0)


def build_pair(pair, features, spot, keys, values):
    lanes = lane_ids(pair.shape)
    rows = pl.ds(spot, pair.shape[0])
    keys[rows, :] = jnp.where(lanes < 64, pair, features)
    values[rows, :] = jnp.where(
        lanes < 64, jnp.where(lanes < 3, 1.0, 0.0).astype(LOW), pair
    )


def build_inputs(head, near_refs, query_ref, qf_ref, kf_ref, tf_ref, queries, keys, values, text_keys, text_values):
    rows = query_ref.shape[0]
    queries[...] = query_ref[...] + qf_ref[...]
    each = pl.cdiv(near_refs[0].shape[0], rows) - 1
    text_rows = (near_refs[0].shape[0] - each * rows) // each
    for index, ref in enumerate(near_refs):
        spot = pl.ds(pl.multiple_of(head * rows, rows), rows)
        build_pair(ref[spot, :], kf_ref[rows * index : rows * index + rows, :], rows * index, keys, values)
        spot = pl.ds(pl.multiple_of(each * rows + head * text_rows, 16), text_rows)
        first = text_rows * index
        build_pair(
            ref[spot, :], tf_ref[first : first + text_rows, :], first, text_keys, text_values
        )


def forward_kernel(near, chunk, *refs):
    near_refs, refs = refs[:near], refs[near:]
    query_ref, qf_ref, kf_ref, tf_ref, gate_ref = refs[:5]
    mixed_refs, refs = refs[5 : 5 + SPLIT], refs[5 + SPLIT :]
    outs_ref, stats_ref, queries, keys, values, text_keys, text_values, hold = refs
    build_inputs(
        pl.program_id(0), near_refs, query_ref, qf_ref, kf_ref, tf_ref,
        queries, keys, values, text_keys, text_values,
    )
    rows = queries.shape[0] // SPLIT * FORWARD_SLOTS
    text_chunk = pick_tile(text_keys.shape[0], 256)

    def tile_step(tile, carry):
        spot = pl.ds(pl.multiple_of(tile * rows, rows), rows)
        query = queries[spot, :]

        def attend(key_part, value_part):
            scores = matmul(query, key_part, 1, 1)
            return matmul(jnp.exp(scores).astype(LOW), value_part, 1, 0)

        def step(index, total):
            part = pl.ds(pl.multiple_of(index * chunk, chunk), chunk)
            return total + attend(keys[part, :], values[part, :])

        def text_step(index, total):
            part = pl.ds(pl.multiple_of(index * text_chunk, text_chunk), text_chunk)
            return total + attend(text_keys[part, :], text_values[part, :])

        blank = jnp.zeros((rows, 128), FLOAT)
        own = lax.fori_loop(0, keys.shape[0] // chunk, step, blank)
        cross = lax.fori_loop(0, text_keys.shape[0] // text_chunk, text_step, blank, unroll=True)
        own_inverse = 1.0 / own[:, 0:1]
        cross_inverse = 1.0 / cross[:, 0:1]
        own = own * own_inverse
        cross = cross * cross_inverse
        lanes = lane_ids(own.shape)
        mixed = own + gate_ref[0, 0:1, :] * cross
        each = rows // FORWARD_SLOTS
        for slot in range(FORWARD_SLOTS):
            hold[tile * FORWARD_SLOTS + slot] = fold_high(mixed[each * slot : each * slot + each])
        outs_ref[spot, :] = jnp.where(lanes < 64, turn(cross), own)
        stats_ref[spot, :] = jnp.where(lanes == 0, own_inverse, cross_inverse)
        return carry

    lax.fori_loop(0, SPLIT // FORWARD_SLOTS, tile_step, 0)
    for index, ref in enumerate(mixed_refs):
        ref[...] = hold[index]


def whole(shape):
    return pl.BlockSpec(shape, lambda i: (0,) * len(shape))


def attention_specs(pairs, queries, qf, kf, tf):
    return [whole(value.shape) for value in pairs] + [
        pl.BlockSpec(qf.shape, lambda i: (i, 0)),
        whole(qf.shape),
        whole(kf.shape),
        whole(tf.shape),
        pl.BlockSpec((1, 8, 128), lambda i: (i, 0, 0)),
    ]


def attention_scratch(qf, kf, tf):
    return [
        pltpu.VMEM(qf.shape, LOW),
        pltpu.VMEM(kf.shape, LOW),
        pltpu.VMEM(kf.shape, LOW),
        pltpu.VMEM(tf.shape, LOW),
        pltpu.VMEM(tf.shape, LOW),
    ]


def attention_forward(pairs, queries, qf, kf, tf, gates):
    rows = qf.shape[0]
    heads = gates.shape[0]
    half = rows // SPLIT // 2
    folded = jax.ShapeDtypeStruct((heads * half, 128), LOW)
    wide = jax.ShapeDtypeStruct((heads * rows, 128), FLOAT)
    out = pl.pallas_call(
        functools.partial(forward_kernel, len(pairs), pick_tile(kf.shape[0], 1024)),
        grid=(heads,),
        in_specs=attention_specs(pairs, queries, qf, kf, tf),
        out_specs=[pl.BlockSpec((half, 128), lambda i: (i, 0))] * SPLIT
        + [pl.BlockSpec((rows, 128), lambda i: (i, 0))] * 2,
        out_shape=[folded] * SPLIT + [wide] * 2,
        scratch_shapes=attention_scratch(qf, kf, tf) + [pltpu.VMEM((SPLIT, half, 128), LOW)],
        compiler_params=pltpu.CompilerParams(vmem_limit_bytes=60 * MIB),
        cost_estimate=SMALL,
    )(*pairs, queries, qf, kf, tf, gates)
    return out[:SPLIT], out[SPLIT], out[SPLIT + 1]


def backward_kernel(near, chunk, *refs):
    near_refs, refs = refs[:near], refs[near:]
    query_ref, qf_ref, kf_ref, tf_ref, gate_ref = refs[:5]
    refs = refs[5:]
    grad_refs, refs = refs[:SPLIT], refs[SPLIT:]
    outs_ref, stats_ref, refs = refs[0], refs[1], refs[2:]
    dq_refs, refs = refs[:SPLIT], refs[SPLIT:]
    dkv_refs, dt_refs, dg_ref = refs[:2], refs[2:4], refs[4]
    queries, keys, values, text_keys, text_values, hold, grad_hold, acc, text_acc = refs[5:]
    build_inputs(
        pl.program_id(0), near_refs, query_ref, qf_ref, kf_ref, tf_ref,
        queries, keys, values, text_keys, text_values,
    )
    for index, ref in enumerate(grad_refs):
        grad_hold[index] = ref[...]
    acc[...] = jnp.zeros_like(acc)
    text_acc[...] = jnp.zeros_like(text_acc)
    dg_ref[...] = jnp.zeros_like(dg_ref)
    rows = queries.shape[0] // SPLIT * BACKWARD_SLOTS
    text_chunk = pick_tile(text_keys.shape[0], 256)
    gate = gate_ref[0, 0:1, :]

    def tile_step(tile, carry):
        spot = pl.ds(pl.multiple_of(tile * rows, rows), rows)
        query = queries[spot, :]
        lanes = lane_ids(query.shape)
        query_low = jnp.where(lanes < 64, query, jnp.zeros_like(query))
        grads = jnp.concatenate(
            [unfold_high(grad_hold[tile * BACKWARD_SLOTS + slot]) for slot in range(BACKWARD_SLOTS)],
            axis=0,
        )
        grads = jnp.where(lanes < 64, 0.0, grads)
        outs = outs_ref[spot, :]
        cross_out = jnp.where(lanes < 64, 0.0, turn(outs))
        dg_ref[0] += jnp.sum((grads * cross_out).reshape(rows // 8, 8, 128), axis=0)
        cross_grads = (gate * grads).astype(LOW).astype(FLOAT)

        def widen(grad, out, inverse):
            delta = -jnp.sum(grad * out, axis=1, keepdims=True) * inverse
            first = delta.astype(LOW).astype(FLOAT)
            second = (delta - first).astype(LOW).astype(FLOAT)
            third = delta - first - second
            features = jnp.where(lanes == 0, first, jnp.where(lanes == 1, second, third))
            scaled = grad * inverse
            return jnp.where(lanes < 3, features, scaled).astype(LOW), scaled.astype(LOW)

        stats = stats_ref[spot, :]
        own_wide, own_low = widen(grads, outs, stats[:, 0:1])
        cross_wide, cross_low = widen(cross_grads, cross_out, stats[:, 1:2])
        own_pair = jnp.concatenate([query_low, own_low], axis=0)
        cross_pair = jnp.concatenate([query_low, cross_low], axis=0)

        def attend(key_part, value_part, wide, pair):
            weights = jnp.exp(matmul(key_part, query, 1, 1))
            grad_scores = (weights * matmul(value_part, wide, 1, 1)).astype(LOW)
            low = weights.astype(LOW)
            grad_pair = matmul(jnp.concatenate([grad_scores, low], axis=1), pair, 1, 0)
            return grad_pair, matmul(grad_scores, key_part, 0, 0)

        def step(index, total):
            part = pl.ds(pl.multiple_of(index * chunk, chunk), chunk)
            grad_pair, grad_query = attend(keys[part, :], values[part, :], own_wide, own_pair)
            acc[part, :] += grad_pair
            return total + grad_query

        def text_step(index, total):
            part = pl.ds(pl.multiple_of(index * text_chunk, text_chunk), text_chunk)
            grad_pair, grad_query = attend(
                text_keys[part, :], text_values[part, :], cross_wide, cross_pair
            )
            text_acc[part, :] += grad_pair
            return total + grad_query

        blank = jnp.zeros((rows, 128), FLOAT)
        total = lax.fori_loop(0, keys.shape[0] // chunk, step, blank, unroll=2)
        total = lax.fori_loop(0, text_keys.shape[0] // text_chunk, text_step, total, unroll=True)
        total = total * 0.125
        each = rows // BACKWARD_SLOTS
        for slot in range(BACKWARD_SLOTS):
            hold[tile * BACKWARD_SLOTS + slot] = fold_low(total[each * slot : each * slot + each])
        return carry

    lax.fori_loop(0, SPLIT // BACKWARD_SLOTS, tile_step, 0)
    for index, ref in enumerate(dq_refs):
        ref[...] = hold[index]
    for values, refs in ((acc, dkv_refs), (text_acc, dt_refs)):
        size = refs[0].shape[1]
        refs[0][0] = values[:size, :].astype(LOW)
        refs[1][0] = values[size:, :].astype(LOW)


def attention_backward(pairs, queries, qf, kf, tf, gates, grads, outs, stats):
    rows = qf.shape[0]
    heads = gates.shape[0]
    half = rows // SPLIT // 2
    folded = jax.ShapeDtypeStruct((heads * half, 128), LOW)
    piece = jax.ShapeDtypeStruct((heads, kf.shape[0] // 2, 128), LOW)
    text = jax.ShapeDtypeStruct((heads, tf.shape[0] // 2, 128), LOW)
    sums = jax.ShapeDtypeStruct((heads, 8, 128), FLOAT)
    out = pl.pallas_call(
        functools.partial(backward_kernel, len(pairs), pick_tile(kf.shape[0], 512)),
        grid=(heads,),
        in_specs=attention_specs(pairs, queries, qf, kf, tf)
        + [pl.BlockSpec((half, 128), lambda i: (i, 0))] * SPLIT
        + [pl.BlockSpec((rows, 128), lambda i: (i, 0))] * 2,
        out_specs=[pl.BlockSpec((half, 128), lambda i: (i, 0))] * SPLIT
        + [
            pl.BlockSpec((1,) + value.shape[1:], lambda i: (i, 0, 0))
            for value in (piece, piece, text, text, sums)
        ],
        out_shape=[folded] * SPLIT + [piece, piece, text, text, sums],
        scratch_shapes=attention_scratch(qf, kf, tf)
        + [
            pltpu.VMEM((SPLIT, half, 128), LOW),
            pltpu.VMEM((SPLIT, half, 128), LOW),
            pltpu.VMEM(kf.shape, FLOAT),
            pltpu.VMEM(tf.shape, FLOAT),
        ],
        compiler_params=pltpu.CompilerParams(vmem_limit_bytes=60 * MIB),
        cost_estimate=SMALL,
    )(*pairs, queries, qf, kf, tf, gates, *grads, outs, stats)
    return (out[:SPLIT],) + tuple(out[SPLIT:])


def half_means(values, lanes):
    low = jnp.sum(jnp.where(lanes < 64, values, 0.0), axis=1, keepdims=True)
    high = jnp.sum(jnp.where(lanes < 64, 0.0, values), axis=1, keepdims=True)
    return jnp.where(lanes < 64, low, high) * (1.0 / 64.0)


def swap_halves(values, lanes):
    return jnp.where(
        lax.rem(lanes, 64) < 32, pltpu.roll(values, 96, 1), pltpu.roll(values, 32, 1)
    )


def placed_at(groups, head, upper):
    values = groups[head // 2]
    return values if (head % 2 == 1) == upper else turn(values)


def rope_forward_kernel(heads, far_ref, qkv_ref, cos_ref, sin_ref, gains_ref, *refs):
    outs, hold = refs[:-1], refs[-1]
    width = heads * 64
    each = heads // SPLIT
    rows = qkv_ref.shape[0]
    cosine, sine = cos_ref[...], sin_ref[...]
    lanes = lane_ids(cosine.shape)

    def turned(start, gain):
        groups = []
        for index in range(heads // 2):
            raw = qkv_ref[:, start + 128 * index : start + 128 * index + 128]
            normed = raw * lax.rsqrt(half_means(raw * raw, lanes) + EPS) * gain
            groups.append(normed * cosine + swap_halves(normed, lanes) * sine)
        return groups

    queries = turned(0, gains_ref[0:1, :])
    keys = turned(width, gains_ref[1:2, :])
    values = [
        qkv_ref[:, 2 * width + 128 * index : 2 * width + 128 * index + 128]
        for index in range(heads // 2)
    ]
    for head in range(heads):
        group, index = head // each, head % each
        slot = lax.rem(group - far_ref[0] + SPLIT, SPLIT)
        pair = jnp.where(
            lanes < 64, placed_at(keys, head, False), placed_at(values, head, True)
        )
        hold[slot, index, :rows, :] = pair.astype(LOW)
        hold[slot, index, rows:, :] = fold_low(placed_at(queries, head, False))
    size = rows * 3 // 2
    for slot in range(SPLIT):
        for index in range(each):
            outs[slot][size * index : size * index + size, :] = hold[slot, index]


def small_call(kernel, operands, shapes, scratch):
    out = pl.pallas_call(
        kernel,
        in_specs=[pl.BlockSpec(memory_space=pltpu.SMEM)]
        + [pl.BlockSpec(memory_space=pltpu.VMEM)] * (len(operands) - 1),
        out_specs=[pl.BlockSpec(memory_space=pltpu.VMEM)] * len(shapes),
        out_shape=shapes,
        scratch_shapes=scratch,
        compiler_params=pltpu.CompilerParams(vmem_limit_bytes=32 * MIB),
        cost_estimate=SMALL,
    )(*operands)
    return out


def rope_forward(far, qkv, cosine, sine, gains, heads):
    rows = qkv.shape[0] * 3 // 2
    each = heads // SPLIT
    out = small_call(
        functools.partial(rope_forward_kernel, heads),
        (far, qkv, cosine, sine, gains),
        [jax.ShapeDtypeStruct((each * rows, 128), LOW)] * SPLIT,
        [pltpu.VMEM((SPLIT, each, rows, 128), LOW)],
    )
    return list(out)


def rope_backward_kernel(heads, far_ref, *refs):
    parts, refs = refs[:SPLIT], refs[SPLIT:]
    qkv_ref, cos_ref, sin_ref, gains_ref, out_ref, sums_ref, hold = refs
    width = heads * 64
    each = heads // SPLIT
    rows = qkv_ref.shape[0]
    for slot in range(SPLIT):
        group = lax.rem(far_ref[0] + slot, SPLIT)
        size = hold.shape[2]
        for index in range(each):
            hold[group, index] = parts[slot][size * index : size * index + size, :]
    cosine, sine = cos_ref[...], sin_ref[...]
    lanes = lane_ids(cosine.shape)

    def found(kind, head):
        group, index, upper = head // each, head % each, head % 2 == 1
        if kind == 0:
            packed = hold[group, index, rows:, :]
            return unfold_high(packed) if upper else unfold_low(packed)
        values = hold[group, index, :rows, :].astype(FLOAT)
        return values if upper == (kind == 2) else turn(values)

    def joined(kind, index):
        return jnp.where(lanes < 64, found(kind, 2 * index), found(kind, 2 * index + 1))

    for kind in range(2):
        gain = gains_ref[kind : kind + 1, :]
        total = jnp.zeros((1, 128), FLOAT)
        for index in range(heads // 2):
            spot = kind * width + 128 * index
            raw = qkv_ref[:, spot : spot + 128]
            inverse = lax.rsqrt(half_means(raw * raw, lanes) + EPS)
            unit = raw * inverse
            grad = joined(kind, index)
            back = grad * cosine - swap_halves(grad, lanes) * sine
            total = total + jnp.sum(back * unit, axis=0, keepdims=True)
            scaled = back * gain
            raw_grad = inverse * (scaled - unit * half_means(scaled * unit, lanes))
            out_ref[:, spot : spot + 128] = raw_grad.astype(LOW)
        sums_ref[kind : kind + 1, :] = total
    sums_ref[2:8, :] = jnp.zeros((6, 128), FLOAT)
    for index in range(heads // 2):
        spot = 2 * width + 128 * index
        out_ref[:, spot : spot + 128] = joined(2, index).astype(LOW)


def rope_backward(far, parts, qkv, cosine, sine, gains, heads):
    each = heads // SPLIT
    return small_call(
        functools.partial(rope_backward_kernel, heads),
        (far, *parts, qkv, cosine, sine, gains),
        [jax.ShapeDtypeStruct(qkv.shape, LOW), jax.ShapeDtypeStruct((8, 128), FLOAT)],
        [pltpu.VMEM((SPLIT, each, parts[0].shape[0] // each, 128), LOW)],
    )


def join_kernel(heads, far_ref, *refs):
    parts, out_ref, hold = refs[:SPLIT], refs[SPLIT], refs[SPLIT + 1]
    each = heads // SPLIT
    half = hold.shape[2]
    for slot in range(SPLIT):
        group = lax.rem(far_ref[0] + slot, SPLIT)
        for index in range(each):
            hold[group, index] = parts[slot][half * index : half * index + half, :]
    for pair in range(heads // 2):
        low = unfold_low(hold[2 * pair // each, 2 * pair % each])
        high = unfold_high(hold[(2 * pair + 1) // each, (2 * pair + 1) % each])
        out_ref[:, 128 * pair : 128 * pair + 128] = jnp.where(
            lane_ids(low.shape) < 64, low, high
        ).astype(LOW)


def join_heads(far, parts, heads):
    each = heads // SPLIT
    half = parts[0].shape[0] // each
    return small_call(
        functools.partial(join_kernel, heads),
        (far, *parts),
        [jax.ShapeDtypeStruct((2 * half, heads * 64), LOW)],
        [pltpu.VMEM((SPLIT, each, half, 128), LOW)],
    )[0]


def split_kernel(heads, far_ref, grad_ref, *refs):
    outs, hold = refs[:-1], refs[-1]
    each = heads // SPLIT
    half = hold.shape[2]
    for head in range(heads):
        group, index = head // each, head % each
        slot = lax.rem(group - far_ref[0] + SPLIT, SPLIT)
        values = grad_ref[:, 128 * (head // 2) : 128 * (head // 2) + 128]
        hold[slot, index] = fold_high(values) if head % 2 else fold_low(values)
    for slot in range(SPLIT):
        for index in range(each):
            outs[slot][half * index : half * index + half, :] = hold[slot, index]


def split_heads(far, grads, heads):
    each = heads // SPLIT
    half = grads.shape[0] // 2
    return small_call(
        functools.partial(split_kernel, heads),
        (far, grads),
        [jax.ShapeDtypeStruct((each * half, 128), LOW)] * SPLIT,
        [pltpu.VMEM((SPLIT, each, half, 128), LOW)],
    )


def local_call(kernel, operands, shapes):
    return pl.pallas_call(
        kernel,
        out_shape=shapes,
        compiler_params=pltpu.CompilerParams(vmem_limit_bytes=40 * MIB),
        cost_estimate=SMALL,
    )(*operands)


def gather_kernel(each, *refs):
    slots, text_ref, pairs_ref, queries_ref = refs[:SPLIT], refs[SPLIT], refs[-2], refs[-1]
    size = slots[0].shape[0] // each
    rows = size * 2 // 3
    for head in range(each):
        for index, slot in enumerate(slots):
            spot = (head * SPLIT + index) * rows
            first = head * size
            pairs_ref[spot : spot + rows, :] = slot[first : first + rows, :]
            query = unfold_low(slot[first + rows : first + size, :])
            query = jnp.where(lane_ids(query.shape) < 64, query * 0.125, 0.0)
            queries_ref[spot : spot + rows, :] = query.astype(LOW)
    pairs_ref[each * SPLIT * rows :, :] = text_ref[...]


def gather_slots(slots, text, each):
    rows = slots[0].shape[0] * 2 // 3 * SPLIT
    return local_call(
        functools.partial(gather_kernel, each),
        (*slots, text),
        [
            jax.ShapeDtypeStruct((rows + text.shape[0], 128), LOW),
            jax.ShapeDtypeStruct((rows, 128), LOW),
        ],
    )


def pack_kernel(terms, *refs):
    inputs, folded, outs = refs[:terms], refs[terms : terms + SPLIT], refs[terms + SPLIT :]
    each = inputs[0].shape[0]
    size = outs[0].shape[0] // each
    rows = size * 2 // 3
    half = size - rows
    for head in range(each):
        for slot in range(SPLIT):
            total = sum(
                term[head, rows * slot : rows * slot + rows, :].astype(FLOAT) for term in inputs
            )
            spot = size * head
            outs[slot][spot : spot + rows, :] = total.astype(LOW)
            outs[slot][spot + rows : spot + size, :] = folded[slot][
                half * head : half * head + half, :
            ]


def pack_slots(terms, folded):
    return local_call(
        functools.partial(pack_kernel, len(terms)),
        (*terms, *folded),
        [jax.ShapeDtypeStruct((3 * folded[0].shape[0], 128), LOW)] * SPLIT,
    )


def text_split_kernel(far_ref, text_ref, *outs):
    size = outs[0].shape[1]
    for slot in range(SPLIT):
        group = lax.rem(far_ref[0] + slot, SPLIT)
        spot = pl.ds(pl.multiple_of(group * size, 128), size)
        outs[slot][...] = text_ref[:, spot].astype(LOW)


def text_join_kernel(far_ref, *refs):
    parts, out_ref = refs[:SPLIT], refs[SPLIT]
    size = parts[0].shape[1]
    for slot in range(SPLIT):
        group = lax.rem(far_ref[0] + slot, SPLIT)
        out_ref[:, pl.ds(pl.multiple_of(group * size, 128), size)] = parts[slot][...]


def low_means(values, lanes):
    return jnp.sum(jnp.where(lanes < 64, values, 0.0), axis=1, keepdims=True) * (1.0 / 64.0)


def text_norm_kernel(*refs):
    parts, gain_ref, raw_ref, out_ref = refs[:SPLIT], refs[SPLIT], refs[-2], refs[-1]
    rows = raw_ref.shape[0]
    raw = sum(part[...].astype(FLOAT) for part in parts)
    raw_ref[...] = raw
    for head in range(raw.shape[1] // 128):
        values = raw[:, 128 * head : 128 * head + 128]
        lanes = lane_ids(values.shape)
        normed = values * lax.rsqrt(low_means(values * values, lanes) + EPS) * gain_ref[0:1, :]
        out_ref[rows * head : rows * head + rows, :] = jnp.where(
            lanes < 64, normed, values
        ).astype(LOW)


def text_back_kernel(terms, *refs):
    inputs, refs = refs[:terms], refs[terms:]
    raw_ref, gain_ref, out_ref, sums_ref = refs
    rows = raw_ref.shape[0]
    total_gain = jnp.zeros((1, 128), FLOAT)
    for head in range(inputs[0].shape[0]):
        grad = sum(term[head, :rows, :].astype(FLOAT) for term in inputs)
        grad = grad.astype(LOW).astype(FLOAT)
        raw = raw_ref[:, 128 * head : 128 * head + 128]
        lanes = lane_ids(raw.shape)
        inverse = lax.rsqrt(low_means(raw * raw, lanes) + EPS)
        unit = raw * inverse
        total_gain = total_gain + jnp.sum(grad * unit, axis=0, keepdims=True)
        scaled = grad * gain_ref[0:1, :]
        back = inverse * (scaled - unit * low_means(scaled * unit, lanes))
        out_ref[:, 128 * head : 128 * head + 128] = jnp.where(lanes < 64, back, grad).astype(LOW)
    sums_ref[...] = jnp.broadcast_to(total_gain, sums_ref.shape)


def tie(*values):
    return lax.optimization_barrier(values)


def stacked_kernel(left_ref, own_ref, other_ref, out_ref):
    rows = own_ref.shape[1]
    out_ref[...] = (
        matmul(left_ref[:, :rows], own_ref[0], 1, 0)
        + matmul(left_ref[:, rows:], other_ref[0], 1, 0)
    ).astype(LOW)


def stacked_outer(left, own, other, tile):
    depth = left.shape[0]
    count, rows, columns = own.shape
    tiles = columns // tile
    part = pl.BlockSpec((1, rows, tile), lambda i: (i // tiles, 0, i % tiles))
    return pl.pallas_call(
        stacked_kernel,
        grid=(count * tiles,),
        in_specs=[pl.BlockSpec(left.shape, lambda i: (0, 0)), part, part],
        out_specs=pl.BlockSpec((depth, tile), lambda i: (0, i)),
        out_shape=jax.ShapeDtypeStruct((depth, count * columns), LOW),
        compiler_params=pltpu.CompilerParams(vmem_limit_bytes=40 * MIB),
        cost_estimate=SMALL,
    )(left, own, other)


def joint_kernel(count, left_ref, own_ref, other_ref, own_last_ref, other_last_ref, out_ref):
    step = pl.program_id(0)
    rows = own_ref.shape[1]

    @pl.when(step < count)
    def _():
        out_ref[...] = (
            matmul(left_ref[0, :, :rows], own_ref[0], 1, 0)
            + matmul(left_ref[0, :, rows:], other_ref[0], 1, 0)
        ).astype(LOW)

    @pl.when(step >= count)
    def _():
        out_ref[...] = (
            matmul(left_ref[0, :, :rows], own_last_ref[...], 1, 0)
            + matmul(left_ref[0, :, rows:], other_last_ref[...], 1, 0)
        ).astype(LOW)


def joint_outer(left, own, other, own_last, other_last, tile):
    depth, tokens = left.shape[1:]
    rows, columns = own.shape[1:]
    tiles = columns // tile
    count = own.shape[0] * tiles
    extra = own_last.shape[1] // tile

    def right_at(i):
        at = jnp.minimum(i, count - 1)
        return (at // tiles, 0, at % tiles)

    def left_at(i):
        return (jnp.where(i < 2 * tiles, 0, jnp.where(i < count, 1, 2)), 0, 0)

    right = pl.BlockSpec((1, rows, tile), right_at)
    last = pl.BlockSpec((rows, tile), lambda i: (0, jnp.maximum(i - count, 0)))
    return pl.pallas_call(
        functools.partial(joint_kernel, count),
        grid=(count + extra,),
        in_specs=[
            pl.BlockSpec((1, depth, tokens), left_at),
            right,
            right,
            last,
            last,
        ],
        out_specs=pl.BlockSpec((depth, tile), lambda i: (0, i)),
        out_shape=jax.ShapeDtypeStruct((depth, (count + extra) * tile), LOW),
        compiler_params=pltpu.CompilerParams(vmem_limit_bytes=40 * MIB),
        cost_estimate=SMALL,
    )(left, own, other, own_last, other_last)


def feed_kernel(
    normed_ref, grad_ref, gate_ref, up_ref, down_ref,
    grads_ref, feed_own_ref, feed_other_ref, norm_own_ref, norm_other_ref,
    feed_acc, norm_acc,
):
    step = pl.program_id(0)

    @pl.when(step == 0)
    def _():
        feed_acc[...] = jnp.zeros_like(feed_acc)
        norm_acc[...] = jnp.zeros_like(norm_acc)

    normed = normed_ref[...]
    gate = matmul(normed, gate_ref[...], 1, 0)
    up = matmul(normed, up_ref[...], 1, 0)
    grad_hidden = matmul(grad_ref[...], down_ref[...], 1, 0)
    sigmoid = 1.0 / (1.0 + jnp.exp(-gate))
    silu = gate * sigmoid
    hidden = (silu * up).astype(LOW)
    grad_gate = (grad_hidden * up * sigmoid * (1.0 + gate * (1.0 - sigmoid))).astype(LOW)
    grad_up = (grad_hidden * silu).astype(LOW)
    grads_ref[2] = hidden
    grads_ref[0] = grad_gate
    grads_ref[1] = grad_up
    feed_acc[...] += matmul(hidden, down_ref[...], 1, 1)
    norm_acc[...] += matmul(grad_gate, gate_ref[...], 1, 1) + matmul(grad_up, up_ref[...], 1, 1)

    @pl.when(step == pl.num_programs(0) - 1)
    def _():
        half = feed_own_ref.shape[0]
        feed_own_ref[...] = feed_acc[:half, :]
        feed_other_ref[...] = feed_acc[half:, :].astype(LOW)
        norm_own_ref[...] = norm_acc[:half, :]
        norm_other_ref[...] = norm_acc[half:, :].astype(LOW)


def feed_forward(normed, grads, weights, columns, tile):
    rows, width = normed.shape
    tiles = columns // tile
    own = jax.ShapeDtypeStruct((rows // 2, width), FLOAT)
    other = jax.ShapeDtypeStruct((rows // 2, width), LOW)
    return pl.pallas_call(
        feed_kernel,
        grid=(tiles,),
        in_specs=[whole(normed.shape), whole(grads.shape)]
        + [
            pl.BlockSpec((width, tile), lambda i, part=part: (0, part * tiles + i))
            for part in range(3)
        ],
        out_specs=[
            pl.BlockSpec((3, rows, tile), lambda i: (0, 0, i)),
        ]
        + [whole(own.shape)] * 4,
        out_shape=[
            jax.ShapeDtypeStruct((3, rows, columns), LOW),
            own,
            other,
            own,
            other,
        ],
        scratch_shapes=[pltpu.VMEM((rows, width), FLOAT)] * 2,
        compiler_params=pltpu.CompilerParams(vmem_limit_bytes=48 * MIB),
        cost_estimate=SMALL,
    )(normed, grads, weights, weights, weights)


def dot_float(left, right):
    return jnp.dot(left, right, preferred_element_type=FLOAT)


def dot_turned(left, right):
    return matmul(left, right, 1, 1)


def norm_rows(values, gains):
    return values * lax.rsqrt(jnp.mean(values * values, axis=-1, keepdims=True) + EPS) * gains


def modulated(values, gains, shifts, scales):
    return norm_rows(values, gains) * (1.0 + scales) + shifts


def swapped(values):
    return lax.ppermute(values, "tensor", [(0, 1), (1, 0)])


def both_rows(values):
    return jnp.concatenate([values, swapped(values)], axis=0)


def own_rows(partial):
    rows = partial.shape[0] // 2
    return partial[:rows] + swapped(partial[rows:].astype(LOW)).astype(FLOAT)


def shards(
    inputs,
    clip_ids,
    positions,
    text_tokens,
    conditioning,
    ada_weight,
    ada_bias,
    first_norm_gain,
    query_gain,
    key_gain,
    text_key_gain,
    head_gate,
    qkv_weight,
    out_weight,
    text_kv_weight,
    second_norm_gain,
    gate_up_weight,
    down_weight,
    grad_output,
):
    dp = lax.axis_size("dp")
    near = dp // SPLIT
    bits = [near >> (step + 1) for step in range(near.bit_length() - 1)]
    tensor_index = lax.axis_index("tensor")
    dp_index = lax.axis_index("dp")
    far_index, near_index = dp_index // near, dp_index % near
    row_count, width = inputs.shape
    token_count = clip_ids.shape[0]
    head_size = query_gain.shape[0]
    local_width = qkv_weight.shape[2]
    heads = local_width // head_size
    each = heads // SPLIT
    part_width = each * head_size
    clip_count = conditioning.shape[0]
    hidden_count = gate_up_weight.shape[2]
    weight_rows = qkv_weight.shape[1]

    def flip(values, bit):
        return lax.ppermute(values, "dp", [(j, j ^ bit) for j in range(dp)])

    def shift(values, steps):
        pairs = [(j, ((j // near + steps) % SPLIT) * near + j % near) for j in range(dp)]
        return lax.ppermute(values, "dp", pairs)

    def sum_dp(values):
        step = 1
        while step < dp:
            values = values + flip(values, step)
            step *= 2
        return values

    def spread(values):
        for bit in bits:
            values = jnp.concatenate([values, flip(values, bit)], axis=0)
        return values

    def spread_list(values):
        values = [values]
        for bit in bits:
            values = values + [flip(value, bit) for value in values]
        return values

    def collect(values):
        for bit in reversed(bits):
            half = values.shape[0] // 2
            values = values[:half].astype(FLOAT) + flip(
                values[half:].astype(LOW), bit
            ).astype(FLOAT)
        return values

    def pick(stacked, index):
        return lax.dynamic_index_in_dim(stacked, index, 0, keepdims=False)

    def send_parts(stacked):
        out = [pick(stacked, far_index)]
        for steps in range(1, SPLIT):
            out.append(shift(pick(stacked, (far_index + steps) % SPLIT), steps))
        return out

    def send_slots(slots):
        return [slots[0]] + [shift(slots[steps], steps) for steps in range(1, SPLIT)]

    def return_slots(slots):
        return [slots[0]] + [shift(slots[steps], -steps) for steps in range(1, SPLIT)]

    flips = []
    for order in range(near):
        mask = 0
        for place, bit in enumerate(bits):
            if order >> place & 1:
                mask |= bit
        flips.append(mask)

    core = dp_index % 2
    core_groups = [list(range(first, dp, 2)) for first in range(2)]

    def core_columns(values):
        halves = (
            values.T.reshape(dp // 2, 2, weight_rows, token_count)
            .transpose(1, 0, 2, 3)
            .reshape(2, width // 2, token_count)
        )
        return jnp.concatenate([pick(halves, core), flip(pick(halves, 1 - core), 1)], axis=1)

    def scatter(values):
        return lax.psum_scatter(
            values, "dp", scatter_dimension=0, axis_index_groups=core_groups, tiled=True
        )

    qkv_full = lax.all_gather(
        qkv_weight.transpose(1, 0, 2).reshape(weight_rows, 3 * local_width),
        "dp",
        axis=0,
        tiled=True,
    )
    cond_float = conditioning.astype(FLOAT)
    silu_cond = jax.nn.silu(cond_float).astype(LOW)
    cond_rows = ada_weight.shape[0]
    silu_slice = lax.dynamic_slice_in_dim(silu_cond, dp_index * cond_rows, cond_rows, axis=1)
    first_rows = jnp.sum((clip_ids == 0).astype(FLOAT))
    spots = jnp.arange(ada_weight.shape[1], dtype=jnp.int32)
    early = 2 * width
    early_part = jnp.concatenate(
        [
            dot_float(silu_slice, ada_weight[:, :early]),
            jnp.where(spots[:early] == dp_index, first_rows, 0.0)[None],
        ],
        axis=0,
    )
    text_columns = lax.all_to_all(text_tokens, "dp", split_axis=1, concat_axis=0, tiled=True)
    early_part, text_columns = tie(early_part, text_columns)
    early_sum = sum_dp(early_part)
    bias = ada_bias.astype(FLOAT)
    early_mod = early_sum[:clip_count] + bias[:early]
    counts = early_sum[clip_count, :dp].astype(jnp.int32)

    own_ids = lax.dynamic_slice_in_dim(clip_ids, tensor_index * row_count, row_count)
    row_positions = jnp.where(
        tensor_index == 0, positions, jnp.roll(positions, row_count)
    )
    other_clip = jnp.max(clip_ids)
    first_clip = (own_ids == 0)[:, None]

    def mod_blocks(modulation):
        rows = jnp.where(
            first_clip,
            modulation[0:1],
            lax.dynamic_slice_in_dim(modulation, other_clip, 1, 0),
        )
        return jnp.split(rows, rows.shape[1] // width, axis=1)

    shift_one, scale_one = mod_blocks(early_mod)
    input_rows = inputs.astype(FLOAT)
    first_gain = first_norm_gain.astype(FLOAT)
    normed_one = modulated(input_rows, first_gain, shift_one, scale_one).astype(LOW)
    normed_all = both_rows(normed_one)
    late_sum = sum_dp(dot_float(silu_slice, ada_weight[:, early:]))

    half_size = head_size // 2
    frequency = 10000.0 ** (-(jnp.arange(half_size, dtype=FLOAT) * 2.0 / head_size))
    angles = row_positions.astype(FLOAT)[:, None] * frequency[None, :]
    cosine = jnp.cos(angles)
    sine = jnp.sin(angles)
    cosine = jnp.concatenate([cosine] * 4, axis=1)
    sine = jnp.concatenate([-sine, sine, -sine, sine], axis=1)
    gains = jnp.stack([jnp.tile(query_gain, 2), jnp.tile(key_gain, 2)]).astype(FLOAT)
    gains = jnp.concatenate([gains, jnp.zeros((6, 128), FLOAT)], axis=0)

    text_rows = text_tokens.shape[0]
    group_rows = text_rows * SPLIT
    text_groups = text_columns.reshape(near, group_rows, text_columns.shape[1])
    text_near = jnp.concatenate([pick(text_groups, near_index ^ mask) for mask in flips], axis=0)
    text_weight = (
        text_kv_weight.reshape(2, -1, SPLIT, each, head_size)
        .transpose(1, 2, 3, 0, 4)
        .reshape(-1, 2 * local_width)
    )
    far = far_index.astype(jnp.int32).reshape(1)
    text_sum = collect(dot_float(text_near, text_weight))
    part_shape = jax.ShapeDtypeStruct((group_rows, 2 * part_width), LOW)
    text_parts = small_call(text_split_kernel, (far, text_sum), [part_shape] * SPLIT, [])
    ky_gain = jnp.concatenate([text_key_gain.astype(FLOAT), jnp.zeros((128 - head_size,), FLOAT)])
    ky_gain = jnp.broadcast_to(ky_gain[None], (8, 128))

    lanes = jnp.arange(128, dtype=jnp.int32)[None, :]
    text_groups_at = jnp.stack([near_index ^ mask for mask in flips])
    text_clip = (
        text_groups_at[:, None] * group_rows + jnp.arange(group_rows, dtype=jnp.int32)[None, :]
    ).reshape(-1) // TXT
    text_features = (lanes == 64 + text_clip[:, None]).astype(LOW)
    block_at = jnp.stack(
        [
            ((far_index - steps) % SPLIT) * near + (near_index ^ mask)
            for mask in flips
            for steps in range(SPLIT)
        ]
    )
    block_count = jnp.sum(
        jnp.where(block_at[:, None] == jnp.arange(dp, dtype=jnp.int32)[None, :], counts[None, :], 0),
        axis=1,
    )
    row_at = (jnp.arange(token_count, dtype=jnp.int32) + tensor_index * row_count) % token_count
    key_clip = jnp.where(
        row_at[None, :] < block_count[:, None], 0, 1 + block_at[:, None] // GROUP
    ).reshape(-1)
    key_features = (lanes == 64 + key_clip[:, None]).astype(LOW)
    group_tokens = SPLIT * token_count
    query_clip = key_clip[:group_tokens, None]
    query_features = jnp.where(
        (lanes >= 64) & (lanes < 64 + clip_count) & (lanes != 64 + query_clip), MASK, 0.0
    ).astype(LOW)
    gate_heads = jnp.tanh(
        lax.dynamic_slice_in_dim(
            head_gate.astype(FLOAT), tensor_index * heads + far_index * each, each
        )
    )
    gate_lanes = jnp.broadcast_to(gate_heads[:, None, None], (each, 8, 128))

    rest_weights, qkv_full, normed_all, text_parts, late_sum, key_features, query_features = tie(
        jnp.concatenate(
            [gate_up_weight[0], gate_up_weight[1], down_weight.T, out_weight.T], axis=1
        ),
        qkv_full,
        normed_all,
        text_parts,
        late_sum,
        key_features,
        query_features,
    )
    rest_full = lax.all_gather(rest_weights, "dp", axis=0, tiled=True)
    out_full = rest_full[:, 3 * hidden_count :]
    text_arrived = send_slots(text_parts)
    qkv_raw = dot_float(normed_all, qkv_full)
    head_slots = rope_forward(far, qkv_raw, cosine, sine, gains, heads)
    gate_one, shift_two, scale_two, gate_two = mod_blocks(late_sum + bias[early:])
    grad_two = grad_output.astype(FLOAT)
    grad_ffn = both_rows((gate_two * grad_two).astype(LOW))
    head_slots, text_arrived = tie(head_slots, text_arrived)
    text_raw, text_pairs = local_call(
        text_norm_kernel,
        (*text_arrived, ky_gain),
        [
            jax.ShapeDtypeStruct((group_rows, 2 * part_width), FLOAT),
            jax.ShapeDtypeStruct((each * group_rows, 128), LOW),
        ],
    )
    arrived = send_slots(head_slots)
    own_pairs, queries = gather_slots(arrived, text_pairs, each)
    pairs = spread_list(own_pairs)
    pairs, grad_ffn = tie(pairs, grad_ffn)
    mixed_slots, head_outs, head_stats = attention_forward(
        pairs, queries, query_features, key_features, text_features, gate_lanes
    )
    mixed = join_heads(far, return_slots(mixed_slots), heads)
    attn_rows = own_rows(dot_turned(mixed, out_full))
    after_attn = input_rows + gate_one * attn_rows
    second_gain = second_norm_gain.astype(FLOAT)
    normed_two_all = both_rows(modulated(after_attn, second_gain, shift_two, scale_two).astype(LOW))
    feed_grads, feed_own, feed_other, norm_own, norm_other = feed_forward(
        normed_two_all, grad_ffn, rest_full, hidden_count, 512
    )
    grad_normed_two = norm_own + swapped(norm_other).astype(FLOAT)
    _, pull_two = jax.vjp(modulated, after_attn, second_gain, shift_two, scale_two)
    back_two, grad_second_gain, grad_shift_two, grad_scale_two = pull_two(grad_normed_two)
    grad_after = grad_two + back_two
    grad_attn, feed_other = tie(both_rows((gate_one * grad_after).astype(LOW)), feed_other)
    ffn_rows = feed_own + swapped(feed_other).astype(FLOAT)
    output = (after_attn + gate_two * ffn_rows).astype(LOW)
    grad_gate_two = grad_two * ffn_rows
    grad_gate_one = grad_after * attn_rows
    grad_slots = send_slots(split_heads(far, dot_float(grad_attn, out_full), heads))
    joint_grads = joint_outer(
        jnp.stack(
            [core_columns(normed_two_all), core_columns(grad_ffn), core_columns(grad_attn)]
        ),
        feed_grads,
        flip(feed_grads, 1),
        mixed,
        flip(mixed, 1),
        256,
    )
    normed_core = core_columns(normed_all)
    grad_slots, joint_grads, normed_core = tie(grad_slots, joint_grads, normed_core)
    joint_low = scatter(joint_grads)

    def total_rows(terms, first, last):
        return sum(term[:, first:last].astype(FLOAT) for term in terms).astype(LOW)

    def start_sums(keep, send, text_keep, text_send):
        return (
            [keep, flip(send, bits[-1])],
            [text_keep, flip(text_send, bits[-1])],
        )

    def next_send(state):
        terms, text_terms = state
        size, text_size = terms[-1].shape[1], text_terms[-1].shape[1]
        return jnp.concatenate(
            [
                total_rows(terms, size // 2, size),
                total_rows(text_terms, text_size // 2, text_size),
            ],
            axis=1,
        )

    def next_state(state, sent, bit):
        terms, text_terms = state
        size = terms[-1].shape[1] // 2
        other = flip(sent, bit)
        return terms + [other[:, :size]], text_terms + [other[:, size:]]

    folded, *pieces, gate_parts = attention_backward(
        pairs,
        queries,
        query_features,
        key_features,
        text_features,
        gate_lanes,
        grad_slots,
        head_outs,
        head_stats,
    )
    state = start_sums(*pieces)
    for bit in reversed(bits[:-1]):
        state = next_state(state, next_send(state), bit)
    pair_terms, text_terms = state
    back_slots = pack_slots(pair_terms, folded)
    clip_at = jnp.arange(clip_count, dtype=jnp.int32)[:, None]

    def clip_sums(values):
        first_sum = jnp.sum(jnp.where(first_clip, values, 0.0), axis=0)[None]
        other_sum = jnp.sum(jnp.where(first_clip, 0.0, values), axis=0)[None]
        return jnp.where(clip_at == 0, first_sum, jnp.where(clip_at == other_clip, other_sum, 0.0))

    def pair_sums(blocks, gains_row):
        wide = jnp.concatenate([clip_sums(values) for values in blocks], axis=1)
        gains_row = jnp.concatenate(
            [gains_row, jnp.zeros((wide.shape[1] - gains_row.shape[0],), FLOAT)]
        )
        wide = jnp.concatenate([wide, gains_row[None]], axis=0)
        return wide + swapped(wide)

    back_parts = return_slots(back_slots)
    text_low, ky_sums = local_call(
        functools.partial(text_back_kernel, len(text_terms)),
        (*text_terms, text_raw, ky_gain),
        [part_shape, jax.ShapeDtypeStruct((8, 128), FLOAT)],
    )
    back_parts, text_low = tie(back_parts, text_low)
    qkv_grad, gain_sums = rope_backward(far, back_parts, qkv_raw, cosine, sine, gains, heads)
    grad_normed_one = own_rows(dot_turned(qkv_grad, qkv_full))
    qkv_right = qkv_grad[None]
    qkv_grads = stacked_outer(
        normed_core, qkv_right, flip(qkv_right, 1), local_width
    )
    qkv_grads, joint_low = tie(qkv_grads, joint_low)
    qkv_low = scatter(qkv_grads)
    grad_normed_one, qkv_grads = tie(grad_normed_one, qkv_grads)
    _, pull_one = jax.vjp(modulated, input_rows, first_gain, shift_one, scale_one)
    back_one, grad_first_gain, grad_shift_one, grad_scale_one = pull_one(grad_normed_one)
    grad_inputs = grad_after + back_one
    head_sums = (1.0 - gate_heads * gate_heads) * jnp.sum(gate_parts, axis=(1, 2))
    head_row = lax.dynamic_update_slice_in_dim(
        jnp.zeros((head_gate.shape[0],), FLOAT),
        head_sums,
        tensor_index * heads + far_index * each,
        0,
    )
    gain_halves = gain_sums[:2, :head_size] + gain_sums[:2, head_size:]
    all_pairs = pair_sums(
        (
            grad_shift_one,
            grad_scale_one,
            grad_gate_one,
            grad_shift_two,
            grad_scale_two,
            grad_gate_two,
        ),
        jnp.concatenate(
            [
                grad_first_gain,
                grad_second_gain,
                gain_halves.reshape(-1),
                ky_sums[0, :head_size],
                head_row,
            ]
        ),
    )
    text_wide = small_call(
        text_join_kernel,
        (far, *return_slots([text_low] * SPLIT)),
        [jax.ShapeDtypeStruct((group_rows, 2 * local_width), LOW)],
        [],
    )[0]
    text_all = spread(text_wide)
    all_pairs, text_all = tie(all_pairs, text_all)
    grad_sums = sum_dp(all_pairs)
    grad_mod_low, sums = grad_sums[:clip_count].astype(LOW), grad_sums[clip_count]
    first_gain_sum = sums[:width]
    second_gain_sum = sums[width : 2 * width]
    at = 2 * width
    q_gain_sum = sums[at : at + head_size]
    k_gain_sum = sums[at + head_size : at + 2 * head_size]
    ky_gain_sum = sums[at + 2 * head_size : at + 3 * head_size]
    gate_sum = sums[at + 3 * head_size : at + 3 * head_size + head_gate.shape[0]]
    grad_text_kv = (
        matmul(text_near, text_all, 0, 0)
        .reshape(-1, SPLIT, each, 2, head_size)
        .transpose(3, 0, 1, 2, 4)
        .reshape(2, -1, local_width)
    )
    grad_text_part = dot_turned(text_all, text_weight).astype(LOW)
    grad_text_pair = grad_text_part.astype(FLOAT) + swapped(grad_text_part).astype(FLOAT)
    grad_text_groups = grad_text_pair.astype(LOW).reshape(near, group_rows, -1)
    orders = jnp.arange(near, dtype=jnp.int32)
    flip_at = jnp.array(flips, jnp.int32)
    grad_text_rows = jnp.concatenate(
        [
            pick(grad_text_groups, jnp.sum(jnp.where(flip_at == near_index ^ group, orders, 0)))
            for group in range(near)
        ],
        axis=0,
    )
    grad_text_all = lax.all_to_all(grad_text_rows, "dp", split_axis=0, concat_axis=1, tiled=True)
    half_text = text_tokens.shape[1] // 2
    grad_text = lax.dynamic_slice_in_dim(
        grad_text_all, tensor_index * half_text, half_text, 1
    ).astype(FLOAT)
    grad_ada_bias = jnp.sum(grad_mod_low.astype(FLOAT), axis=0)
    grad_ada = matmul(silu_slice, grad_mod_low, 0, 0)
    cond_part = lax.dynamic_update_slice_in_dim(
        jnp.zeros(cond_float.shape, FLOAT),
        dot_turned(grad_mod_low, ada_weight),
        dp_index * cond_rows,
        1,
    )
    cond_sigmoid = jax.nn.sigmoid(cond_float)
    grad_conditioning = (
        sum_dp(cond_part) * cond_sigmoid * (1.0 + cond_float * (1.0 - cond_sigmoid))
    )
    qkv_shard = qkv_low.astype(FLOAT).reshape(weight_rows, 3, local_width).transpose(1, 0, 2)
    joint_shard = joint_low.astype(FLOAT)
    gate_up_shard = jnp.stack(
        [joint_shard[:, :hidden_count], joint_shard[:, hidden_count : 2 * hidden_count]]
    )
    out_shard = joint_shard[:, 3 * hidden_count :]
    down_shard = joint_shard[:, 2 * hidden_count : 3 * hidden_count]
    return (
        output,
        grad_inputs,
        grad_text,
        grad_conditioning,
        grad_ada,
        grad_ada_bias,
        first_gain_sum,
        q_gain_sum,
        k_gain_sum,
        ky_gain_sum,
        gate_sum,
        qkv_shard,
        out_shard.T,
        grad_text_kv,
        second_gain_sum,
        gate_up_shard,
        down_shard.T,
    )


def solution(mesh):
    placed = (
        P(("dp", "tensor"), None),
        P("dp"),
        P("dp"),
        P("dp", None),
        P(),
        P("dp", None),
        P(),
        P(),
        P(),
        P(),
        P(),
        P(),
        P(None, "dp", "tensor"),
        P("tensor", "dp"),
        P(None, "dp", "tensor"),
        P(),
        P(None, "dp", "tensor"),
        P("tensor", "dp"),
        P(("dp", "tensor"), None),
    )
    return jax.shard_map(
        shards,
        mesh=mesh,
        in_specs=placed,
        out_specs=(
            P(("dp", "tensor"), None),
            P(("dp", "tensor"), None),
            P("dp", "tensor"),
            P(),
            P("dp", None),
            P(),
            P(),
            P(),
            P(),
            P(),
            P(),
            P(None, "dp", "tensor"),
            P("tensor", "dp"),
            P(None, "dp", "tensor"),
            P(),
            P(None, "dp", "tensor"),
            P("tensor", "dp"),
        ),
        check_vma=False,
    )
```

```python
import functools

import jax
import jax.numpy as jnp
from jax import lax
from jax.experimental import pallas as pl
from jax.experimental.pallas import tpu as pltpu
from jax.sharding import PartitionSpec as P

TXT = 256
GROUP = 8
SPLIT = 4
EPS = 1e-06
MASK = -1e4
FORWARD_SLOTS = 4
LOW = jnp.bfloat16
FLOAT = jnp.float32
MIB = 1024 * 1024
SMALL = pl.CostEstimate(flops=1024, bytes_accessed=1024, transcendentals=0)


def pick_tile(total, most):
    size = most
    while total % size:
        size //= 2
    return size


def matmul(left, right, left_dim, right_dim):
    return lax.dot_general(
        left, right, (((left_dim,), (right_dim,)), ((), ())), preferred_element_type=jnp.float32
    )


def lane_ids(shape):
    return lax.broadcasted_iota(jnp.int32, shape, len(shape) - 1)


def turn(values):
    return pltpu.roll(values, 64, 1)


def fold_low(values):
    half = values.shape[0] // 2
    top, bottom = values[:half], turn(values)[half:]
    return jnp.where(lane_ids(top.shape) < 64, top, bottom).astype(LOW)


def fold_high(values):
    half = values.shape[0] // 2
    top, bottom = turn(values)[:half], values[half:]
    return jnp.where(lane_ids(top.shape) < 64, top, bottom).astype(LOW)


def unfold_low(packed):
    wide = packed.astype(FLOAT)
    return jnp.concatenate([wide, turn(wide)], axis=0)


def unfold_high(packed):
    wide = packed.astype(FLOAT)
    return jnp.concatenate([turn(wide), wide], axis=0)


def build_pair(pair, features, spot, keys, values):
    lanes = lane_ids(pair.shape)
    rows = pl.ds(spot, pair.shape[0])
    keys[rows, :] = jnp.where(lanes < 64, pair, features)
    values[rows, :] = jnp.where(
        lanes < 64, jnp.where(lanes < 3, 1.0, 0.0).astype(LOW), pair
    )


def build_inputs(head, near_refs, query_ref, qf_ref, kf_ref, tf_ref, queries, keys, values, text_keys, text_values):
    rows = query_ref.shape[0]
    queries[...] = query_ref[...] + qf_ref[...]
    each = pl.cdiv(near_refs[0].shape[0], rows) - 1
    text_rows = (near_refs[0].shape[0] - each * rows) // each
    for index, ref in enumerate(near_refs):
        spot = pl.ds(pl.multiple_of(head * rows, rows), rows)
        build_pair(ref[spot, :], kf_ref[rows * index : rows * index + rows, :], rows * index, keys, values)
        spot = pl.ds(pl.multiple_of(each * rows + head * text_rows, 16), text_rows)
        first = text_rows * index
        build_pair(
            ref[spot, :], tf_ref[first : first + text_rows, :], first, text_keys, text_values
        )


def forward_kernel(near, chunk, *refs):
    near_refs, refs = refs[:near], refs[near:]
    query_ref, qf_ref, kf_ref, tf_ref, gate_ref = refs[:5]
    mixed_refs, refs = refs[5 : 5 + SPLIT], refs[5 + SPLIT :]
    outs_ref, stats_ref, queries, keys, values, text_keys, text_values, hold = refs
    build_inputs(
        pl.program_id(0), near_refs, query_ref, qf_ref, kf_ref, tf_ref,
        queries, keys, values, text_keys, text_values,
    )
    rows = queries.shape[0] // SPLIT * FORWARD_SLOTS
    text_chunk = pick_tile(text_keys.shape[0], 256)

    def tile_step(tile, carry):
        spot = pl.ds(pl.multiple_of(tile * rows, rows), rows)
        query = queries[spot, :]

        def attend(key_part, value_part):
            scores = matmul(query, key_part, 1, 1)
            return matmul(jnp.exp(scores).astype(LOW), value_part, 1, 0)

        def step(index, total):
            part = pl.ds(pl.multiple_of(index * chunk, chunk), chunk)
            return total + attend(keys[part, :], values[part, :])

        def text_step(index, total):
            part = pl.ds(pl.multiple_of(index * text_chunk, text_chunk), text_chunk)
            return total + attend(text_keys[part, :], text_values[part, :])

        blank = jnp.zeros((rows, 128), FLOAT)
        own = lax.fori_loop(0, keys.shape[0] // chunk, step, blank)
        cross = lax.fori_loop(0, text_keys.shape[0] // text_chunk, text_step, blank, unroll=True)
        own_inverse = 1.0 / own[:, 0:1]
        cross_inverse = 1.0 / cross[:, 0:1]
        own = own * own_inverse
        cross = cross * cross_inverse
        lanes = lane_ids(own.shape)
        mixed = own + gate_ref[0, 0:1, :] * cross
        each = rows // FORWARD_SLOTS
        for slot in range(FORWARD_SLOTS):
            hold[tile * FORWARD_SLOTS + slot] = fold_high(mixed[each * slot : each * slot + each])
        outs_ref[spot, :] = jnp.where(lanes < 64, turn(cross), own)
        stats_ref[spot, :] = jnp.where(lanes == 0, own_inverse, cross_inverse)
        return carry

    lax.fori_loop(0, SPLIT // FORWARD_SLOTS, tile_step, 0)
    for index, ref in enumerate(mixed_refs):
        ref[...] = hold[index]


def whole(shape):
    return pl.BlockSpec(shape, lambda i: (0,) * len(shape))


def attention_specs(pairs, queries, qf, kf, tf):
    return [whole(value.shape) for value in pairs] + [
        pl.BlockSpec(qf.shape, lambda i: (i, 0)),
        whole(qf.shape),
        whole(kf.shape),
        whole(tf.shape),
        pl.BlockSpec((1, 8, 128), lambda i: (i, 0, 0)),
    ]


def attention_scratch(qf, kf, tf):
    return [
        pltpu.VMEM(qf.shape, LOW),
        pltpu.VMEM(kf.shape, LOW),
        pltpu.VMEM(kf.shape, LOW),
        pltpu.VMEM(tf.shape, LOW),
        pltpu.VMEM(tf.shape, LOW),
    ]


def attention_forward(pairs, queries, qf, kf, tf, gates):
    rows = qf.shape[0]
    heads = gates.shape[0]
    half = rows // SPLIT // 2
    folded = jax.ShapeDtypeStruct((heads * half, 128), LOW)
    wide = jax.ShapeDtypeStruct((heads * rows, 128), FLOAT)
    out = pl.pallas_call(
        functools.partial(forward_kernel, len(pairs), pick_tile(kf.shape[0], 2048)),
        grid=(heads,),
        in_specs=attention_specs(pairs, queries, qf, kf, tf),
        out_specs=[pl.BlockSpec((half, 128), lambda i: (i, 0))] * SPLIT
        + [pl.BlockSpec((rows, 128), lambda i: (i, 0))] * 2,
        out_shape=[folded] * SPLIT + [wide] * 2,
        scratch_shapes=attention_scratch(qf, kf, tf) + [pltpu.VMEM((SPLIT, half, 128), LOW)],
        compiler_params=pltpu.CompilerParams(vmem_limit_bytes=60 * MIB),
        cost_estimate=SMALL,
    )(*pairs, queries, qf, kf, tf, gates)
    return out[:SPLIT], out[SPLIT], out[SPLIT + 1]


def backward_kernel(near, chunk, *refs):
    near_refs, refs = refs[:near], refs[near:]
    query_ref, qf_ref, kf_ref, tf_ref, gate_ref = refs[:5]
    refs = refs[5:]
    grad_refs, refs = refs[:SPLIT], refs[SPLIT:]
    outs_ref, stats_ref, refs = refs[0], refs[1], refs[2:]
    dq_refs, refs = refs[:SPLIT], refs[SPLIT:]
    dkv_refs, dt_refs, dg_ref = refs[:2], refs[2:4], refs[4]
    queries, keys, values, text_keys, text_values, hold, grad_hold, acc, text_acc = refs[5:]
    build_inputs(
        pl.program_id(0), near_refs, query_ref, qf_ref, kf_ref, tf_ref,
        queries, keys, values, text_keys, text_values,
    )
    for index, ref in enumerate(grad_refs):
        grad_hold[index] = ref[...]
    dg_ref[...] = jnp.zeros_like(dg_ref)
    rows = queries.shape[0]
    text_chunk = pick_tile(text_keys.shape[0], 256)
    gate = gate_ref[0, 0:1, :]

    def tile_step(tile, carry):
        spot = pl.ds(pl.multiple_of(tile * rows, rows), rows)
        query = queries[spot, :]
        lanes = lane_ids(query.shape)
        query_low = jnp.where(lanes < 64, query, jnp.zeros_like(query))
        grads = jnp.concatenate([unfold_high(grad_hold[slot]) for slot in range(SPLIT)], axis=0)
        grads = jnp.where(lanes < 64, 0.0, grads)
        outs = outs_ref[spot, :]
        cross_out = jnp.where(lanes < 64, 0.0, turn(outs))
        dg_ref[0] += jnp.sum((grads * cross_out).reshape(rows // 8, 8, 128), axis=0)
        cross_grads = (gate * grads).astype(LOW).astype(FLOAT)

        def widen(grad, out, inverse):
            delta = -jnp.sum(grad * out, axis=1, keepdims=True) * inverse
            first = delta.astype(LOW).astype(FLOAT)
            second = (delta - first).astype(LOW).astype(FLOAT)
            third = delta - first - second
            features = jnp.where(lanes == 0, first, jnp.where(lanes == 1, second, third))
            scaled = grad * inverse
            return jnp.where(lanes < 3, features, scaled).astype(LOW), scaled.astype(LOW)

        stats = stats_ref[spot, :]
        own_wide, own_low = widen(grads, outs, stats[:, 0:1])
        cross_wide, cross_low = widen(cross_grads, cross_out, stats[:, 1:2])
        own_pair = jnp.concatenate([query_low, own_low], axis=0)
        cross_pair = jnp.concatenate([query_low, cross_low], axis=0)

        def attend(key_part, value_part, wide, pair):
            weights = jnp.exp(matmul(key_part, query, 1, 1))
            grad_scores = (weights * matmul(value_part, wide, 1, 1)).astype(LOW)
            low = weights.astype(LOW)
            grad_pair = matmul(jnp.concatenate([grad_scores, low], axis=1), pair, 1, 0)
            return grad_pair, matmul(grad_scores, key_part, 0, 0)

        def step(index, total):
            part = pl.ds(pl.multiple_of(index * chunk, chunk), chunk)
            grad_pair, grad_query = attend(keys[part, :], values[part, :], own_wide, own_pair)
            acc[part, :] = grad_pair
            return total + grad_query

        def text_step(index, total):
            part = pl.ds(pl.multiple_of(index * text_chunk, text_chunk), text_chunk)
            grad_pair, grad_query = attend(
                text_keys[part, :], text_values[part, :], cross_wide, cross_pair
            )
            text_acc[part, :] = grad_pair
            return total + grad_query

        blank = jnp.zeros((rows, 128), FLOAT)
        total = lax.fori_loop(0, keys.shape[0] // chunk, step, blank, unroll=4)
        total = lax.fori_loop(0, text_keys.shape[0] // text_chunk, text_step, total, unroll=True)
        total = total * 0.125
        each = rows // SPLIT
        for slot in range(SPLIT):
            hold[slot] = fold_low(total[each * slot : each * slot + each])
        return carry

    lax.fori_loop(0, 1, tile_step, 0)
    for index, ref in enumerate(dq_refs):
        ref[...] = hold[index]
    for values, refs in ((acc, dkv_refs), (text_acc, dt_refs)):
        size = refs[0].shape[1]
        refs[0][0] = values[:size, :].astype(LOW)
        refs[1][0] = values[size:, :].astype(LOW)


def attention_backward(pairs, queries, qf, kf, tf, gates, grads, outs, stats):
    rows = qf.shape[0]
    heads = gates.shape[0]
    half = rows // SPLIT // 2
    folded = jax.ShapeDtypeStruct((heads * half, 128), LOW)
    piece = jax.ShapeDtypeStruct((heads, kf.shape[0] // 2, 128), LOW)
    text = jax.ShapeDtypeStruct((heads, tf.shape[0] // 2, 128), LOW)
    sums = jax.ShapeDtypeStruct((heads, 8, 128), FLOAT)
    out = pl.pallas_call(
        functools.partial(backward_kernel, len(pairs), pick_tile(kf.shape[0], 1024)),
        grid=(heads,),
        in_specs=attention_specs(pairs, queries, qf, kf, tf)
        + [pl.BlockSpec((half, 128), lambda i: (i, 0))] * SPLIT
        + [pl.BlockSpec((rows, 128), lambda i: (i, 0))] * 2,
        out_specs=[pl.BlockSpec((half, 128), lambda i: (i, 0))] * SPLIT
        + [
            pl.BlockSpec((1,) + value.shape[1:], lambda i: (i, 0, 0))
            for value in (piece, piece, text, text, sums)
        ],
        out_shape=[folded] * SPLIT + [piece, piece, text, text, sums],
        scratch_shapes=attention_scratch(qf, kf, tf)
        + [
            pltpu.VMEM((SPLIT, half, 128), LOW),
            pltpu.VMEM((SPLIT, half, 128), LOW),
            pltpu.VMEM(kf.shape, FLOAT),
            pltpu.VMEM(tf.shape, FLOAT),
        ],
        compiler_params=pltpu.CompilerParams(vmem_limit_bytes=60 * MIB),
        cost_estimate=SMALL,
    )(*pairs, queries, qf, kf, tf, gates, *grads, outs, stats)
    return (out[:SPLIT],) + tuple(out[SPLIT:])


def half_means(values, lanes):
    low = jnp.sum(jnp.where(lanes < 64, values, 0.0), axis=1, keepdims=True)
    high = jnp.sum(jnp.where(lanes < 64, 0.0, values), axis=1, keepdims=True)
    return jnp.where(lanes < 64, low, high) * (1.0 / 64.0)


def swap_halves(values, lanes):
    return jnp.where(
        lax.rem(lanes, 64) < 32, pltpu.roll(values, 96, 1), pltpu.roll(values, 32, 1)
    )


def placed_at(groups, head, upper):
    values = groups[head // 2]
    return values if (head % 2 == 1) == upper else turn(values)


def rope_forward_kernel(heads, far_ref, qkv_ref, cos_ref, sin_ref, gains_ref, *refs):
    outs, hold = refs[:-1], refs[-1]
    width = heads * 64
    each = heads // SPLIT
    rows = qkv_ref.shape[0]
    cosine, sine = cos_ref[...], sin_ref[...]
    lanes = lane_ids(cosine.shape)

    def turned(start, gain):
        groups = []
        for index in range(heads // 2):
            raw = qkv_ref[:, start + 128 * index : start + 128 * index + 128]
            normed = raw * lax.rsqrt(half_means(raw * raw, lanes) + EPS) * gain
            groups.append(normed * cosine + swap_halves(normed, lanes) * sine)
        return groups

    queries = turned(0, gains_ref[0:1, :])
    keys = turned(width, gains_ref[1:2, :])
    values = [
        qkv_ref[:, 2 * width + 128 * index : 2 * width + 128 * index + 128]
        for index in range(heads // 2)
    ]
    for head in range(heads):
        group, index = head // each, head % each
        slot = lax.rem(group - far_ref[0] + SPLIT, SPLIT)
        pair = jnp.where(
            lanes < 64, placed_at(keys, head, False), placed_at(values, head, True)
        )
        hold[slot, index, :rows, :] = pair.astype(LOW)
        hold[slot, index, rows:, :] = fold_low(placed_at(queries, head, False))
    size = rows * 3 // 2
    for slot in range(SPLIT):
        for index in range(each):
            outs[slot][size * index : size * index + size, :] = hold[slot, index]


def small_call(kernel, operands, shapes, scratch):
    out = pl.pallas_call(
        kernel,
        in_specs=[pl.BlockSpec(memory_space=pltpu.SMEM)]
        + [pl.BlockSpec(memory_space=pltpu.VMEM)] * (len(operands) - 1),
        out_specs=[pl.BlockSpec(memory_space=pltpu.VMEM)] * len(shapes),
        out_shape=shapes,
        scratch_shapes=scratch,
        compiler_params=pltpu.CompilerParams(vmem_limit_bytes=32 * MIB),
        cost_estimate=SMALL,
    )(*operands)
    return out


def rope_forward(far, qkv, cosine, sine, gains, heads):
    rows = qkv.shape[0] * 3 // 2
    each = heads // SPLIT
    out = small_call(
        functools.partial(rope_forward_kernel, heads),
        (far, qkv, cosine, sine, gains),
        [jax.ShapeDtypeStruct((each * rows, 128), LOW)] * SPLIT,
        [pltpu.VMEM((SPLIT, each, rows, 128), LOW)],
    )
    return list(out)


def rope_backward_kernel(heads, far_ref, *refs):
    parts, refs = refs[:SPLIT], refs[SPLIT:]
    qkv_ref, cos_ref, sin_ref, gains_ref, out_ref, sums_ref, hold = refs
    width = heads * 64
    each = heads // SPLIT
    rows = qkv_ref.shape[0]
    for slot in range(SPLIT):
        group = lax.rem(far_ref[0] + slot, SPLIT)
        size = hold.shape[2]
        for index in range(each):
            hold[group, index] = parts[slot][size * index : size * index + size, :]
    cosine, sine = cos_ref[...], sin_ref[...]
    lanes = lane_ids(cosine.shape)

    def found(kind, head):
        group, index, upper = head // each, head % each, head % 2 == 1
        if kind == 0:
            packed = hold[group, index, rows:, :]
            return unfold_high(packed) if upper else unfold_low(packed)
        values = hold[group, index, :rows, :].astype(FLOAT)
        return values if upper == (kind == 2) else turn(values)

    def joined(kind, index):
        return jnp.where(lanes < 64, found(kind, 2 * index), found(kind, 2 * index + 1))

    for kind in range(2):
        gain = gains_ref[kind : kind + 1, :]
        total = jnp.zeros((1, 128), FLOAT)
        for index in range(heads // 2):
            spot = kind * width + 128 * index
            raw = qkv_ref[:, spot : spot + 128]
            inverse = lax.rsqrt(half_means(raw * raw, lanes) + EPS)
            unit = raw * inverse
            grad = joined(kind, index)
            back = grad * cosine - swap_halves(grad, lanes) * sine
            total = total + jnp.sum(back * unit, axis=0, keepdims=True)
            scaled = back * gain
            raw_grad = inverse * (scaled - unit * half_means(scaled * unit, lanes))
            out_ref[:, spot : spot + 128] = raw_grad.astype(LOW)
        sums_ref[kind : kind + 1, :] = total
    sums_ref[2:8, :] = jnp.zeros((6, 128), FLOAT)
    for index in range(heads // 2):
        spot = 2 * width + 128 * index
        out_ref[:, spot : spot + 128] = joined(2, index).astype(LOW)


def rope_backward(far, parts, qkv, cosine, sine, gains, heads):
    each = heads // SPLIT
    return small_call(
        functools.partial(rope_backward_kernel, heads),
        (far, *parts, qkv, cosine, sine, gains),
        [jax.ShapeDtypeStruct(qkv.shape, LOW), jax.ShapeDtypeStruct((8, 128), FLOAT)],
        [pltpu.VMEM((SPLIT, each, parts[0].shape[0] // each, 128), LOW)],
    )


def join_kernel(heads, far_ref, *refs):
    parts, out_ref, hold = refs[:SPLIT], refs[SPLIT], refs[SPLIT + 1]
    each = heads // SPLIT
    half = hold.shape[2]
    for slot in range(SPLIT):
        group = lax.rem(far_ref[0] + slot, SPLIT)
        for index in range(each):
            hold[group, index] = parts[slot][half * index : half * index + half, :]
    for pair in range(heads // 2):
        low = unfold_low(hold[2 * pair // each, 2 * pair % each])
        high = unfold_high(hold[(2 * pair + 1) // each, (2 * pair + 1) % each])
        out_ref[:, 128 * pair : 128 * pair + 128] = jnp.where(
            lane_ids(low.shape) < 64, low, high
        ).astype(LOW)


def join_heads(far, parts, heads):
    each = heads // SPLIT
    half = parts[0].shape[0] // each
    return small_call(
        functools.partial(join_kernel, heads),
        (far, *parts),
        [jax.ShapeDtypeStruct((2 * half, heads * 64), LOW)],
        [pltpu.VMEM((SPLIT, each, half, 128), LOW)],
    )[0]


def split_kernel(heads, far_ref, grad_ref, *refs):
    outs, hold = refs[:-1], refs[-1]
    each = heads // SPLIT
    half = hold.shape[2]
    for head in range(heads):
        group, index = head // each, head % each
        slot = lax.rem(group - far_ref[0] + SPLIT, SPLIT)
        values = grad_ref[:, 128 * (head // 2) : 128 * (head // 2) + 128]
        hold[slot, index] = fold_high(values) if head % 2 else fold_low(values)
    for slot in range(SPLIT):
        for index in range(each):
            outs[slot][half * index : half * index + half, :] = hold[slot, index]


def split_heads(far, grads, heads):
    each = heads // SPLIT
    half = grads.shape[0] // 2
    return small_call(
        functools.partial(split_kernel, heads),
        (far, grads),
        [jax.ShapeDtypeStruct((each * half, 128), LOW)] * SPLIT,
        [pltpu.VMEM((SPLIT, each, half, 128), LOW)],
    )


def local_call(kernel, operands, shapes):
    return pl.pallas_call(
        kernel,
        out_shape=shapes,
        compiler_params=pltpu.CompilerParams(vmem_limit_bytes=40 * MIB),
        cost_estimate=SMALL,
    )(*operands)


def gather_kernel(each, *refs):
    slots, text_ref, pairs_ref, queries_ref = refs[:SPLIT], refs[SPLIT], refs[-2], refs[-1]
    size = slots[0].shape[0] // each
    rows = size * 2 // 3
    for head in range(each):
        for index, slot in enumerate(slots):
            spot = (head * SPLIT + index) * rows
            first = head * size
            pairs_ref[spot : spot + rows, :] = slot[first : first + rows, :]
            query = unfold_low(slot[first + rows : first + size, :])
            query = jnp.where(lane_ids(query.shape) < 64, query * 0.125, 0.0)
            queries_ref[spot : spot + rows, :] = query.astype(LOW)
    pairs_ref[each * SPLIT * rows :, :] = text_ref[...]


def gather_slots(slots, text, each):
    rows = slots[0].shape[0] * 2 // 3 * SPLIT
    return local_call(
        functools.partial(gather_kernel, each),
        (*slots, text),
        [
            jax.ShapeDtypeStruct((rows + text.shape[0], 128), LOW),
            jax.ShapeDtypeStruct((rows, 128), LOW),
        ],
    )


def pack_kernel(terms, *refs):
    inputs, folded, outs = refs[:terms], refs[terms : terms + SPLIT], refs[terms + SPLIT :]
    each = inputs[0].shape[0]
    size = outs[0].shape[0] // each
    rows = size * 2 // 3
    half = size - rows
    for head in range(each):
        for slot in range(SPLIT):
            total = sum(
                term[head, rows * slot : rows * slot + rows, :].astype(FLOAT) for term in inputs
            )
            spot = size * head
            outs[slot][spot : spot + rows, :] = total.astype(LOW)
            outs[slot][spot + rows : spot + size, :] = folded[slot][
                half * head : half * head + half, :
            ]


def pack_slots(terms, folded):
    return local_call(
        functools.partial(pack_kernel, len(terms)),
        (*terms, *folded),
        [jax.ShapeDtypeStruct((3 * folded[0].shape[0], 128), LOW)] * SPLIT,
    )


def text_split_kernel(far_ref, text_ref, *outs):
    size = outs[0].shape[1]
    for slot in range(SPLIT):
        group = lax.rem(far_ref[0] + slot, SPLIT)
        spot = pl.ds(pl.multiple_of(group * size, 128), size)
        outs[slot][...] = text_ref[:, spot].astype(LOW)


def text_join_kernel(far_ref, *refs):
    parts, out_ref = refs[:SPLIT], refs[SPLIT]
    size = parts[0].shape[1]
    for slot in range(SPLIT):
        group = lax.rem(far_ref[0] + slot, SPLIT)
        out_ref[:, pl.ds(pl.multiple_of(group * size, 128), size)] = parts[slot][...]


def low_means(values, lanes):
    return jnp.sum(jnp.where(lanes < 64, values, 0.0), axis=1, keepdims=True) * (1.0 / 64.0)


def text_norm_kernel(*refs):
    parts, gain_ref, raw_ref, out_ref = refs[:SPLIT], refs[SPLIT], refs[-2], refs[-1]
    rows = raw_ref.shape[0]
    raw = sum(part[...].astype(FLOAT) for part in parts)
    raw_ref[...] = raw
    for head in range(raw.shape[1] // 128):
        values = raw[:, 128 * head : 128 * head + 128]
        lanes = lane_ids(values.shape)
        normed = values * lax.rsqrt(low_means(values * values, lanes) + EPS) * gain_ref[0:1, :]
        out_ref[rows * head : rows * head + rows, :] = jnp.where(
            lanes < 64, normed, values
        ).astype(LOW)


def text_back_kernel(terms, *refs):
    inputs, refs = refs[:terms], refs[terms:]
    raw_ref, gain_ref, out_ref, sums_ref = refs
    rows = raw_ref.shape[0]
    total_gain = jnp.zeros((1, 128), FLOAT)
    for head in range(inputs[0].shape[0]):
        grad = sum(term[head, :rows, :].astype(FLOAT) for term in inputs)
        grad = grad.astype(LOW).astype(FLOAT)
        raw = raw_ref[:, 128 * head : 128 * head + 128]
        lanes = lane_ids(raw.shape)
        inverse = lax.rsqrt(low_means(raw * raw, lanes) + EPS)
        unit = raw * inverse
        total_gain = total_gain + jnp.sum(grad * unit, axis=0, keepdims=True)
        scaled = grad * gain_ref[0:1, :]
        back = inverse * (scaled - unit * low_means(scaled * unit, lanes))
        out_ref[:, 128 * head : 128 * head + 128] = jnp.where(lanes < 64, back, grad).astype(LOW)
    sums_ref[...] = jnp.broadcast_to(total_gain, sums_ref.shape)


def tie(*values):
    return lax.optimization_barrier(values)


def outer_kernel(bound, *refs):
    first, second, out_ref = refs[:4], refs[4:8], refs[8]
    step = pl.program_id(0)

    def run(group):
        own_left, other_left, own_right, other_right = group
        out_ref[...] = (
            matmul(own_left[...], own_right[0], 1, 0)
            + matmul(other_left[...], other_right[0], 1, 0)
        ).astype(LOW)

    @pl.when(step < bound)
    def _():
        run(first)

    @pl.when(step >= bound)
    def _():
        run(second)


def outer_products(first, second, tile):
    depth = first[0].shape[0]
    steps = [group[2].shape[0] * group[2].shape[2] // tile for group in (first, second)]
    specs, operands = [], []
    for index, group in enumerate((first, second)):
        rows, columns = group[2].shape[1:]
        tiles = columns // tile

        def right_at(i, index=index, tiles=tiles):
            if index == 0:
                at = jnp.minimum(i, steps[0] - 1)
            else:
                at = jnp.maximum(i - steps[0], 0)
            return (at // tiles, 0, at % tiles)

        specs += [whole(group[0].shape)] * 2
        specs += [pl.BlockSpec((1, rows, tile), right_at)] * 2
        operands += group
    return pl.pallas_call(
        functools.partial(outer_kernel, steps[0]),
        grid=(sum(steps),),
        in_specs=specs,
        out_specs=pl.BlockSpec((depth, tile), lambda i: (0, i)),
        out_shape=jax.ShapeDtypeStruct((depth, sum(steps) * tile), LOW),
        compiler_params=pltpu.CompilerParams(vmem_limit_bytes=48 * MIB),
        cost_estimate=SMALL,
    )(*operands)


def columns_kernel(core_ref, values_ref, own_ref, other_ref, hold):
    turned = jnp.transpose(values_ref[...].astype(FLOAT))
    hold[...] = turned.reshape(hold.shape)
    pairs = hold.shape[0] // 2
    core = core_ref[0]
    own_ref[...] = jnp.concatenate(
        [hold[2 * pair + core] for pair in range(pairs)], axis=0
    ).astype(LOW)
    other_ref[...] = jnp.concatenate(
        [hold[2 * pair + 1 - core] for pair in range(pairs)], axis=0
    ).astype(LOW)


def split_columns(core, values, block):
    rows, width = values.shape
    half = jax.ShapeDtypeStruct((width // 2, rows), LOW)
    return small_call(
        columns_kernel,
        (core, values),
        [half, half],
        [pltpu.VMEM((width // block, block, rows), FLOAT)],
    )


def feed_kernel(
    normed_ref, grad_ref, gate_ref, up_ref, down_ref,
    hidden_ref, grads_ref, feed_own_ref, feed_other_ref, norm_own_ref, norm_other_ref,
    feed_acc, norm_acc,
):
    step = pl.program_id(0)

    @pl.when(step == 0)
    def _():
        feed_acc[...] = jnp.zeros_like(feed_acc)
        norm_acc[...] = jnp.zeros_like(norm_acc)

    normed = normed_ref[...]
    gate = matmul(normed, gate_ref[...], 1, 0)
    up = matmul(normed, up_ref[...], 1, 0)
    grad_hidden = matmul(grad_ref[...], down_ref[...], 1, 0)
    sigmoid = 1.0 / (1.0 + jnp.exp(-gate))
    silu = gate * sigmoid
    hidden = (silu * up).astype(LOW)
    grad_gate = (grad_hidden * up * sigmoid * (1.0 + gate * (1.0 - sigmoid))).astype(LOW)
    grad_up = (grad_hidden * silu).astype(LOW)
    hidden_ref[0] = hidden
    grads_ref[0] = grad_gate
    grads_ref[1] = grad_up
    feed_acc[...] += matmul(hidden, down_ref[...], 1, 1)
    norm_acc[...] += matmul(grad_gate, gate_ref[...], 1, 1) + matmul(grad_up, up_ref[...], 1, 1)

    @pl.when(step == pl.num_programs(0) - 1)
    def _():
        half = feed_own_ref.shape[0]
        feed_own_ref[...] = feed_acc[:half, :]
        feed_other_ref[...] = feed_acc[half:, :].astype(LOW)
        norm_own_ref[...] = norm_acc[:half, :]
        norm_other_ref[...] = norm_acc[half:, :].astype(LOW)


def feed_forward(normed, grads, weights, columns, tile):
    rows, width = normed.shape
    tiles = columns // tile
    own = jax.ShapeDtypeStruct((rows // 2, width), FLOAT)
    other = jax.ShapeDtypeStruct((rows // 2, width), LOW)
    return pl.pallas_call(
        feed_kernel,
        grid=(tiles,),
        in_specs=[whole(normed.shape), whole(grads.shape)]
        + [
            pl.BlockSpec((width, tile), lambda i, part=part: (0, part * tiles + i))
            for part in range(3)
        ],
        out_specs=[
            pl.BlockSpec((1, rows, tile), lambda i: (0, 0, i)),
            pl.BlockSpec((2, rows, tile), lambda i: (0, 0, i)),
        ]
        + [whole(own.shape)] * 4,
        out_shape=[
            jax.ShapeDtypeStruct((1, rows, columns), LOW),
            jax.ShapeDtypeStruct((2, rows, columns), LOW),
            own,
            other,
            own,
            other,
        ],
        scratch_shapes=[pltpu.VMEM((rows, width), FLOAT)] * 2,
        compiler_params=pltpu.CompilerParams(vmem_limit_bytes=48 * MIB),
        cost_estimate=SMALL,
    )(normed, grads, weights, weights, weights)


def dot_float(left, right):
    return jnp.dot(left, right, preferred_element_type=FLOAT)


def dot_turned(left, right):
    return matmul(left, right, 1, 1)


def norm_rows(values, gains):
    return values * lax.rsqrt(jnp.mean(values * values, axis=-1, keepdims=True) + EPS) * gains


def modulated(values, gains, shifts, scales):
    return norm_rows(values, gains) * (1.0 + scales) + shifts


def swapped(values):
    return lax.ppermute(values, "tensor", [(0, 1), (1, 0)])


def both_rows(values):
    return jnp.concatenate([values, swapped(values)], axis=0)


def own_rows(partial):
    rows = partial.shape[0] // 2
    return partial[:rows] + swapped(partial[rows:].astype(LOW)).astype(FLOAT)


def shards(
    inputs,
    clip_ids,
    positions,
    text_tokens,
    conditioning,
    ada_weight,
    ada_bias,
    first_norm_gain,
    query_gain,
    key_gain,
    text_key_gain,
    head_gate,
    qkv_weight,
    out_weight,
    text_kv_weight,
    second_norm_gain,
    gate_up_weight,
    down_weight,
    grad_output,
):
    dp = lax.axis_size("dp")
    near = dp // SPLIT
    bits = [near >> (step + 1) for step in range(near.bit_length() - 1)]
    tensor_index = lax.axis_index("tensor")
    dp_index = lax.axis_index("dp")
    far_index, near_index = dp_index // near, dp_index % near
    row_count, width = inputs.shape
    token_count = clip_ids.shape[0]
    head_size = query_gain.shape[0]
    local_width = qkv_weight.shape[2]
    heads = local_width // head_size
    each = heads // SPLIT
    part_width = each * head_size
    clip_count = conditioning.shape[0]
    hidden_count = gate_up_weight.shape[2]
    weight_rows = qkv_weight.shape[1]

    def flip(values, bit):
        return lax.ppermute(values, "dp", [(j, j ^ bit) for j in range(dp)])

    def shift(values, steps):
        pairs = [(j, ((j // near + steps) % SPLIT) * near + j % near) for j in range(dp)]
        return lax.ppermute(values, "dp", pairs)

    def sum_dp(values):
        step = 1
        while step < dp:
            values = values + flip(values, step)
            step *= 2
        return values

    def spread(values):
        for bit in bits:
            values = jnp.concatenate([values, flip(values, bit)], axis=0)
        return values

    def spread_list(values):
        values = [values]
        for bit in bits:
            values = values + [flip(value, bit) for value in values]
        return values

    def collect(values):
        for bit in reversed(bits):
            half = values.shape[0] // 2
            values = values[:half].astype(FLOAT) + flip(
                values[half:].astype(LOW), bit
            ).astype(FLOAT)
        return values

    def pick(stacked, index):
        return lax.dynamic_index_in_dim(stacked, index, 0, keepdims=False)

    def send_parts(stacked):
        out = [pick(stacked, far_index)]
        for steps in range(1, SPLIT):
            out.append(shift(pick(stacked, (far_index + steps) % SPLIT), steps))
        return out

    def send_slots(slots):
        return [slots[0]] + [shift(slots[steps], steps) for steps in range(1, SPLIT)]

    def return_slots(slots):
        return [slots[0]] + [shift(slots[steps], -steps) for steps in range(1, SPLIT)]

    flips = []
    for order in range(near):
        mask = 0
        for place, bit in enumerate(bits):
            if order >> place & 1:
                mask |= bit
        flips.append(mask)

    core = dp_index % 2
    core_groups = [list(range(first, dp, 2)) for first in range(2)]

    core_at = core.astype(jnp.int32).reshape(1)

    def core_columns(values):
        own, other = split_columns(core_at, values, weight_rows)
        return own, flip(other, 1)

    def scatter(values):
        return lax.psum_scatter(
            values, "dp", scatter_dimension=0, axis_index_groups=core_groups, tiled=True
        )

    qkv_full = lax.all_gather(
        qkv_weight.transpose(1, 0, 2).reshape(weight_rows, 3 * local_width),
        "dp",
        axis=0,
        tiled=True,
    )
    cond_float = conditioning.astype(FLOAT)
    silu_cond = jax.nn.silu(cond_float).astype(LOW)
    cond_rows = ada_weight.shape[0]
    silu_slice = lax.dynamic_slice_in_dim(silu_cond, dp_index * cond_rows, cond_rows, axis=1)
    first_rows = jnp.sum((clip_ids == 0).astype(FLOAT))
    spots = jnp.arange(ada_weight.shape[1], dtype=jnp.int32)
    early = 2 * width
    early_part = jnp.concatenate(
        [
            dot_float(silu_slice, ada_weight[:, :early]),
            jnp.where(spots[:early] == dp_index, first_rows, 0.0)[None],
        ],
        axis=0,
    )
    text_columns = lax.all_to_all(text_tokens, "dp", split_axis=1, concat_axis=0, tiled=True)
    early_part, text_columns = tie(early_part, text_columns)
    early_sum = sum_dp(early_part)
    bias = ada_bias.astype(FLOAT)
    early_mod = early_sum[:clip_count] + bias[:early]
    counts = early_sum[clip_count, :dp].astype(jnp.int32)

    own_ids = lax.dynamic_slice_in_dim(clip_ids, tensor_index * row_count, row_count)
    row_positions = jnp.where(
        tensor_index == 0, positions, jnp.roll(positions, row_count)
    )
    other_clip = jnp.max(clip_ids)
    first_clip = (own_ids == 0)[:, None]

    def mod_blocks(modulation):
        rows = jnp.where(
            first_clip,
            modulation[0:1],
            lax.dynamic_slice_in_dim(modulation, other_clip, 1, 0),
        )
        return jnp.split(rows, rows.shape[1] // width, axis=1)

    shift_one, scale_one = mod_blocks(early_mod)
    input_rows = inputs.astype(FLOAT)
    first_gain = first_norm_gain.astype(FLOAT)
    normed_one = modulated(input_rows, first_gain, shift_one, scale_one).astype(LOW)
    normed_all = both_rows(normed_one)
    late_sum = sum_dp(dot_float(silu_slice, ada_weight[:, early:]))

    half_size = head_size // 2
    frequency = 10000.0 ** (-(jnp.arange(half_size, dtype=FLOAT) * 2.0 / head_size))
    angles = row_positions.astype(FLOAT)[:, None] * frequency[None, :]
    cosine = jnp.cos(angles)
    sine = jnp.sin(angles)
    cosine = jnp.concatenate([cosine] * 4, axis=1)
    sine = jnp.concatenate([-sine, sine, -sine, sine], axis=1)
    gains = jnp.stack([jnp.tile(query_gain, 2), jnp.tile(key_gain, 2)]).astype(FLOAT)
    gains = jnp.concatenate([gains, jnp.zeros((6, 128), FLOAT)], axis=0)

    text_rows = text_tokens.shape[0]
    group_rows = text_rows * SPLIT
    text_groups = text_columns.reshape(near, group_rows, text_columns.shape[1])
    text_near = jnp.concatenate([pick(text_groups, near_index ^ mask) for mask in flips], axis=0)
    text_weight = (
        text_kv_weight.reshape(2, -1, SPLIT, each, head_size)
        .transpose(1, 2, 3, 0, 4)
        .reshape(-1, 2 * local_width)
    )
    far = far_index.astype(jnp.int32).reshape(1)
    text_sum = collect(dot_float(text_near, text_weight))
    part_shape = jax.ShapeDtypeStruct((group_rows, 2 * part_width), LOW)
    text_parts = small_call(text_split_kernel, (far, text_sum), [part_shape] * SPLIT, [])
    ky_gain = jnp.concatenate([text_key_gain.astype(FLOAT), jnp.zeros((128 - head_size,), FLOAT)])
    ky_gain = jnp.broadcast_to(ky_gain[None], (8, 128))

    lanes = jnp.arange(128, dtype=jnp.int32)[None, :]
    text_groups_at = jnp.stack([near_index ^ mask for mask in flips])
    text_clip = (
        text_groups_at[:, None] * group_rows + jnp.arange(group_rows, dtype=jnp.int32)[None, :]
    ).reshape(-1) // TXT
    text_features = (lanes == 64 + text_clip[:, None]).astype(LOW)
    block_at = jnp.stack(
        [
            ((far_index - steps) % SPLIT) * near + (near_index ^ mask)
            for mask in flips
            for steps in range(SPLIT)
        ]
    )
    block_count = jnp.sum(
        jnp.where(block_at[:, None] == jnp.arange(dp, dtype=jnp.int32)[None, :], counts[None, :], 0),
        axis=1,
    )
    row_at = (jnp.arange(token_count, dtype=jnp.int32) + tensor_index * row_count) % token_count
    key_clip = jnp.where(
        row_at[None, :] < block_count[:, None], 0, 1 + block_at[:, None] // GROUP
    ).reshape(-1)
    key_features = (lanes == 64 + key_clip[:, None]).astype(LOW)
    group_tokens = SPLIT * token_count
    query_clip = key_clip[:group_tokens, None]
    query_features = jnp.where(
        (lanes >= 64) & (lanes < 64 + clip_count) & (lanes != 64 + query_clip), MASK, 0.0
    ).astype(LOW)
    gate_heads = jnp.tanh(
        lax.dynamic_slice_in_dim(
            head_gate.astype(FLOAT), tensor_index * heads + far_index * each, each
        )
    )
    gate_lanes = jnp.broadcast_to(gate_heads[:, None, None], (each, 8, 128))

    rest_weights, qkv_full, normed_all, text_parts, late_sum, key_features, query_features = tie(
        jnp.concatenate(
            [gate_up_weight[0], gate_up_weight[1], down_weight.T, out_weight.T], axis=1
        ),
        qkv_full,
        normed_all,
        text_parts,
        late_sum,
        key_features,
        query_features,
    )
    rest_full = lax.all_gather(rest_weights, "dp", axis=0, tiled=True)
    out_full = rest_full[:, 3 * hidden_count :]
    text_arrived = send_slots(text_parts)
    qkv_raw = dot_float(normed_all, qkv_full)
    head_slots = rope_forward(far, qkv_raw, cosine, sine, gains, heads)
    gate_one, shift_two, scale_two, gate_two = mod_blocks(late_sum + bias[early:])
    grad_two = grad_output.astype(FLOAT)
    grad_ffn = both_rows((gate_two * grad_two).astype(LOW))
    head_slots, text_arrived = tie(head_slots, text_arrived)
    text_raw, text_pairs = local_call(
        text_norm_kernel,
        (*text_arrived, ky_gain),
        [
            jax.ShapeDtypeStruct((group_rows, 2 * part_width), FLOAT),
            jax.ShapeDtypeStruct((each * group_rows, 128), LOW),
        ],
    )
    arrived = send_slots(head_slots)
    arrived, grad_ffn = tie(arrived, grad_ffn)
    own_pairs, queries = gather_slots(arrived, text_pairs, each)
    pairs = spread_list(own_pairs)
    mixed_slots, head_outs, head_stats = attention_forward(
        pairs, queries, query_features, key_features, text_features, gate_lanes
    )
    mixed = join_heads(far, return_slots(mixed_slots), heads)
    attn_rows = own_rows(dot_turned(mixed, out_full))
    after_attn = input_rows + gate_one * attn_rows
    second_gain = second_norm_gain.astype(FLOAT)
    normed_two_all = both_rows(modulated(after_attn, second_gain, shift_two, scale_two).astype(LOW))
    hidden_low, feed_grads, feed_own, feed_other, norm_own, norm_other = feed_forward(
        normed_two_all, grad_ffn, rest_full, hidden_count, 512
    )
    feed_weights_grad = outer_products(
        [*core_columns(normed_two_all), feed_grads, flip(feed_grads, 1)],
        [*core_columns(grad_ffn), hidden_low, flip(hidden_low, 1)],
        512,
    )
    norm_other = swapped(norm_other)
    grad_normed_two = norm_own + norm_other.astype(FLOAT)
    _, pull_two = jax.vjp(modulated, after_attn, second_gain, shift_two, scale_two)
    back_two, grad_second_gain, grad_shift_two, grad_scale_two = pull_two(grad_normed_two)
    grad_after = grad_two + back_two
    grad_attn, feed_other = tie(both_rows((gate_one * grad_after).astype(LOW)), feed_other)
    ffn_rows = feed_own + swapped(feed_other).astype(FLOAT)
    output = (after_attn + gate_two * ffn_rows).astype(LOW)
    grad_gate_two = grad_two * ffn_rows
    grad_gate_one = grad_after * attn_rows
    grad_slots = send_slots(split_heads(far, dot_float(grad_attn, out_full), heads))
    normed_core = core_columns(normed_all)
    last_left = [normed_core, core_columns(grad_attn)]
    mixed_right = mixed[None]
    mixed_other = flip(mixed_right, 1)
    grad_slots, feed_weights_grad, last_left, mixed_other = tie(
        grad_slots, feed_weights_grad, last_left, mixed_other
    )
    feed_low = scatter(feed_weights_grad)

    def total_rows(terms, first, last):
        return sum(term[:, first:last].astype(FLOAT) for term in terms).astype(LOW)

    def start_sums(keep, send, text_keep, text_send):
        return (
            [keep, flip(send, bits[-1])],
            [text_keep, flip(text_send, bits[-1])],
        )

    def next_send(state):
        terms, text_terms = state
        size, text_size = terms[-1].shape[1], text_terms[-1].shape[1]
        return jnp.concatenate(
            [
                total_rows(terms, size // 2, size),
                total_rows(text_terms, text_size // 2, text_size),
            ],
            axis=1,
        )

    def next_state(state, sent, bit):
        terms, text_terms = state
        size = terms[-1].shape[1] // 2
        other = flip(sent, bit)
        return terms + [other[:, :size]], text_terms + [other[:, size:]]

    folded, *pieces, gate_parts = attention_backward(
        pairs,
        queries,
        query_features,
        key_features,
        text_features,
        gate_lanes,
        grad_slots,
        head_outs,
        head_stats,
    )
    state = start_sums(*pieces)
    for bit in reversed(bits[:-1]):
        state = next_state(state, next_send(state), bit)
    pair_terms, text_terms = state
    back_slots = pack_slots(pair_terms, folded)
    clip_at = jnp.arange(clip_count, dtype=jnp.int32)[:, None]

    def clip_sums(values):
        first_sum = jnp.sum(jnp.where(first_clip, values, 0.0), axis=0)[None]
        other_sum = jnp.sum(jnp.where(first_clip, 0.0, values), axis=0)[None]
        return jnp.where(clip_at == 0, first_sum, jnp.where(clip_at == other_clip, other_sum, 0.0))

    def pair_sums(blocks, gains_row):
        wide = jnp.concatenate([clip_sums(values) for values in blocks], axis=1)
        gains_row = jnp.concatenate(
            [gains_row, jnp.zeros((wide.shape[1] - gains_row.shape[0],), FLOAT)]
        )
        wide = jnp.concatenate([wide, gains_row[None]], axis=0)
        return wide + swapped(wide)

    back_parts = return_slots(back_slots)
    text_low, ky_sums = local_call(
        functools.partial(text_back_kernel, len(text_terms)),
        (*text_terms, text_raw, ky_gain),
        [part_shape, jax.ShapeDtypeStruct((8, 128), FLOAT)],
    )
    qkv_grad, gain_sums = rope_backward(far, back_parts, qkv_raw, cosine, sine, gains, heads)
    normed_part = dot_turned(qkv_grad, qkv_full)
    qkv_right = qkv_grad[None]
    last_grads = outer_products(
        [*last_left[0], qkv_right, flip(qkv_right, 1)],
        [*last_left[1], mixed_right, mixed_other],
        local_width,
    )
    last_grads, feed_low = tie(last_grads, feed_low)
    last_low = scatter(last_grads)
    normed_part, last_grads, text_low = tie(normed_part, last_grads, text_low)
    grad_normed_one = own_rows(normed_part)
    _, pull_one = jax.vjp(modulated, input_rows, first_gain, shift_one, scale_one)
    back_one, grad_first_gain, grad_shift_one, grad_scale_one = pull_one(grad_normed_one)
    grad_inputs = grad_after + back_one
    head_sums = (1.0 - gate_heads * gate_heads) * jnp.sum(gate_parts, axis=(1, 2))
    head_row = lax.dynamic_update_slice_in_dim(
        jnp.zeros((head_gate.shape[0],), FLOAT),
        head_sums,
        tensor_index * heads + far_index * each,
        0,
    )
    gain_halves = gain_sums[:2, :head_size] + gain_sums[:2, head_size:]
    all_pairs = pair_sums(
        (
            grad_shift_one,
            grad_scale_one,
            grad_gate_one,
            grad_shift_two,
            grad_scale_two,
            grad_gate_two,
        ),
        jnp.concatenate(
            [
                grad_first_gain,
                grad_second_gain,
                gain_halves.reshape(-1),
                ky_sums[0, :head_size],
                head_row,
            ]
        ),
    )
    text_wide = small_call(
        text_join_kernel,
        (far, *return_slots([text_low] * SPLIT)),
        [jax.ShapeDtypeStruct((group_rows, 2 * local_width), LOW)],
        [],
    )[0]
    text_all = spread(text_wide)
    all_pairs, text_all = tie(all_pairs, text_all)
    grad_sums = sum_dp(all_pairs)
    grad_mod_low, sums = grad_sums[:clip_count].astype(LOW), grad_sums[clip_count]
    first_gain_sum = sums[:width]
    second_gain_sum = sums[width : 2 * width]
    at = 2 * width
    q_gain_sum = sums[at : at + head_size]
    k_gain_sum = sums[at + head_size : at + 2 * head_size]
    ky_gain_sum = sums[at + 2 * head_size : at + 3 * head_size]
    gate_sum = sums[at + 3 * head_size : at + 3 * head_size + head_gate.shape[0]]
    grad_text_kv = (
        matmul(text_near, text_all, 0, 0)
        .reshape(-1, SPLIT, each, 2, head_size)
        .transpose(3, 0, 1, 2, 4)
        .reshape(2, -1, local_width)
    )
    grad_text_part = dot_turned(text_all, text_weight).astype(LOW)
    grad_text_pair = grad_text_part.astype(FLOAT) + swapped(grad_text_part).astype(FLOAT)
    grad_text_groups = grad_text_pair.astype(LOW).reshape(near, group_rows, -1)
    orders = jnp.arange(near, dtype=jnp.int32)
    flip_at = jnp.array(flips, jnp.int32)
    grad_text_rows = jnp.concatenate(
        [
            pick(grad_text_groups, jnp.sum(jnp.where(flip_at == near_index ^ group, orders, 0)))
            for group in range(near)
        ],
        axis=0,
    )
    grad_text_all = lax.all_to_all(grad_text_rows, "dp", split_axis=0, concat_axis=1, tiled=True)
    half_text = text_tokens.shape[1] // 2
    grad_text = lax.dynamic_slice_in_dim(
        grad_text_all, tensor_index * half_text, half_text, 1
    ).astype(FLOAT)
    grad_ada_bias = jnp.sum(grad_mod_low.astype(FLOAT), axis=0)
    grad_ada = matmul(silu_slice, grad_mod_low, 0, 0)
    cond_part = lax.dynamic_update_slice_in_dim(
        jnp.zeros(cond_float.shape, FLOAT),
        dot_turned(grad_mod_low, ada_weight),
        dp_index * cond_rows,
        1,
    )
    cond_sigmoid = jax.nn.sigmoid(cond_float)
    grad_conditioning = (
        sum_dp(cond_part) * cond_sigmoid * (1.0 + cond_float * (1.0 - cond_sigmoid))
    )
    last_shard = last_low.astype(FLOAT)
    qkv_shard = last_shard[:, : 3 * local_width].reshape(weight_rows, 3, local_width).transpose(1, 0, 2)
    feed_shard = feed_low.astype(FLOAT)
    gate_up_shard = jnp.stack(
        [feed_shard[:, :hidden_count], feed_shard[:, hidden_count : 2 * hidden_count]]
    )
    out_shard = last_shard[:, 3 * local_width :]
    down_shard = feed_shard[:, 2 * hidden_count : 3 * hidden_count]
    return (
        output,
        grad_inputs,
        grad_text,
        grad_conditioning,
        grad_ada,
        grad_ada_bias,
        first_gain_sum,
        q_gain_sum,
        k_gain_sum,
        ky_gain_sum,
        gate_sum,
        qkv_shard,
        out_shard.T,
        grad_text_kv,
        second_gain_sum,
        gate_up_shard,
        down_shard.T,
    )


def solution(mesh):
    placed = (
        P(("dp", "tensor"), None),
        P("dp"),
        P("dp"),
        P("dp", None),
        P(),
        P("dp", None),
        P(),
        P(),
        P(),
        P(),
        P(),
        P(),
        P(None, "dp", "tensor"),
        P("tensor", "dp"),
        P(None, "dp", "tensor"),
        P(),
        P(None, "dp", "tensor"),
        P("tensor", "dp"),
        P(("dp", "tensor"), None),
    )
    return jax.shard_map(
        shards,
        mesh=mesh,
        in_specs=placed,
        out_specs=(
            P(("dp", "tensor"), None),
            P(("dp", "tensor"), None),
            P("dp", "tensor"),
            P(),
            P("dp", None),
            P(),
            P(),
            P(),
            P(),
            P(),
            P(),
            P(None, "dp", "tensor"),
            P("tensor", "dp"),
            P(None, "dp", "tensor"),
            P(),
            P(None, "dp", "tensor"),
            P("tensor", "dp"),
        ),
        check_vma=False,
    )
```

```python
import functools

import jax
import jax.numpy as jnp
from jax import lax
from jax.experimental import pallas as pl
from jax.experimental.pallas import tpu as pltpu
from jax.sharding import PartitionSpec as P

TXT = 256
GROUP = 8
SPLIT = 4
EPS = 1e-06
MASK = -1e4
FORWARD_SLOTS = 4
LOW = jnp.bfloat16
FLOAT = jnp.float32
MIB = 1024 * 1024
LARGE = pl.CostEstimate(flops=25 * 10**9, bytes_accessed=1024, transcendentals=0)
SMALL = pl.CostEstimate(flops=1024, bytes_accessed=1024, transcendentals=0)


def pick_tile(total, most):
    size = most
    while total % size:
        size //= 2
    return size


def matmul(left, right, left_dim, right_dim):
    return lax.dot_general(
        left, right, (((left_dim,), (right_dim,)), ((), ())), preferred_element_type=jnp.float32
    )


def lane_ids(shape):
    return lax.broadcasted_iota(jnp.int32, shape, len(shape) - 1)


def turn(values):
    return pltpu.roll(values, 64, 1)


def fold_low(values):
    half = values.shape[0] // 2
    top, bottom = values[:half], turn(values)[half:]
    return jnp.where(lane_ids(top.shape) < 64, top, bottom).astype(LOW)


def fold_high(values):
    half = values.shape[0] // 2
    top, bottom = turn(values)[:half], values[half:]
    return jnp.where(lane_ids(top.shape) < 64, top, bottom).astype(LOW)


def unfold_low(packed):
    wide = packed.astype(FLOAT)
    return jnp.concatenate([wide, turn(wide)], axis=0)


def unfold_high(packed):
    wide = packed.astype(FLOAT)
    return jnp.concatenate([turn(wide), wide], axis=0)


def build_pair(pair, features, spot, keys, values):
    lanes = lane_ids(pair.shape)
    rows = pl.ds(spot, pair.shape[0])
    keys[rows, :] = jnp.where(lanes < 64, pair, features)
    values[rows, :] = jnp.where(
        lanes < 64, jnp.where(lanes < 3, 1.0, 0.0).astype(LOW), pair
    )


def build_inputs(head, near_refs, query_ref, qf_ref, kf_ref, tf_ref, queries, keys, values, text_keys, text_values):
    rows = query_ref.shape[0]
    queries[...] = query_ref[...] + qf_ref[...]
    each = pl.cdiv(near_refs[0].shape[0], rows) - 1
    text_rows = (near_refs[0].shape[0] - each * rows) // each
    for index, ref in enumerate(near_refs):
        spot = pl.ds(pl.multiple_of(head * rows, rows), rows)
        build_pair(ref[spot, :], kf_ref[rows * index : rows * index + rows, :], rows * index, keys, values)
        spot = pl.ds(pl.multiple_of(each * rows + head * text_rows, 16), text_rows)
        first = text_rows * index
        build_pair(
            ref[spot, :], tf_ref[first : first + text_rows, :], first, text_keys, text_values
        )


def forward_kernel(near, chunk, last, *refs):
    near_refs, refs = refs[:near], refs[near:]
    query_ref, qf_ref, kf_ref, tf_ref, gate_ref = refs[:5]
    refs = refs[5:]
    if last:
        before_refs, mixed_refs, refs = refs[:2], refs[2 : 2 + SPLIT], refs[2 + SPLIT :]
    outs_ref, stats_ref, queries, keys, values, text_keys, text_values, hold = refs
    build_inputs(
        pl.program_id(0), near_refs, query_ref, qf_ref, kf_ref, tf_ref,
        queries, keys, values, text_keys, text_values,
    )
    rows = queries.shape[0] // SPLIT * FORWARD_SLOTS
    text_chunk = pick_tile(text_keys.shape[0], 384)

    def tile_step(tile, carry):
        spot = pl.ds(pl.multiple_of(tile * rows, rows), rows)
        query = queries[spot, :]

        def attend(key_part, value_part):
            scores = matmul(query, key_part, 1, 1)
            return matmul(jnp.exp(scores).astype(LOW), value_part, 1, 0)

        def step(index, total):
            part = pl.ds(pl.multiple_of(index * chunk, chunk), chunk)
            return total + attend(keys[part, :], values[part, :])

        def text_step(index, total):
            part = pl.ds(pl.multiple_of(index * text_chunk, text_chunk), text_chunk)
            return total + attend(text_keys[part, :], text_values[part, :])

        blank = jnp.zeros((rows, 128), FLOAT)
        own = lax.fori_loop(0, keys.shape[0] // chunk, step, blank)
        cross = lax.fori_loop(0, text_keys.shape[0] // text_chunk, text_step, blank, unroll=True)
        if not last:
            outs_ref[spot, :] = own
            stats_ref[spot, :] = cross
            return carry
        own = own + before_refs[0][spot, :]
        cross = cross + before_refs[1][spot, :]
        own_inverse = 1.0 / own[:, 0:1]
        cross_inverse = 1.0 / cross[:, 0:1]
        own = own * own_inverse
        cross = cross * cross_inverse
        lanes = lane_ids(own.shape)
        mixed = own + gate_ref[0, 0:1, :] * cross
        each = rows // FORWARD_SLOTS
        for slot in range(FORWARD_SLOTS):
            hold[tile * FORWARD_SLOTS + slot] = fold_high(mixed[each * slot : each * slot + each])
        outs_ref[spot, :] = jnp.where(lanes < 64, turn(cross), own)
        stats_ref[spot, :] = jnp.where(lanes == 0, own_inverse, cross_inverse)
        return carry

    lax.fori_loop(0, SPLIT // FORWARD_SLOTS, tile_step, 0)
    if last:
        for index, ref in enumerate(mixed_refs):
            ref[...] = hold[index]


def whole(shape):
    return pl.BlockSpec(shape, lambda i: (0,) * len(shape))


def attention_specs(part, pairs, queries, qf, kf, tf):
    return [whole(value.shape) for value in pairs] + [
        pl.BlockSpec(qf.shape, lambda i: (i, 0)),
        whole(qf.shape),
        pl.BlockSpec((kf.shape[0] // 2, 128), lambda i: (part, 0)),
        pl.BlockSpec((tf.shape[0] // 2, 128), lambda i: (part, 0)),
        pl.BlockSpec((1, 8, 128), lambda i: (i, 0, 0)),
    ]


def attention_scratch(qf, kf, tf):
    keys, text_keys = (kf.shape[0] // 2, 128), (tf.shape[0] // 2, 128)
    return [
        pltpu.VMEM(qf.shape, LOW),
        pltpu.VMEM(keys, LOW),
        pltpu.VMEM(keys, LOW),
        pltpu.VMEM(text_keys, LOW),
        pltpu.VMEM(text_keys, LOW),
    ]


def attention_forward(pairs, queries, qf, kf, tf, gates, before):
    rows = qf.shape[0]
    heads = gates.shape[0]
    half = rows // SPLIT // 2
    folded = jax.ShapeDtypeStruct((heads * half, 128), LOW)
    wide = jax.ShapeDtypeStruct((heads * rows, 128), FLOAT)
    wide_spec = pl.BlockSpec((rows, 128), lambda i: (i, 0))
    last = len(before) > 0
    slots = SPLIT if last else 0
    out = pl.pallas_call(
        functools.partial(forward_kernel, len(pairs), pick_tile(kf.shape[0] // 2, 2048), last),
        grid=(heads,),
        in_specs=attention_specs(int(last), pairs, queries, qf, kf, tf) + [wide_spec] * len(before),
        out_specs=[pl.BlockSpec((half, 128), lambda i: (i, 0))] * slots + [wide_spec] * 2,
        out_shape=[folded] * slots + [wide] * 2,
        scratch_shapes=attention_scratch(qf, kf, tf) + [pltpu.VMEM((SPLIT, half, 128), LOW)],
        compiler_params=pltpu.CompilerParams(vmem_limit_bytes=60 * MIB),
        cost_estimate=LARGE,
    )(*pairs, queries, qf, kf, tf, gates, *before)
    return (out[:slots], out[slots], out[slots + 1]) if last else tuple(out)


def backward_kernel(near, chunk, last, *refs):
    near_refs, refs = refs[:near], refs[near:]
    query_ref, qf_ref, kf_ref, tf_ref, gate_ref = refs[:5]
    refs = refs[5:]
    grad_refs, refs = refs[:SPLIT], refs[SPLIT:]
    outs_ref, stats_ref, refs = refs[0], refs[1], refs[2:]
    if last:
        before_ref, dq_refs, dg_ref, refs = refs[0], refs[1 : 1 + SPLIT], refs[1 + SPLIT], refs[2 + SPLIT :]
    else:
        dq_ref, refs = refs[0], refs[1:]
    dkv_refs, dt_refs = refs[:2], refs[2:4]
    queries, keys, values, text_keys, text_values, hold, grad_hold, acc, text_acc = refs[4:]
    build_inputs(
        pl.program_id(0), near_refs, query_ref, qf_ref, kf_ref, tf_ref,
        queries, keys, values, text_keys, text_values,
    )
    for index, ref in enumerate(grad_refs):
        grad_hold[index] = ref[...]
    if last:
        dg_ref[...] = jnp.zeros_like(dg_ref)
    rows = queries.shape[0]
    text_chunk = pick_tile(text_keys.shape[0], 384)
    gate = gate_ref[0, 0:1, :]

    def tile_step(tile, carry):
        spot = pl.ds(pl.multiple_of(tile * rows, rows), rows)
        query = queries[spot, :]
        lanes = lane_ids(query.shape)
        query_low = jnp.where(lanes < 64, query, jnp.zeros_like(query))
        grads = jnp.concatenate([unfold_high(grad_hold[slot]) for slot in range(SPLIT)], axis=0)
        grads = jnp.where(lanes < 64, 0.0, grads)
        outs = outs_ref[spot, :]
        cross_out = jnp.where(lanes < 64, 0.0, turn(outs))
        if last:
            dg_ref[0] += jnp.sum((grads * cross_out).reshape(rows // 8, 8, 128), axis=0)
        cross_grads = (gate * grads).astype(LOW).astype(FLOAT)

        def widen(grad, out, inverse):
            delta = -jnp.sum(grad * out, axis=1, keepdims=True) * inverse
            first = delta.astype(LOW).astype(FLOAT)
            second = (delta - first).astype(LOW).astype(FLOAT)
            third = delta - first - second
            features = jnp.where(lanes == 0, first, jnp.where(lanes == 1, second, third))
            scaled = grad * inverse
            return jnp.where(lanes < 3, features, scaled).astype(LOW), scaled.astype(LOW)

        stats = stats_ref[spot, :]
        own_wide, own_low = widen(grads, outs, stats[:, 0:1])
        cross_wide, cross_low = widen(cross_grads, cross_out, stats[:, 1:2])
        own_pair = jnp.concatenate([query_low, own_low], axis=0)
        cross_pair = jnp.concatenate([query_low, cross_low], axis=0)

        def attend(key_part, value_part, wide, pair):
            weights = jnp.exp(matmul(key_part, query, 1, 1))
            grad_scores = (weights * matmul(value_part, wide, 1, 1)).astype(LOW)
            low = weights.astype(LOW)
            grad_pair = matmul(jnp.concatenate([grad_scores, low], axis=1), pair, 1, 0)
            return grad_pair, matmul(grad_scores, key_part, 0, 0)

        def step(index, total):
            part = pl.ds(pl.multiple_of(index * chunk, chunk), chunk)
            grad_pair, grad_query = attend(keys[part, :], values[part, :], own_wide, own_pair)
            acc[part, :] = grad_pair
            return total + grad_query

        def text_step(index, total):
            part = pl.ds(pl.multiple_of(index * text_chunk, text_chunk), text_chunk)
            grad_pair, grad_query = attend(
                text_keys[part, :], text_values[part, :], cross_wide, cross_pair
            )
            text_acc[part, :] = grad_pair
            return total + grad_query

        blank = jnp.zeros((rows, 128), FLOAT)
        total = lax.fori_loop(0, keys.shape[0] // chunk, step, blank, unroll=4)
        total = lax.fori_loop(0, text_keys.shape[0] // text_chunk, text_step, total, unroll=True)
        if not last:
            dq_ref[spot, :] = total
            return carry
        total = (total + before_ref[spot, :]) * 0.125
        each = rows // SPLIT
        for slot in range(SPLIT):
            hold[slot] = fold_low(total[each * slot : each * slot + each])
        return carry

    lax.fori_loop(0, 1, tile_step, 0)
    if last:
        for index, ref in enumerate(dq_refs):
            ref[...] = hold[index]
    for values, refs in ((acc, dkv_refs), (text_acc, dt_refs)):
        size = refs[0].shape[1]
        refs[0][0] = values[:size, :].astype(LOW)
        refs[1][0] = values[size:, :].astype(LOW)


def attention_backward(pairs, queries, qf, kf, tf, gates, grads, outs, stats, before):
    rows = qf.shape[0]
    heads = gates.shape[0]
    half = rows // SPLIT // 2
    last = len(before) > 0
    folded = jax.ShapeDtypeStruct((heads * half, 128), LOW)
    piece = jax.ShapeDtypeStruct((heads, kf.shape[0] // 4, 128), LOW)
    text = jax.ShapeDtypeStruct((heads, tf.shape[0] // 4, 128), LOW)
    sums = jax.ShapeDtypeStruct((heads, 8, 128), FLOAT)
    wide = jax.ShapeDtypeStruct((heads * rows, 128), FLOAT)
    wide_spec = pl.BlockSpec((rows, 128), lambda i: (i, 0))
    folded_spec = pl.BlockSpec((half, 128), lambda i: (i, 0))
    split = [piece, piece, text, text]

    def split_spec(value):
        return pl.BlockSpec((1,) + value.shape[1:], lambda i: (i, 0, 0))

    first_shapes = [folded] * SPLIT + [sums] if last else [wide]
    first_specs = [folded_spec] * SPLIT + [split_spec(sums)] if last else [wide_spec]
    out = pl.pallas_call(
        functools.partial(backward_kernel, len(pairs), pick_tile(kf.shape[0] // 2, 2048), last),
        grid=(heads,),
        in_specs=attention_specs(int(not last), pairs, queries, qf, kf, tf)
        + [folded_spec] * SPLIT
        + [wide_spec] * (2 + len(before)),
        out_specs=first_specs + [split_spec(value) for value in split],
        out_shape=first_shapes + split,
        scratch_shapes=attention_scratch(qf, kf, tf)
        + [
            pltpu.VMEM((SPLIT, half, 128), LOW),
            pltpu.VMEM((SPLIT, half, 128), LOW),
            pltpu.VMEM((kf.shape[0] // 2, 128), FLOAT),
            pltpu.VMEM((tf.shape[0] // 2, 128), FLOAT),
        ],
        compiler_params=pltpu.CompilerParams(vmem_limit_bytes=60 * MIB),
        cost_estimate=LARGE,
    )(*pairs, queries, qf, kf, tf, gates, *grads, outs, stats, *before)
    return out[: len(first_shapes)], out[len(first_shapes) :]


def half_means(values, lanes):
    low = jnp.sum(jnp.where(lanes < 64, values, 0.0), axis=1, keepdims=True)
    high = jnp.sum(jnp.where(lanes < 64, 0.0, values), axis=1, keepdims=True)
    return jnp.where(lanes < 64, low, high) * (1.0 / 64.0)


def swap_halves(values, lanes):
    return jnp.where(
        lax.rem(lanes, 64) < 32, pltpu.roll(values, 96, 1), pltpu.roll(values, 32, 1)
    )


def placed_at(groups, head, upper):
    values = groups[head // 2]
    return values if (head % 2 == 1) == upper else turn(values)


def rope_forward_kernel(heads, far_ref, qkv_ref, cos_ref, sin_ref, gains_ref, *refs):
    outs, hold = refs[:-1], refs[-1]
    width = heads * 64
    each = heads // SPLIT
    rows = qkv_ref.shape[0]
    cosine, sine = cos_ref[...], sin_ref[...]
    lanes = lane_ids(cosine.shape)

    def turned(start, gain):
        groups = []
        for index in range(heads // 2):
            raw = qkv_ref[:, start + 128 * index : start + 128 * index + 128]
            normed = raw * lax.rsqrt(half_means(raw * raw, lanes) + EPS) * gain
            groups.append(normed * cosine + swap_halves(normed, lanes) * sine)
        return groups

    queries = turned(0, gains_ref[0:1, :])
    keys = turned(width, gains_ref[1:2, :])
    values = [
        qkv_ref[:, 2 * width + 128 * index : 2 * width + 128 * index + 128]
        for index in range(heads // 2)
    ]
    for head in range(heads):
        group, index = head // each, head % each
        slot = lax.rem(group - far_ref[0] + SPLIT, SPLIT)
        pair = jnp.where(
            lanes < 64, placed_at(keys, head, False), placed_at(values, head, True)
        )
        hold[slot, index, :rows, :] = pair.astype(LOW)
        hold[slot, index, rows:, :] = fold_low(placed_at(queries, head, False))
    size = rows * 3 // 2
    for slot in range(SPLIT):
        for index in range(each):
            outs[slot][size * index : size * index + size, :] = hold[slot, index]


def small_call(kernel, operands, shapes, scratch):
    out = pl.pallas_call(
        kernel,
        in_specs=[pl.BlockSpec(memory_space=pltpu.SMEM)]
        + [pl.BlockSpec(memory_space=pltpu.VMEM)] * (len(operands) - 1),
        out_specs=[pl.BlockSpec(memory_space=pltpu.VMEM)] * len(shapes),
        out_shape=shapes,
        scratch_shapes=scratch,
        compiler_params=pltpu.CompilerParams(vmem_limit_bytes=32 * MIB),
        cost_estimate=SMALL,
    )(*operands)
    return out


def rope_forward(far, qkv, cosine, sine, gains, heads):
    rows = qkv.shape[0] * 3 // 2
    each = heads // SPLIT
    out = small_call(
        functools.partial(rope_forward_kernel, heads),
        (far, qkv, cosine, sine, gains),
        [jax.ShapeDtypeStruct((each * rows, 128), LOW)] * SPLIT,
        [pltpu.VMEM((SPLIT, each, rows, 128), LOW)],
    )
    return list(out)


def rope_backward_kernel(heads, far_ref, *refs):
    parts, refs = refs[:SPLIT], refs[SPLIT:]
    qkv_ref, cos_ref, sin_ref, gains_ref, out_ref, sums_ref, hold = refs
    width = heads * 64
    each = heads // SPLIT
    rows = qkv_ref.shape[0]
    for slot in range(SPLIT):
        group = lax.rem(far_ref[0] + slot, SPLIT)
        size = hold.shape[2]
        for index in range(each):
            hold[group, index] = parts[slot][size * index : size * index + size, :]
    cosine, sine = cos_ref[...], sin_ref[...]
    lanes = lane_ids(cosine.shape)

    def found(kind, head):
        group, index, upper = head // each, head % each, head % 2 == 1
        if kind == 0:
            packed = hold[group, index, rows:, :]
            return unfold_high(packed) if upper else unfold_low(packed)
        values = hold[group, index, :rows, :].astype(FLOAT)
        return values if upper == (kind == 2) else turn(values)

    def joined(kind, index):
        return jnp.where(lanes < 64, found(kind, 2 * index), found(kind, 2 * index + 1))

    for kind in range(2):
        gain = gains_ref[kind : kind + 1, :]
        total = jnp.zeros((1, 128), FLOAT)
        for index in range(heads // 2):
            spot = kind * width + 128 * index
            raw = qkv_ref[:, spot : spot + 128]
            inverse = lax.rsqrt(half_means(raw * raw, lanes) + EPS)
            unit = raw * inverse
            grad = joined(kind, index)
            back = grad * cosine - swap_halves(grad, lanes) * sine
            total = total + jnp.sum(back * unit, axis=0, keepdims=True)
            scaled = back * gain
            raw_grad = inverse * (scaled - unit * half_means(scaled * unit, lanes))
            out_ref[:, spot : spot + 128] = raw_grad.astype(LOW)
        sums_ref[kind : kind + 1, :] = total
    sums_ref[2:8, :] = jnp.zeros((6, 128), FLOAT)
    for index in range(heads // 2):
        spot = 2 * width + 128 * index
        out_ref[:, spot : spot + 128] = joined(2, index).astype(LOW)


def rope_backward(far, parts, qkv, cosine, sine, gains, heads):
    each = heads // SPLIT
    return small_call(
        functools.partial(rope_backward_kernel, heads),
        (far, *parts, qkv, cosine, sine, gains),
        [jax.ShapeDtypeStruct(qkv.shape, LOW), jax.ShapeDtypeStruct((8, 128), FLOAT)],
        [pltpu.VMEM((SPLIT, each, parts[0].shape[0] // each, 128), LOW)],
    )


def join_kernel(heads, far_ref, *refs):
    parts, out_ref, hold = refs[:SPLIT], refs[SPLIT], refs[SPLIT + 1]
    each = heads // SPLIT
    half = hold.shape[2]
    for slot in range(SPLIT):
        group = lax.rem(far_ref[0] + slot, SPLIT)
        for index in range(each):
            hold[group, index] = parts[slot][half * index : half * index + half, :]
    for pair in range(heads // 2):
        low = unfold_low(hold[2 * pair // each, 2 * pair % each])
        high = unfold_high(hold[(2 * pair + 1) // each, (2 * pair + 1) % each])
        out_ref[:, 128 * pair : 128 * pair + 128] = jnp.where(
            lane_ids(low.shape) < 64, low, high
        ).astype(LOW)


def join_heads(far, parts, heads):
    each = heads // SPLIT
    half = parts[0].shape[0] // each
    return small_call(
        functools.partial(join_kernel, heads),
        (far, *parts),
        [jax.ShapeDtypeStruct((2 * half, heads * 64), LOW)],
        [pltpu.VMEM((SPLIT, each, half, 128), LOW)],
    )[0]


def split_kernel(heads, far_ref, grad_ref, *refs):
    outs, hold = refs[:-1], refs[-1]
    each = heads // SPLIT
    half = hold.shape[2]
    for head in range(heads):
        group, index = head // each, head % each
        slot = lax.rem(group - far_ref[0] + SPLIT, SPLIT)
        values = grad_ref[:, 128 * (head // 2) : 128 * (head // 2) + 128]
        hold[slot, index] = fold_high(values) if head % 2 else fold_low(values)
    for slot in range(SPLIT):
        for index in range(each):
            outs[slot][half * index : half * index + half, :] = hold[slot, index]


def split_heads(far, grads, heads):
    each = heads // SPLIT
    half = grads.shape[0] // 2
    return small_call(
        functools.partial(split_kernel, heads),
        (far, grads),
        [jax.ShapeDtypeStruct((each * half, 128), LOW)] * SPLIT,
        [pltpu.VMEM((SPLIT, each, half, 128), LOW)],
    )


def local_call(kernel, operands, shapes):
    return pl.pallas_call(
        kernel,
        out_shape=shapes,
        compiler_params=pltpu.CompilerParams(vmem_limit_bytes=40 * MIB),
        cost_estimate=SMALL,
    )(*operands)


def gather_kernel(each, *refs):
    slots, text_ref, pairs_ref, queries_ref = refs[:SPLIT], refs[SPLIT], refs[-2], refs[-1]
    size = slots[0].shape[0] // each
    rows = size * 2 // 3
    for head in range(each):
        for index, slot in enumerate(slots):
            spot = (head * SPLIT + index) * rows
            first = head * size
            pairs_ref[spot : spot + rows, :] = slot[first : first + rows, :]
            query = unfold_low(slot[first + rows : first + size, :])
            query = jnp.where(lane_ids(query.shape) < 64, query * 0.125, 0.0)
            queries_ref[spot : spot + rows, :] = query.astype(LOW)
    pairs_ref[each * SPLIT * rows :, :] = text_ref[...]


def gather_slots(slots, text, each):
    rows = slots[0].shape[0] * 2 // 3 * SPLIT
    return local_call(
        functools.partial(gather_kernel, each),
        (*slots, text),
        [
            jax.ShapeDtypeStruct((rows + text.shape[0], 128), LOW),
            jax.ShapeDtypeStruct((rows, 128), LOW),
        ],
    )


def pack_kernel(terms, *refs):
    inputs, folded, outs = refs[:terms], refs[terms : terms + SPLIT], refs[terms + SPLIT :]
    each = inputs[0].shape[0]
    size = outs[0].shape[0] // each
    rows = size * 2 // 3
    half = size - rows
    for head in range(each):
        for slot in range(SPLIT):
            total = sum(
                term[head, rows * slot : rows * slot + rows, :].astype(FLOAT) for term in inputs
            )
            spot = size * head
            outs[slot][spot : spot + rows, :] = total.astype(LOW)
            outs[slot][spot + rows : spot + size, :] = folded[slot][
                half * head : half * head + half, :
            ]


def pack_slots(terms, folded):
    return local_call(
        functools.partial(pack_kernel, len(terms)),
        (*terms, *folded),
        [jax.ShapeDtypeStruct((3 * folded[0].shape[0], 128), LOW)] * SPLIT,
    )


def text_split_kernel(far_ref, text_ref, *outs):
    size = outs[0].shape[1]
    for slot in range(SPLIT):
        group = lax.rem(far_ref[0] + slot, SPLIT)
        spot = pl.ds(pl.multiple_of(group * size, 128), size)
        outs[slot][...] = text_ref[:, spot].astype(LOW)


def text_join_kernel(far_ref, *refs):
    parts, out_ref = refs[:SPLIT], refs[SPLIT]
    size = parts[0].shape[1]
    for slot in range(SPLIT):
        group = lax.rem(far_ref[0] + slot, SPLIT)
        out_ref[:, pl.ds(pl.multiple_of(group * size, 128), size)] = parts[slot][...]


def low_means(values, lanes):
    return jnp.sum(jnp.where(lanes < 64, values, 0.0), axis=1, keepdims=True) * (1.0 / 64.0)


def text_norm_kernel(*refs):
    parts, gain_ref, raw_ref, out_ref = refs[:SPLIT], refs[SPLIT], refs[-2], refs[-1]
    rows = raw_ref.shape[0]
    raw = sum(part[...].astype(FLOAT) for part in parts)
    raw_ref[...] = raw
    for head in range(raw.shape[1] // 128):
        values = raw[:, 128 * head : 128 * head + 128]
        lanes = lane_ids(values.shape)
        normed = values * lax.rsqrt(low_means(values * values, lanes) + EPS) * gain_ref[0:1, :]
        out_ref[rows * head : rows * head + rows, :] = jnp.where(
            lanes < 64, normed, values
        ).astype(LOW)


def text_back_kernel(terms, *refs):
    inputs, refs = refs[:terms], refs[terms:]
    raw_ref, gain_ref, out_ref, sums_ref = refs
    rows = raw_ref.shape[0]
    total_gain = jnp.zeros((1, 128), FLOAT)
    for head in range(inputs[0].shape[0]):
        grad = sum(term[head, :rows, :].astype(FLOAT) for term in inputs)
        grad = grad.astype(LOW).astype(FLOAT)
        raw = raw_ref[:, 128 * head : 128 * head + 128]
        lanes = lane_ids(raw.shape)
        inverse = lax.rsqrt(low_means(raw * raw, lanes) + EPS)
        unit = raw * inverse
        total_gain = total_gain + jnp.sum(grad * unit, axis=0, keepdims=True)
        scaled = grad * gain_ref[0:1, :]
        back = inverse * (scaled - unit * low_means(scaled * unit, lanes))
        out_ref[:, 128 * head : 128 * head + 128] = jnp.where(lanes < 64, back, grad).astype(LOW)
    sums_ref[...] = jnp.broadcast_to(total_gain, sums_ref.shape)


def tie(*values):
    return lax.optimization_barrier(values)


def outer_kernel(bound, *refs):
    first, second, out_ref = refs[:4], refs[4:8], refs[8]
    step = pl.program_id(0)

    def run(group):
        own_left, other_left, own_right, other_right = group
        out_ref[...] = (
            matmul(own_left[...], own_right[0], 1, 0)
            + matmul(other_left[...], other_right[0], 1, 0)
        ).astype(LOW)

    @pl.when(step < bound)
    def _():
        run(first)

    @pl.when(step >= bound)
    def _():
        run(second)


def outer_products(first, second, tile):
    depth = first[0].shape[0]
    steps = [group[2].shape[0] * group[2].shape[2] // tile for group in (first, second)]
    specs, operands = [], []
    for index, group in enumerate((first, second)):
        rows, columns = group[2].shape[1:]
        tiles = columns // tile

        def right_at(i, index=index, tiles=tiles):
            if index == 0:
                at = jnp.minimum(i, steps[0] - 1)
            else:
                at = jnp.maximum(i - steps[0], 0)
            return (at // tiles, 0, at % tiles)

        specs += [whole(group[0].shape)] * 2
        specs += [pl.BlockSpec((1, rows, tile), right_at)] * 2
        operands += group
    return pl.pallas_call(
        functools.partial(outer_kernel, steps[0]),
        grid=(sum(steps),),
        in_specs=specs,
        out_specs=pl.BlockSpec((depth, tile), lambda i: (0, i)),
        out_shape=jax.ShapeDtypeStruct((depth, sum(steps) * tile), LOW),
        compiler_params=pltpu.CompilerParams(vmem_limit_bytes=48 * MIB),
        cost_estimate=SMALL,
    )(*operands)


def columns_kernel(order, core_ref, values_ref, own_ref, other_ref, hold):
    turned = jnp.transpose(values_ref[...].astype(FLOAT))
    hold[...] = turned.reshape(hold.shape)
    core = core_ref[0]
    own_ref[...] = jnp.concatenate(
        [hold[2 * pair + core] for pair in order], axis=0
    ).astype(LOW)
    other_ref[...] = jnp.concatenate(
        [hold[2 * pair + 1 - core] for pair in order], axis=0
    ).astype(LOW)


def split_columns(core, values, block, order):
    rows, width = values.shape
    half = jax.ShapeDtypeStruct((width // 2, rows), LOW)
    return small_call(
        functools.partial(columns_kernel, order),
        (core, values),
        [half, half],
        [pltpu.VMEM((width // block, block, rows), FLOAT)],
    )


def feed_kernel(
    normed_ref, grad_ref, gate_ref, up_ref, down_ref,
    hidden_ref, grads_ref, feed_own_ref, feed_other_ref, norm_own_ref, norm_other_ref,
    feed_acc, norm_acc,
):
    step = pl.program_id(0)

    @pl.when(step == 0)
    def _():
        feed_acc[...] = jnp.zeros_like(feed_acc)
        norm_acc[...] = jnp.zeros_like(norm_acc)

    normed = normed_ref[...]
    gate = matmul(normed, gate_ref[...], 1, 0)
    up = matmul(normed, up_ref[...], 1, 0)
    grad_hidden = matmul(grad_ref[...], down_ref[...], 1, 0)
    sigmoid = 1.0 / (1.0 + jnp.exp(-gate))
    silu = gate * sigmoid
    hidden = (silu * up).astype(LOW)
    grad_gate = (grad_hidden * up * sigmoid * (1.0 + gate * (1.0 - sigmoid))).astype(LOW)
    grad_up = (grad_hidden * silu).astype(LOW)
    hidden_ref[0] = hidden
    grads_ref[0] = grad_gate
    grads_ref[1] = grad_up
    feed_acc[...] += matmul(hidden, down_ref[...], 1, 1)
    norm_acc[...] += matmul(grad_gate, gate_ref[...], 1, 1) + matmul(grad_up, up_ref[...], 1, 1)

    @pl.when(step == pl.num_programs(0) - 1)
    def _():
        half = feed_own_ref.shape[0]
        feed_own_ref[...] = feed_acc[:half, :]
        feed_other_ref[...] = feed_acc[half:, :].astype(LOW)
        norm_own_ref[...] = norm_acc[:half, :]
        norm_other_ref[...] = norm_acc[half:, :].astype(LOW)


def feed_forward(normed, grads, weights, columns, tile):
    rows, width = normed.shape
    tiles = columns // tile
    own = jax.ShapeDtypeStruct((rows // 2, width), FLOAT)
    other = jax.ShapeDtypeStruct((rows // 2, width), LOW)
    return pl.pallas_call(
        feed_kernel,
        grid=(tiles,),
        in_specs=[whole(normed.shape), whole(grads.shape)]
        + [
            pl.BlockSpec((width, tile), lambda i, part=part: (0, part * tiles + i))
            for part in range(3)
        ],
        out_specs=[
            pl.BlockSpec((1, rows, tile), lambda i: (0, 0, i)),
            pl.BlockSpec((2, rows, tile), lambda i: (0, 0, i)),
        ]
        + [whole(own.shape)] * 4,
        out_shape=[
            jax.ShapeDtypeStruct((1, rows, columns), LOW),
            jax.ShapeDtypeStruct((2, rows, columns), LOW),
            own,
            other,
            own,
            other,
        ],
        scratch_shapes=[pltpu.VMEM((rows, width), FLOAT)] * 2,
        compiler_params=pltpu.CompilerParams(vmem_limit_bytes=48 * MIB),
        cost_estimate=SMALL,
    )(normed, grads, weights, weights, weights)


def dot_float(left, right):
    return jnp.dot(left, right, preferred_element_type=FLOAT)


def dot_turned(left, right):
    return matmul(left, right, 1, 1)


def norm_rows(values, gains):
    return values * lax.rsqrt(jnp.mean(values * values, axis=-1, keepdims=True) + EPS) * gains


def modulated(values, gains, shifts, scales):
    return norm_rows(values, gains) * (1.0 + scales) + shifts


def swapped(values):
    return lax.ppermute(values, "tensor", [(0, 1), (1, 0)])


def both_rows(values):
    return jnp.concatenate([values, swapped(values)], axis=0)


def own_rows(partial):
    rows = partial.shape[0] // 2
    return partial[:rows] + swapped(partial[rows:].astype(LOW)).astype(FLOAT)


def shards(
    inputs,
    clip_ids,
    positions,
    text_tokens,
    conditioning,
    ada_weight,
    ada_bias,
    first_norm_gain,
    query_gain,
    key_gain,
    text_key_gain,
    head_gate,
    qkv_weight,
    out_weight,
    text_kv_weight,
    second_norm_gain,
    gate_up_weight,
    down_weight,
    grad_output,
):
    dp = lax.axis_size("dp")
    near = dp // SPLIT
    bits = [near >> (step + 1) for step in range(near.bit_length() - 1)]
    tensor_index = lax.axis_index("tensor")
    dp_index = lax.axis_index("dp")
    far_index, near_index = dp_index // near, dp_index % near
    row_count, width = inputs.shape
    token_count = clip_ids.shape[0]
    head_size = query_gain.shape[0]
    local_width = qkv_weight.shape[2]
    heads = local_width // head_size
    each = heads // SPLIT
    part_width = each * head_size
    clip_count = conditioning.shape[0]
    hidden_count = gate_up_weight.shape[2]
    weight_rows = qkv_weight.shape[1]

    def flip(values, bit):
        return lax.ppermute(values, "dp", [(j, j ^ bit) for j in range(dp)])

    def shift(values, steps):
        pairs = [(j, ((j // near + steps) % SPLIT) * near + j % near) for j in range(dp)]
        return lax.ppermute(values, "dp", pairs)

    def sum_dp(values):
        step = 1
        while step < dp:
            values = values + flip(values, step)
            step *= 2
        return values

    def spread(values):
        for bit in bits:
            values = jnp.concatenate([values, flip(values, bit)], axis=0)
        return values

    def spread_list(values):
        values = [values]
        for bit in bits[1:]:
            values = values + [flip(value, bit) for value in values]
        return values

    def collect(values):
        for bit in reversed(bits):
            half = values.shape[0] // 2
            values = values[:half].astype(FLOAT) + flip(
                values[half:].astype(LOW), bit
            ).astype(FLOAT)
        return values

    def pick(stacked, index):
        return lax.dynamic_index_in_dim(stacked, index, 0, keepdims=False)

    def send_parts(stacked):
        out = [pick(stacked, far_index)]
        for steps in range(1, SPLIT):
            out.append(shift(pick(stacked, (far_index + steps) % SPLIT), steps))
        return out

    def send_slots(slots):
        return [slots[0]] + [shift(slots[steps], steps) for steps in range(1, SPLIT)]

    def return_slots(slots):
        return [slots[0]] + [shift(slots[steps], -steps) for steps in range(1, SPLIT)]

    flips = []
    for order in range(near):
        mask = 0
        for place, bit in enumerate(bits):
            if order >> place & 1:
                mask |= bit
        flips.append(mask)

    core = dp_index % 2
    pair_order = []
    for column in range(near // 2):
        line = [group * (near // 2) + column for group in range(SPLIT)]
        pair_order += line if column % 2 == 0 else line[::-1]
    core_groups = [[2 * pair + first for pair in pair_order] for first in range(2)]

    core_at = core.astype(jnp.int32).reshape(1)

    def core_columns(values):
        own, other = split_columns(core_at, values, weight_rows, pair_order)
        return own, flip(other, 1)

    def scatter(values):
        return lax.psum_scatter(
            values, "dp", scatter_dimension=0, axis_index_groups=core_groups, tiled=True
        )

    qkv_full = lax.all_gather(
        qkv_weight.transpose(1, 0, 2).reshape(weight_rows, 3 * local_width),
        "dp",
        axis=0,
        tiled=True,
    )
    cond_float = conditioning.astype(FLOAT)
    silu_cond = jax.nn.silu(cond_float).astype(LOW)
    cond_rows = ada_weight.shape[0]
    silu_slice = lax.dynamic_slice_in_dim(silu_cond, dp_index * cond_rows, cond_rows, axis=1)
    first_rows = jnp.sum((clip_ids == 0).astype(FLOAT))
    spots = jnp.arange(ada_weight.shape[1], dtype=jnp.int32)
    early = 2 * width
    early_part = jnp.concatenate(
        [
            dot_float(silu_slice, ada_weight[:, :early]),
            jnp.where(spots[:early] == dp_index, first_rows, 0.0)[None],
        ],
        axis=0,
    )
    text_columns = lax.all_to_all(text_tokens, "dp", split_axis=1, concat_axis=0, tiled=True)
    early_part, text_columns = tie(early_part, text_columns)
    early_sum = sum_dp(early_part)
    bias = ada_bias.astype(FLOAT)
    early_mod = early_sum[:clip_count] + bias[:early]
    counts = early_sum[clip_count, :dp].astype(jnp.int32)

    own_ids = lax.dynamic_slice_in_dim(clip_ids, tensor_index * row_count, row_count)
    row_positions = jnp.where(
        tensor_index == 0, positions, jnp.roll(positions, row_count)
    )
    other_clip = jnp.max(clip_ids)
    first_clip = (own_ids == 0)[:, None]

    def mod_blocks(modulation):
        rows = jnp.where(
            first_clip,
            modulation[0:1],
            lax.dynamic_slice_in_dim(modulation, other_clip, 1, 0),
        )
        return jnp.split(rows, rows.shape[1] // width, axis=1)

    shift_one, scale_one = mod_blocks(early_mod)
    input_rows = inputs.astype(FLOAT)
    first_gain = first_norm_gain.astype(FLOAT)
    normed_one = modulated(input_rows, first_gain, shift_one, scale_one).astype(LOW)
    normed_all = both_rows(normed_one)
    late_sum = sum_dp(dot_float(silu_slice, ada_weight[:, early:]))

    half_size = head_size // 2
    frequency = 10000.0 ** (-(jnp.arange(half_size, dtype=FLOAT) * 2.0 / head_size))
    angles = row_positions.astype(FLOAT)[:, None] * frequency[None, :]
    cosine = jnp.cos(angles)
    sine = jnp.sin(angles)
    cosine = jnp.concatenate([cosine] * 4, axis=1)
    sine = jnp.concatenate([-sine, sine, -sine, sine], axis=1)
    gains = jnp.stack([jnp.tile(query_gain, 2), jnp.tile(key_gain, 2)]).astype(FLOAT)
    gains = jnp.concatenate([gains, jnp.zeros((6, 128), FLOAT)], axis=0)

    text_rows = text_tokens.shape[0]
    group_rows = text_rows * SPLIT
    text_groups = text_columns.reshape(near, group_rows, text_columns.shape[1])
    text_near = jnp.concatenate([pick(text_groups, near_index ^ mask) for mask in flips], axis=0)
    text_weight = (
        text_kv_weight.reshape(2, -1, SPLIT, each, head_size)
        .transpose(1, 2, 3, 0, 4)
        .reshape(-1, 2 * local_width)
    )
    far = far_index.astype(jnp.int32).reshape(1)
    text_sum = collect(dot_float(text_near, text_weight))
    part_shape = jax.ShapeDtypeStruct((group_rows, 2 * part_width), LOW)
    text_parts = small_call(text_split_kernel, (far, text_sum), [part_shape] * SPLIT, [])
    ky_gain = jnp.concatenate([text_key_gain.astype(FLOAT), jnp.zeros((128 - head_size,), FLOAT)])
    ky_gain = jnp.broadcast_to(ky_gain[None], (8, 128))

    lanes = jnp.arange(128, dtype=jnp.int32)[None, :]
    ordered = flips[0::2] + flips[1::2]
    text_groups_at = jnp.stack([near_index ^ mask for mask in ordered])
    text_clip = (
        text_groups_at[:, None] * group_rows + jnp.arange(group_rows, dtype=jnp.int32)[None, :]
    ).reshape(-1) // TXT
    text_features = (lanes == 64 + text_clip[:, None]).astype(LOW)
    block_at = jnp.stack(
        [
            ((far_index - steps) % SPLIT) * near + (near_index ^ mask)
            for mask in ordered
            for steps in range(SPLIT)
        ]
    )
    block_count = jnp.sum(
        jnp.where(block_at[:, None] == jnp.arange(dp, dtype=jnp.int32)[None, :], counts[None, :], 0),
        axis=1,
    )
    row_at = (jnp.arange(token_count, dtype=jnp.int32) + tensor_index * row_count) % token_count
    key_clip = jnp.where(
        row_at[None, :] < block_count[:, None], 0, 1 + block_at[:, None] // GROUP
    ).reshape(-1)
    key_features = (lanes == 64 + key_clip[:, None]).astype(LOW)
    group_tokens = SPLIT * token_count
    query_clip = key_clip[:group_tokens, None]
    query_features = jnp.where(
        (lanes >= 64) & (lanes < 64 + clip_count) & (lanes != 64 + query_clip), MASK, 0.0
    ).astype(LOW)
    gate_heads = jnp.tanh(
        lax.dynamic_slice_in_dim(
            head_gate.astype(FLOAT), tensor_index * heads + far_index * each, each
        )
    )
    gate_lanes = jnp.broadcast_to(gate_heads[:, None, None], (each, 8, 128))

    rest_weights, qkv_full, normed_all, text_parts, late_sum, key_features, query_features = tie(
        jnp.concatenate(
            [gate_up_weight[0], gate_up_weight[1], down_weight.T, out_weight.T], axis=1
        ),
        qkv_full,
        normed_all,
        text_parts,
        late_sum,
        key_features,
        query_features,
    )
    rest_full = lax.all_gather(rest_weights, "dp", axis=0, tiled=True)
    out_full = rest_full[:, 3 * hidden_count :]
    text_arrived = send_slots(text_parts)
    qkv_raw = dot_float(normed_all, qkv_full)
    head_slots = rope_forward(far, qkv_raw, cosine, sine, gains, heads)
    gate_one, shift_two, scale_two, gate_two = mod_blocks(late_sum + bias[early:])
    grad_two = grad_output.astype(FLOAT)
    grad_ffn = both_rows((gate_two * grad_two).astype(LOW))
    head_slots, text_arrived = tie(head_slots, text_arrived)
    text_raw, text_pairs = local_call(
        text_norm_kernel,
        (*text_arrived, ky_gain),
        [
            jax.ShapeDtypeStruct((group_rows, 2 * part_width), FLOAT),
            jax.ShapeDtypeStruct((each * group_rows, 128), LOW),
        ],
    )
    arrived = send_slots(head_slots)
    arrived, grad_ffn = tie(arrived, grad_ffn)
    own_pairs, queries = gather_slots(arrived, text_pairs, each)
    far_pairs = flip(own_pairs, bits[0])
    near_keys = spread_list(own_pairs)
    shared = (queries, query_features, key_features, text_features, gate_lanes)
    partial_sums = attention_forward(near_keys, *shared, ())
    far_pairs, partial_sums = tie(far_pairs, partial_sums)
    far_keys = spread_list(far_pairs)
    mixed_slots, head_outs, head_stats = attention_forward(far_keys, *shared, partial_sums)
    mixed = join_heads(far, return_slots(mixed_slots), heads)
    attn_rows = own_rows(dot_turned(mixed, out_full))
    after_attn = input_rows + gate_one * attn_rows
    second_gain = second_norm_gain.astype(FLOAT)
    normed_two_all = both_rows(modulated(after_attn, second_gain, shift_two, scale_two).astype(LOW))
    hidden_low, feed_grads, feed_own, feed_other, norm_own, norm_other = feed_forward(
        normed_two_all, grad_ffn, rest_full, hidden_count, 512
    )
    feed_weights_grad = outer_products(
        [*core_columns(normed_two_all), feed_grads, flip(feed_grads, 1)],
        [*core_columns(grad_ffn), hidden_low, flip(hidden_low, 1)],
        512,
    )
    norm_other = swapped(norm_other)
    grad_normed_two = norm_own + norm_other.astype(FLOAT)
    _, pull_two = jax.vjp(modulated, after_attn, second_gain, shift_two, scale_two)
    back_two, grad_second_gain, grad_shift_two, grad_scale_two = pull_two(grad_normed_two)
    grad_after = grad_two + back_two
    grad_attn, feed_other = tie(both_rows((gate_one * grad_after).astype(LOW)), feed_other)
    ffn_rows = feed_own + swapped(feed_other).astype(FLOAT)
    output = (after_attn + gate_two * ffn_rows).astype(LOW)
    grad_gate_two = grad_two * ffn_rows
    grad_gate_one = grad_after * attn_rows
    grad_slots = send_slots(split_heads(far, dot_float(grad_attn, out_full), heads))
    normed_core = core_columns(normed_all)
    last_left = [normed_core, core_columns(grad_attn)]
    mixed_right = mixed[None]
    mixed_other = flip(mixed_right, 1)
    grad_slots, feed_weights_grad, last_left, mixed_other = tie(
        grad_slots, feed_weights_grad, last_left, mixed_other
    )
    feed_low = scatter(feed_weights_grad)

    def total_rows(terms, first, last):
        return sum(term[:, first:last].astype(FLOAT) for term in terms).astype(LOW)

    def start_sums(keep, send, text_keep, text_send):
        return (
            [keep, flip(send, bits[-1])],
            [text_keep, flip(text_send, bits[-1])],
        )

    def next_send(state):
        terms, text_terms = state
        size, text_size = terms[-1].shape[1], text_terms[-1].shape[1]
        return jnp.concatenate(
            [
                total_rows(terms, size // 2, size),
                total_rows(text_terms, text_size // 2, text_size),
            ],
            axis=1,
        )

    def next_state(state, sent, bit):
        terms, text_terms = state
        size = terms[-1].shape[1] // 2
        other = flip(sent, bit)
        return terms + [other[:, :size]], text_terms + [other[:, size:]]

    def reduce_near(pieces):
        state = start_sums(*pieces)
        for bit in reversed(bits[1:-1]):
            state = next_state(state, next_send(state), bit)
        return state

    saved = (head_outs, head_stats)
    query_part, far_pieces = attention_backward(far_keys, *shared, grad_slots, *saved, ())
    far_terms, far_text = reduce_near(far_pieces)
    sent = jnp.concatenate(
        [
            total_rows(far_terms, 0, group_tokens),
            total_rows(far_text, 0, group_rows),
        ],
        axis=1,
    )
    grad_slots, sent = tie(grad_slots, sent)
    came = flip(sent, bits[0])
    (*folded, gate_parts), own_pieces = attention_backward(
        near_keys, *shared, grad_slots, *saved, query_part
    )
    pair_terms, text_terms = reduce_near(own_pieces)
    pair_terms = pair_terms + [came[:, :group_tokens]]
    text_terms = text_terms + [came[:, group_tokens:]]
    back_slots = pack_slots(pair_terms, folded)
    clip_at = jnp.arange(clip_count, dtype=jnp.int32)[:, None]

    def clip_sums(values):
        first_sum = jnp.sum(jnp.where(first_clip, values, 0.0), axis=0)[None]
        other_sum = jnp.sum(jnp.where(first_clip, 0.0, values), axis=0)[None]
        return jnp.where(clip_at == 0, first_sum, jnp.where(clip_at == other_clip, other_sum, 0.0))

    def pair_sums(blocks, gains_row):
        wide = jnp.concatenate([clip_sums(values) for values in blocks], axis=1)
        gains_row = jnp.concatenate(
            [gains_row, jnp.zeros((wide.shape[1] - gains_row.shape[0],), FLOAT)]
        )
        wide = jnp.concatenate([wide, gains_row[None]], axis=0)
        return wide + swapped(wide)

    back_parts = return_slots(back_slots)
    text_low, ky_sums = local_call(
        functools.partial(text_back_kernel, len(text_terms)),
        (*text_terms, text_raw, ky_gain),
        [part_shape, jax.ShapeDtypeStruct((8, 128), FLOAT)],
    )
    qkv_grad, gain_sums = rope_backward(far, back_parts, qkv_raw, cosine, sine, gains, heads)
    normed_part = dot_turned(qkv_grad, qkv_full)
    qkv_right = qkv_grad[None]
    last_grads = outer_products(
        [*last_left[0], qkv_right, flip(qkv_right, 1)],
        [*last_left[1], mixed_right, mixed_other],
        local_width,
    )
    normed_part, last_grads, text_low = tie(normed_part, last_grads, text_low)
    last_grads, feed_low = tie(last_grads, feed_low)
    last_low = scatter(last_grads)
    grad_normed_one = own_rows(normed_part)
    _, pull_one = jax.vjp(modulated, input_rows, first_gain, shift_one, scale_one)
    back_one, grad_first_gain, grad_shift_one, grad_scale_one = pull_one(grad_normed_one)
    grad_inputs = grad_after + back_one
    head_sums = (1.0 - gate_heads * gate_heads) * jnp.sum(gate_parts, axis=(1, 2))
    head_row = lax.dynamic_update_slice_in_dim(
        jnp.zeros((head_gate.shape[0],), FLOAT),
        head_sums,
        tensor_index * heads + far_index * each,
        0,
    )
    gain_halves = gain_sums[:2, :head_size] + gain_sums[:2, head_size:]
    all_pairs = pair_sums(
        (
            grad_shift_one,
            grad_scale_one,
            grad_gate_one,
            grad_shift_two,
            grad_scale_two,
            grad_gate_two,
        ),
        jnp.concatenate(
            [
                grad_first_gain,
                grad_second_gain,
                gain_halves.reshape(-1),
                ky_sums[0, :head_size],
                head_row,
            ]
        ),
    )
    text_wide = small_call(
        text_join_kernel,
        (far, *return_slots([text_low] * SPLIT)),
        [jax.ShapeDtypeStruct((group_rows, 2 * local_width), LOW)],
        [],
    )[0]
    text_all = spread(text_wide)
    all_pairs, text_all = tie(all_pairs, text_all)
    grad_sums = sum_dp(all_pairs)
    grad_mod_low, sums = grad_sums[:clip_count].astype(LOW), grad_sums[clip_count]
    first_gain_sum = sums[:width]
    second_gain_sum = sums[width : 2 * width]
    at = 2 * width
    q_gain_sum = sums[at : at + head_size]
    k_gain_sum = sums[at + head_size : at + 2 * head_size]
    ky_gain_sum = sums[at + 2 * head_size : at + 3 * head_size]
    gate_sum = sums[at + 3 * head_size : at + 3 * head_size + head_gate.shape[0]]
    grad_text_kv = (
        matmul(text_near, text_all, 0, 0)
        .reshape(-1, SPLIT, each, 2, head_size)
        .transpose(3, 0, 1, 2, 4)
        .reshape(2, -1, local_width)
    )
    grad_text_part = dot_turned(text_all, text_weight).astype(LOW)
    grad_text_pair = grad_text_part.astype(FLOAT) + swapped(grad_text_part).astype(FLOAT)
    grad_text_groups = grad_text_pair.astype(LOW).reshape(near, group_rows, -1)
    orders = jnp.arange(near, dtype=jnp.int32)
    flip_at = jnp.array(flips, jnp.int32)
    grad_text_rows = jnp.concatenate(
        [
            pick(grad_text_groups, jnp.sum(jnp.where(flip_at == near_index ^ group, orders, 0)))
            for group in range(near)
        ],
        axis=0,
    )
    grad_text_all = lax.all_to_all(grad_text_rows, "dp", split_axis=0, concat_axis=1, tiled=True)
    half_text = text_tokens.shape[1] // 2
    grad_text = lax.dynamic_slice_in_dim(
        grad_text_all, tensor_index * half_text, half_text, 1
    ).astype(FLOAT)
    grad_ada_bias = jnp.sum(grad_mod_low.astype(FLOAT), axis=0)
    grad_ada = matmul(silu_slice, grad_mod_low, 0, 0)
    cond_part = lax.dynamic_update_slice_in_dim(
        jnp.zeros(cond_float.shape, FLOAT),
        dot_turned(grad_mod_low, ada_weight),
        dp_index * cond_rows,
        1,
    )
    cond_sigmoid = jax.nn.sigmoid(cond_float)
    grad_conditioning = (
        sum_dp(cond_part) * cond_sigmoid * (1.0 + cond_float * (1.0 - cond_sigmoid))
    )
    last_shard = last_low.astype(FLOAT)
    qkv_shard = last_shard[:, : 3 * local_width].reshape(weight_rows, 3, local_width).transpose(1, 0, 2)
    feed_shard = feed_low.astype(FLOAT)
    gate_up_shard = jnp.stack(
        [feed_shard[:, :hidden_count], feed_shard[:, hidden_count : 2 * hidden_count]]
    )
    out_shard = last_shard[:, 3 * local_width :]
    down_shard = feed_shard[:, 2 * hidden_count : 3 * hidden_count]
    return (
        output,
        grad_inputs,
        grad_text,
        grad_conditioning,
        grad_ada,
        grad_ada_bias,
        first_gain_sum,
        q_gain_sum,
        k_gain_sum,
        ky_gain_sum,
        gate_sum,
        qkv_shard,
        out_shard.T,
        grad_text_kv,
        second_gain_sum,
        gate_up_shard,
        down_shard.T,
    )


def solution(mesh):
    placed = (
        P(("dp", "tensor"), None),
        P("dp"),
        P("dp"),
        P("dp", None),
        P(),
        P("dp", None),
        P(),
        P(),
        P(),
        P(),
        P(),
        P(),
        P(None, "dp", "tensor"),
        P("tensor", "dp"),
        P(None, "dp", "tensor"),
        P(),
        P(None, "dp", "tensor"),
        P("tensor", "dp"),
        P(("dp", "tensor"), None),
    )
    return jax.shard_map(
        shards,
        mesh=mesh,
        in_specs=placed,
        out_specs=(
            P(("dp", "tensor"), None),
            P(("dp", "tensor"), None),
            P("dp", "tensor"),
            P(),
            P("dp", None),
            P(),
            P(),
            P(),
            P(),
            P(),
            P(),
            P(None, "dp", "tensor"),
            P("tensor", "dp"),
            P(None, "dp", "tensor"),
            P(),
            P(None, "dp", "tensor"),
            P("tensor", "dp"),
        ),
        check_vma=False,
    )
```

```python
import functools

import jax
import jax.numpy as jnp
from jax import lax
from jax.experimental import pallas as pl
from jax.experimental.pallas import tpu as pltpu
from jax.sharding import PartitionSpec as P

TXT = 256
GROUP = 8
SPLIT = 4
EPS = 1e-06
MASK = -1e4
FORWARD_SLOTS = 4
LOW = jnp.bfloat16
FLOAT = jnp.float32
MIB = 1024 * 1024
LARGE = pl.CostEstimate(flops=25 * 10**9, bytes_accessed=1024, transcendentals=0)
SMALL = pl.CostEstimate(flops=1024, bytes_accessed=1024, transcendentals=0)


def pick_tile(total, most):
    size = most
    while total % size:
        size //= 2
    return size


def matmul(left, right, left_dim, right_dim):
    return lax.dot_general(
        left, right, (((left_dim,), (right_dim,)), ((), ())), preferred_element_type=jnp.float32
    )


def lane_ids(shape):
    return lax.broadcasted_iota(jnp.int32, shape, len(shape) - 1)


def turn(values):
    return pltpu.roll(values, 64, 1)


def fold_low(values):
    half = values.shape[0] // 2
    top, bottom = values[:half], turn(values)[half:]
    return jnp.where(lane_ids(top.shape) < 64, top, bottom).astype(LOW)


def fold_high(values):
    half = values.shape[0] // 2
    top, bottom = turn(values)[:half], values[half:]
    return jnp.where(lane_ids(top.shape) < 64, top, bottom).astype(LOW)


def unfold_low(packed):
    wide = packed.astype(FLOAT)
    return jnp.concatenate([wide, turn(wide)], axis=0)


def unfold_high(packed):
    wide = packed.astype(FLOAT)
    return jnp.concatenate([turn(wide), wide], axis=0)


def build_pair(pair, features, spot, keys, values):
    lanes = lane_ids(pair.shape)
    rows = pl.ds(spot, pair.shape[0])
    keys[rows, :] = jnp.where(lanes < 64, pair, features)
    values[rows, :] = jnp.where(
        lanes < 64, jnp.where(lanes < 3, 1.0, 0.0).astype(LOW), pair
    )


def build_inputs(head, near_refs, query_ref, qf_ref, kf_ref, tf_ref, queries, keys, values, text_keys, text_values):
    rows = query_ref.shape[0]
    queries[...] = query_ref[...] + qf_ref[...]
    each = pl.cdiv(near_refs[0].shape[0], rows) - 1
    text_rows = (near_refs[0].shape[0] - each * rows) // each
    for index, ref in enumerate(near_refs):
        spot = pl.ds(pl.multiple_of(head * rows, rows), rows)
        build_pair(ref[spot, :], kf_ref[rows * index : rows * index + rows, :], rows * index, keys, values)
        spot = pl.ds(pl.multiple_of(each * rows + head * text_rows, 16), text_rows)
        first = text_rows * index
        build_pair(
            ref[spot, :], tf_ref[first : first + text_rows, :], first, text_keys, text_values
        )


def forward_kernel(near, chunk, last, *refs):
    near_refs, refs = refs[:near], refs[near:]
    query_ref, qf_ref, kf_ref, tf_ref, gate_ref = refs[:5]
    refs = refs[5:]
    if last:
        before_refs, mixed_refs, refs = refs[:2], refs[2 : 2 + SPLIT], refs[2 + SPLIT :]
    outs_ref, stats_ref, queries, keys, values, text_keys, text_values, hold = refs
    build_inputs(
        pl.program_id(0), near_refs, query_ref, qf_ref, kf_ref, tf_ref,
        queries, keys, values, text_keys, text_values,
    )
    rows = queries.shape[0] // SPLIT * FORWARD_SLOTS
    text_chunk = pick_tile(text_keys.shape[0], 384)

    def tile_step(tile, carry):
        spot = pl.ds(pl.multiple_of(tile * rows, rows), rows)
        query = queries[spot, :]

        def attend(key_part, value_part):
            scores = matmul(query, key_part, 1, 1)
            return matmul(jnp.exp(scores).astype(LOW), value_part, 1, 0)

        def step(index, total):
            part = pl.ds(pl.multiple_of(index * chunk, chunk), chunk)
            return total + attend(keys[part, :], values[part, :])

        def text_step(index, total):
            part = pl.ds(pl.multiple_of(index * text_chunk, text_chunk), text_chunk)
            return total + attend(text_keys[part, :], text_values[part, :])

        blank = jnp.zeros((rows, 128), FLOAT)
        own = lax.fori_loop(0, keys.shape[0] // chunk, step, blank)
        cross = lax.fori_loop(0, text_keys.shape[0] // text_chunk, text_step, blank, unroll=True)
        if not last:
            outs_ref[spot, :] = own
            stats_ref[spot, :] = cross
            return carry
        own = own + before_refs[0][spot, :]
        cross = cross + before_refs[1][spot, :]
        own_inverse = 1.0 / own[:, 0:1]
        cross_inverse = 1.0 / cross[:, 0:1]
        own = own * own_inverse
        cross = cross * cross_inverse
        lanes = lane_ids(own.shape)
        mixed = own + gate_ref[0, 0:1, :] * cross
        each = rows // FORWARD_SLOTS
        for slot in range(FORWARD_SLOTS):
            hold[tile * FORWARD_SLOTS + slot] = fold_high(mixed[each * slot : each * slot + each])
        outs_ref[spot, :] = jnp.where(lanes < 64, turn(cross), own)
        stats_ref[spot, :] = jnp.where(lanes == 0, own_inverse, cross_inverse)
        return carry

    lax.fori_loop(0, SPLIT // FORWARD_SLOTS, tile_step, 0)
    if last:
        for index, ref in enumerate(mixed_refs):
            ref[...] = hold[index]


def whole(shape):
    return pl.BlockSpec(shape, lambda i: (0,) * len(shape))


def attention_specs(part, pairs, queries, qf, kf, tf):
    return [whole(value.shape) for value in pairs] + [
        pl.BlockSpec(qf.shape, lambda i: (i, 0)),
        whole(qf.shape),
        pl.BlockSpec((kf.shape[0] // 2, 128), lambda i: (part, 0)),
        pl.BlockSpec((tf.shape[0] // 2, 128), lambda i: (part, 0)),
        pl.BlockSpec((1, 8, 128), lambda i: (i, 0, 0)),
    ]


def attention_scratch(qf, kf, tf):
    keys, text_keys = (kf.shape[0] // 2, 128), (tf.shape[0] // 2, 128)
    return [
        pltpu.VMEM(qf.shape, LOW),
        pltpu.VMEM(keys, LOW),
        pltpu.VMEM(keys, LOW),
        pltpu.VMEM(text_keys, LOW),
        pltpu.VMEM(text_keys, LOW),
    ]


def attention_forward(pairs, queries, qf, kf, tf, gates, before):
    rows = qf.shape[0]
    heads = gates.shape[0]
    half = rows // SPLIT // 2
    folded = jax.ShapeDtypeStruct((heads * half, 128), LOW)
    wide = jax.ShapeDtypeStruct((heads * rows, 128), FLOAT)
    wide_spec = pl.BlockSpec((rows, 128), lambda i: (i, 0))
    last = len(before) > 0
    slots = SPLIT if last else 0
    out = pl.pallas_call(
        functools.partial(forward_kernel, len(pairs), pick_tile(kf.shape[0] // 2, 2048), last),
        grid=(heads,),
        in_specs=attention_specs(int(last), pairs, queries, qf, kf, tf) + [wide_spec] * len(before),
        out_specs=[pl.BlockSpec((half, 128), lambda i: (i, 0))] * slots + [wide_spec] * 2,
        out_shape=[folded] * slots + [wide] * 2,
        scratch_shapes=attention_scratch(qf, kf, tf) + [pltpu.VMEM((SPLIT, half, 128), LOW)],
        compiler_params=pltpu.CompilerParams(vmem_limit_bytes=60 * MIB),
        cost_estimate=LARGE,
    )(*pairs, queries, qf, kf, tf, gates, *before)
    return (out[:slots], out[slots], out[slots + 1]) if last else tuple(out)


def backward_kernel(near, chunk, last, *refs):
    near_refs, refs = refs[:near], refs[near:]
    query_ref, qf_ref, kf_ref, tf_ref, gate_ref = refs[:5]
    refs = refs[5:]
    grad_refs, refs = refs[:SPLIT], refs[SPLIT:]
    outs_ref, stats_ref, refs = refs[0], refs[1], refs[2:]
    if last:
        before_ref, dq_refs, dg_ref, refs = refs[0], refs[1 : 1 + SPLIT], refs[1 + SPLIT], refs[2 + SPLIT :]
    else:
        dq_ref, refs = refs[0], refs[1:]
    dkv_refs, dt_refs = refs[:2], refs[2:4]
    queries, keys, values, text_keys, text_values, hold, grad_hold, acc, text_acc = refs[4:]
    build_inputs(
        pl.program_id(0), near_refs, query_ref, qf_ref, kf_ref, tf_ref,
        queries, keys, values, text_keys, text_values,
    )
    for index, ref in enumerate(grad_refs):
        grad_hold[index] = ref[...]
    if last:
        dg_ref[...] = jnp.zeros_like(dg_ref)
    rows = queries.shape[0]
    text_chunk = pick_tile(text_keys.shape[0], 384)
    gate = gate_ref[0, 0:1, :]

    def tile_step(tile, carry):
        spot = pl.ds(pl.multiple_of(tile * rows, rows), rows)
        query = queries[spot, :]
        lanes = lane_ids(query.shape)
        query_low = jnp.where(lanes < 64, query, jnp.zeros_like(query))
        grads = jnp.concatenate([unfold_high(grad_hold[slot]) for slot in range(SPLIT)], axis=0)
        grads = jnp.where(lanes < 64, 0.0, grads)
        outs = outs_ref[spot, :]
        cross_out = jnp.where(lanes < 64, 0.0, turn(outs))
        if last:
            dg_ref[0] += jnp.sum((grads * cross_out).reshape(rows // 8, 8, 128), axis=0)
        cross_grads = (gate * grads).astype(LOW).astype(FLOAT)

        def widen(grad, out, inverse):
            delta = -jnp.sum(grad * out, axis=1, keepdims=True) * inverse
            first = delta.astype(LOW).astype(FLOAT)
            second = (delta - first).astype(LOW).astype(FLOAT)
            third = delta - first - second
            features = jnp.where(lanes == 0, first, jnp.where(lanes == 1, second, third))
            scaled = grad * inverse
            return jnp.where(lanes < 3, features, scaled).astype(LOW), scaled.astype(LOW)

        stats = stats_ref[spot, :]
        own_wide, own_low = widen(grads, outs, stats[:, 0:1])
        cross_wide, cross_low = widen(cross_grads, cross_out, stats[:, 1:2])
        own_pair = jnp.concatenate([query_low, own_low], axis=0)
        cross_pair = jnp.concatenate([query_low, cross_low], axis=0)

        def attend(key_part, value_part, wide, pair):
            weights = jnp.exp(matmul(key_part, query, 1, 1))
            grad_scores = (weights * matmul(value_part, wide, 1, 1)).astype(LOW)
            low = weights.astype(LOW)
            grad_pair = matmul(jnp.concatenate([grad_scores, low], axis=1), pair, 1, 0)
            return grad_pair, matmul(grad_scores, key_part, 0, 0)

        def step(index, total):
            part = pl.ds(pl.multiple_of(index * chunk, chunk), chunk)
            grad_pair, grad_query = attend(keys[part, :], values[part, :], own_wide, own_pair)
            acc[part, :] = grad_pair
            return total + grad_query

        def text_step(index, total):
            part = pl.ds(pl.multiple_of(index * text_chunk, text_chunk), text_chunk)
            grad_pair, grad_query = attend(
                text_keys[part, :], text_values[part, :], cross_wide, cross_pair
            )
            text_acc[part, :] = grad_pair
            return total + grad_query

        blank = jnp.zeros((rows, 128), FLOAT)
        total = lax.fori_loop(0, keys.shape[0] // chunk, step, blank, unroll=4)
        total = lax.fori_loop(0, text_keys.shape[0] // text_chunk, text_step, total, unroll=True)
        if not last:
            dq_ref[spot, :] = total
            return carry
        total = (total + before_ref[spot, :]) * 0.125
        each = rows // SPLIT
        for slot in range(SPLIT):
            hold[slot] = fold_low(total[each * slot : each * slot + each])
        return carry

    lax.fori_loop(0, 1, tile_step, 0)
    if last:
        for index, ref in enumerate(dq_refs):
            ref[...] = hold[index]
    for values, refs in ((acc, dkv_refs), (text_acc, dt_refs)):
        size = refs[0].shape[1]
        refs[0][0] = values[:size, :].astype(LOW)
        refs[1][0] = values[size:, :].astype(LOW)


def attention_backward(pairs, queries, qf, kf, tf, gates, grads, outs, stats, before):
    rows = qf.shape[0]
    heads = gates.shape[0]
    half = rows // SPLIT // 2
    last = len(before) > 0
    folded = jax.ShapeDtypeStruct((heads * half, 128), LOW)
    piece = jax.ShapeDtypeStruct((heads, kf.shape[0] // 4, 128), LOW)
    text = jax.ShapeDtypeStruct((heads, tf.shape[0] // 4, 128), LOW)
    sums = jax.ShapeDtypeStruct((heads, 8, 128), FLOAT)
    wide = jax.ShapeDtypeStruct((heads * rows, 128), FLOAT)
    wide_spec = pl.BlockSpec((rows, 128), lambda i: (i, 0))
    folded_spec = pl.BlockSpec((half, 128), lambda i: (i, 0))
    split = [piece, piece, text, text]

    def split_spec(value):
        return pl.BlockSpec((1,) + value.shape[1:], lambda i: (i, 0, 0))

    first_shapes = [folded] * SPLIT + [sums] if last else [wide]
    first_specs = [folded_spec] * SPLIT + [split_spec(sums)] if last else [wide_spec]
    out = pl.pallas_call(
        functools.partial(backward_kernel, len(pairs), pick_tile(kf.shape[0] // 2, 2048), last),
        grid=(heads,),
        in_specs=attention_specs(int(not last), pairs, queries, qf, kf, tf)
        + [folded_spec] * SPLIT
        + [wide_spec] * (2 + len(before)),
        out_specs=first_specs + [split_spec(value) for value in split],
        out_shape=first_shapes + split,
        scratch_shapes=attention_scratch(qf, kf, tf)
        + [
            pltpu.VMEM((SPLIT, half, 128), LOW),
            pltpu.VMEM((SPLIT, half, 128), LOW),
            pltpu.VMEM((kf.shape[0] // 2, 128), FLOAT),
            pltpu.VMEM((tf.shape[0] // 2, 128), FLOAT),
        ],
        compiler_params=pltpu.CompilerParams(vmem_limit_bytes=60 * MIB),
        cost_estimate=LARGE,
    )(*pairs, queries, qf, kf, tf, gates, *grads, outs, stats, *before)
    return out[: len(first_shapes)], out[len(first_shapes) :]


def half_means(values, lanes):
    low = jnp.sum(jnp.where(lanes < 64, values, 0.0), axis=1, keepdims=True)
    high = jnp.sum(jnp.where(lanes < 64, 0.0, values), axis=1, keepdims=True)
    return jnp.where(lanes < 64, low, high) * (1.0 / 64.0)


def swap_halves(values, lanes):
    return jnp.where(
        lax.rem(lanes, 64) < 32, pltpu.roll(values, 96, 1), pltpu.roll(values, 32, 1)
    )


def placed_at(groups, head, upper):
    values = groups[head // 2]
    return values if (head % 2 == 1) == upper else turn(values)


def rope_forward_kernel(heads, far_ref, qkv_ref, cos_ref, sin_ref, gains_ref, *refs):
    outs, hold = refs[:-1], refs[-1]
    width = heads * 64
    each = heads // SPLIT
    rows = qkv_ref.shape[0]
    cosine, sine = cos_ref[...], sin_ref[...]
    lanes = lane_ids(cosine.shape)

    def turned(start, gain):
        groups = []
        for index in range(heads // 2):
            raw = qkv_ref[:, start + 128 * index : start + 128 * index + 128]
            normed = raw * lax.rsqrt(half_means(raw * raw, lanes) + EPS) * gain
            groups.append(normed * cosine + swap_halves(normed, lanes) * sine)
        return groups

    queries = turned(0, gains_ref[0:1, :])
    keys = turned(width, gains_ref[1:2, :])
    values = [
        qkv_ref[:, 2 * width + 128 * index : 2 * width + 128 * index + 128]
        for index in range(heads // 2)
    ]
    for head in range(heads):
        group, index = head // each, head % each
        slot = lax.rem(group - far_ref[0] + SPLIT, SPLIT)
        pair = jnp.where(
            lanes < 64, placed_at(keys, head, False), placed_at(values, head, True)
        )
        hold[slot, index, :rows, :] = pair.astype(LOW)
        hold[slot, index, rows:, :] = fold_low(placed_at(queries, head, False))
    size = rows * 3 // 2
    for slot in range(SPLIT):
        for index in range(each):
            outs[slot][size * index : size * index + size, :] = hold[slot, index]


def small_call(kernel, operands, shapes, scratch):
    out = pl.pallas_call(
        kernel,
        in_specs=[pl.BlockSpec(memory_space=pltpu.SMEM)]
        + [pl.BlockSpec(memory_space=pltpu.VMEM)] * (len(operands) - 1),
        out_specs=[pl.BlockSpec(memory_space=pltpu.VMEM)] * len(shapes),
        out_shape=shapes,
        scratch_shapes=scratch,
        compiler_params=pltpu.CompilerParams(vmem_limit_bytes=32 * MIB),
        cost_estimate=SMALL,
    )(*operands)
    return out


def rope_forward(far, qkv, cosine, sine, gains, heads):
    rows = qkv.shape[0] * 3 // 2
    each = heads // SPLIT
    out = small_call(
        functools.partial(rope_forward_kernel, heads),
        (far, qkv, cosine, sine, gains),
        [jax.ShapeDtypeStruct((each * rows, 128), LOW)] * SPLIT,
        [pltpu.VMEM((SPLIT, each, rows, 128), LOW)],
    )
    return list(out)


def rope_backward_kernel(heads, far_ref, *refs):
    parts, refs = refs[:SPLIT], refs[SPLIT:]
    qkv_ref, cos_ref, sin_ref, gains_ref, out_ref, sums_ref, hold = refs
    width = heads * 64
    each = heads // SPLIT
    rows = qkv_ref.shape[0]
    for slot in range(SPLIT):
        group = lax.rem(far_ref[0] + slot, SPLIT)
        size = hold.shape[2]
        for index in range(each):
            hold[group, index] = parts[slot][size * index : size * index + size, :]
    cosine, sine = cos_ref[...], sin_ref[...]
    lanes = lane_ids(cosine.shape)

    def found(kind, head):
        group, index, upper = head // each, head % each, head % 2 == 1
        if kind == 0:
            packed = hold[group, index, rows:, :]
            return unfold_high(packed) if upper else unfold_low(packed)
        values = hold[group, index, :rows, :].astype(FLOAT)
        return values if upper == (kind == 2) else turn(values)

    def joined(kind, index):
        return jnp.where(lanes < 64, found(kind, 2 * index), found(kind, 2 * index + 1))

    for kind in range(2):
        gain = gains_ref[kind : kind + 1, :]
        total = jnp.zeros((1, 128), FLOAT)
        for index in range(heads // 2):
            spot = kind * width + 128 * index
            raw = qkv_ref[:, spot : spot + 128]
            inverse = lax.rsqrt(half_means(raw * raw, lanes) + EPS)
            unit = raw * inverse
            grad = joined(kind, index)
            back = grad * cosine - swap_halves(grad, lanes) * sine
            total = total + jnp.sum(back * unit, axis=0, keepdims=True)
            scaled = back * gain
            raw_grad = inverse * (scaled - unit * half_means(scaled * unit, lanes))
            out_ref[:, spot : spot + 128] = raw_grad.astype(LOW)
        sums_ref[kind : kind + 1, :] = total
    sums_ref[2:8, :] = jnp.zeros((6, 128), FLOAT)
    for index in range(heads // 2):
        spot = 2 * width + 128 * index
        out_ref[:, spot : spot + 128] = joined(2, index).astype(LOW)


def rope_backward(far, parts, qkv, cosine, sine, gains, heads):
    each = heads // SPLIT
    return small_call(
        functools.partial(rope_backward_kernel, heads),
        (far, *parts, qkv, cosine, sine, gains),
        [jax.ShapeDtypeStruct(qkv.shape, LOW), jax.ShapeDtypeStruct((8, 128), FLOAT)],
        [pltpu.VMEM((SPLIT, each, parts[0].shape[0] // each, 128), LOW)],
    )


def join_kernel(heads, far_ref, *refs):
    parts, out_ref, hold = refs[:SPLIT], refs[SPLIT], refs[SPLIT + 1]
    each = heads // SPLIT
    half = hold.shape[2]
    for slot in range(SPLIT):
        group = lax.rem(far_ref[0] + slot, SPLIT)
        for index in range(each):
            hold[group, index] = parts[slot][half * index : half * index + half, :]
    for pair in range(heads // 2):
        low = unfold_low(hold[2 * pair // each, 2 * pair % each])
        high = unfold_high(hold[(2 * pair + 1) // each, (2 * pair + 1) % each])
        out_ref[:, 128 * pair : 128 * pair + 128] = jnp.where(
            lane_ids(low.shape) < 64, low, high
        ).astype(LOW)


def join_heads(far, parts, heads):
    each = heads // SPLIT
    half = parts[0].shape[0] // each
    return small_call(
        functools.partial(join_kernel, heads),
        (far, *parts),
        [jax.ShapeDtypeStruct((2 * half, heads * 64), LOW)],
        [pltpu.VMEM((SPLIT, each, half, 128), LOW)],
    )[0]


def split_kernel(heads, far_ref, grad_ref, *refs):
    outs, hold = refs[:-1], refs[-1]
    each = heads // SPLIT
    half = hold.shape[2]
    for head in range(heads):
        group, index = head // each, head % each
        slot = lax.rem(group - far_ref[0] + SPLIT, SPLIT)
        values = grad_ref[:, 128 * (head // 2) : 128 * (head // 2) + 128]
        hold[slot, index] = fold_high(values) if head % 2 else fold_low(values)
    for slot in range(SPLIT):
        for index in range(each):
            outs[slot][half * index : half * index + half, :] = hold[slot, index]


def split_heads(far, grads, heads):
    each = heads // SPLIT
    half = grads.shape[0] // 2
    return small_call(
        functools.partial(split_kernel, heads),
        (far, grads),
        [jax.ShapeDtypeStruct((each * half, 128), LOW)] * SPLIT,
        [pltpu.VMEM((SPLIT, each, half, 128), LOW)],
    )


def local_call(kernel, operands, shapes):
    return pl.pallas_call(
        kernel,
        out_shape=shapes,
        compiler_params=pltpu.CompilerParams(vmem_limit_bytes=40 * MIB),
        cost_estimate=SMALL,
    )(*operands)


def gather_kernel(each, *refs):
    slots, text_ref, pairs_ref, queries_ref = refs[:SPLIT], refs[SPLIT], refs[-2], refs[-1]
    size = slots[0].shape[0] // each
    rows = size * 2 // 3
    for head in range(each):
        for index, slot in enumerate(slots):
            spot = (head * SPLIT + index) * rows
            first = head * size
            pairs_ref[spot : spot + rows, :] = slot[first : first + rows, :]
            query = unfold_low(slot[first + rows : first + size, :])
            query = jnp.where(lane_ids(query.shape) < 64, query * 0.125, 0.0)
            queries_ref[spot : spot + rows, :] = query.astype(LOW)
    pairs_ref[each * SPLIT * rows :, :] = text_ref[...]


def gather_slots(slots, text, each):
    rows = slots[0].shape[0] * 2 // 3 * SPLIT
    return local_call(
        functools.partial(gather_kernel, each),
        (*slots, text),
        [
            jax.ShapeDtypeStruct((rows + text.shape[0], 128), LOW),
            jax.ShapeDtypeStruct((rows, 128), LOW),
        ],
    )


def pack_kernel(terms, *refs):
    inputs, folded, outs = refs[:terms], refs[terms : terms + SPLIT], refs[terms + SPLIT :]
    each = inputs[0].shape[0]
    size = outs[0].shape[0] // each
    rows = size * 2 // 3
    half = size - rows
    for head in range(each):
        for slot in range(SPLIT):
            total = sum(
                term[head, rows * slot : rows * slot + rows, :].astype(FLOAT) for term in inputs
            )
            spot = size * head
            outs[slot][spot : spot + rows, :] = total.astype(LOW)
            outs[slot][spot + rows : spot + size, :] = folded[slot][
                half * head : half * head + half, :
            ]


def pack_slots(terms, folded):
    return local_call(
        functools.partial(pack_kernel, len(terms)),
        (*terms, *folded),
        [jax.ShapeDtypeStruct((3 * folded[0].shape[0], 128), LOW)] * SPLIT,
    )


def text_split_kernel(far_ref, text_ref, *outs):
    size = outs[0].shape[1]
    for slot in range(SPLIT):
        group = lax.rem(far_ref[0] + slot, SPLIT)
        spot = pl.ds(pl.multiple_of(group * size, 128), size)
        outs[slot][...] = text_ref[:, spot].astype(LOW)


def text_join_kernel(far_ref, *refs):
    parts, out_ref = refs[:SPLIT], refs[SPLIT]
    size = parts[0].shape[1]
    for slot in range(SPLIT):
        group = lax.rem(far_ref[0] + slot, SPLIT)
        out_ref[:, pl.ds(pl.multiple_of(group * size, 128), size)] = parts[slot][...]


def low_means(values, lanes):
    return jnp.sum(jnp.where(lanes < 64, values, 0.0), axis=1, keepdims=True) * (1.0 / 64.0)


def text_norm_kernel(*refs):
    parts, gain_ref, raw_ref, out_ref = refs[:SPLIT], refs[SPLIT], refs[-2], refs[-1]
    rows = raw_ref.shape[0]
    raw = sum(part[...].astype(FLOAT) for part in parts)
    raw_ref[...] = raw
    for head in range(raw.shape[1] // 128):
        values = raw[:, 128 * head : 128 * head + 128]
        lanes = lane_ids(values.shape)
        normed = values * lax.rsqrt(low_means(values * values, lanes) + EPS) * gain_ref[0:1, :]
        out_ref[rows * head : rows * head + rows, :] = jnp.where(
            lanes < 64, normed, values
        ).astype(LOW)


def text_back_kernel(terms, *refs):
    inputs, refs = refs[:terms], refs[terms:]
    raw_ref, gain_ref, out_ref, sums_ref = refs
    rows = raw_ref.shape[0]
    total_gain = jnp.zeros((1, 128), FLOAT)
    for head in range(inputs[0].shape[0]):
        grad = sum(term[head, :rows, :].astype(FLOAT) for term in inputs)
        grad = grad.astype(LOW).astype(FLOAT)
        raw = raw_ref[:, 128 * head : 128 * head + 128]
        lanes = lane_ids(raw.shape)
        inverse = lax.rsqrt(low_means(raw * raw, lanes) + EPS)
        unit = raw * inverse
        total_gain = total_gain + jnp.sum(grad * unit, axis=0, keepdims=True)
        scaled = grad * gain_ref[0:1, :]
        back = inverse * (scaled - unit * low_means(scaled * unit, lanes))
        out_ref[:, 128 * head : 128 * head + 128] = jnp.where(lanes < 64, back, grad).astype(LOW)
    sums_ref[...] = jnp.broadcast_to(total_gain, sums_ref.shape)


def tie(*values):
    return lax.optimization_barrier(values)


def outer_kernel(bound, *refs):
    first, second, out_ref = refs[:4], refs[4:8], refs[8]
    step = pl.program_id(0)

    def run(group):
        own_left, other_left, own_right, other_right = group
        out_ref[...] = (
            matmul(own_left[...], own_right[0], 1, 0)
            + matmul(other_left[...], other_right[0], 1, 0)
        ).astype(LOW)

    @pl.when(step < bound)
    def _():
        run(first)

    @pl.when(step >= bound)
    def _():
        run(second)


def outer_products(first, second, tile):
    depth = first[0].shape[0]
    steps = [group[2].shape[0] * group[2].shape[2] // tile for group in (first, second)]
    specs, operands = [], []
    for index, group in enumerate((first, second)):
        rows, columns = group[2].shape[1:]
        tiles = columns // tile

        def right_at(i, index=index, tiles=tiles):
            if index == 0:
                at = jnp.minimum(i, steps[0] - 1)
            else:
                at = jnp.maximum(i - steps[0], 0)
            return (at // tiles, 0, at % tiles)

        specs += [whole(group[0].shape)] * 2
        specs += [pl.BlockSpec((1, rows, tile), right_at)] * 2
        operands += group
    return pl.pallas_call(
        functools.partial(outer_kernel, steps[0]),
        grid=(sum(steps),),
        in_specs=specs,
        out_specs=pl.BlockSpec((depth, tile), lambda i: (0, i)),
        out_shape=jax.ShapeDtypeStruct((depth, sum(steps) * tile), LOW),
        compiler_params=pltpu.CompilerParams(vmem_limit_bytes=48 * MIB),
        cost_estimate=SMALL,
    )(*operands)


def columns_kernel(order, core_ref, values_ref, own_ref, other_ref, hold):
    turned = jnp.transpose(values_ref[...].astype(FLOAT))
    hold[...] = turned.reshape(hold.shape)
    core = core_ref[0]
    own_ref[...] = jnp.concatenate(
        [hold[2 * pair + core] for pair in order], axis=0
    ).astype(LOW)
    other_ref[...] = jnp.concatenate(
        [hold[2 * pair + 1 - core] for pair in order], axis=0
    ).astype(LOW)


def split_columns(core, values, block, order):
    rows, width = values.shape
    half = jax.ShapeDtypeStruct((width // 2, rows), LOW)
    return small_call(
        functools.partial(columns_kernel, order),
        (core, values),
        [half, half],
        [pltpu.VMEM((width // block, block, rows), FLOAT)],
    )


def feed_kernel(
    normed_ref, grad_ref, gate_ref, up_ref, down_ref,
    hidden_ref, grads_ref, feed_own_ref, feed_other_ref, norm_own_ref, norm_other_ref,
    feed_acc, norm_acc,
):
    step = pl.program_id(0)

    @pl.when(step == 0)
    def _():
        feed_acc[...] = jnp.zeros_like(feed_acc)
        norm_acc[...] = jnp.zeros_like(norm_acc)

    normed = normed_ref[...]
    gate = matmul(normed, gate_ref[...], 1, 0)
    up = matmul(normed, up_ref[...], 1, 0)
    grad_hidden = matmul(grad_ref[...], down_ref[...], 1, 0)
    sigmoid = 1.0 / (1.0 + jnp.exp(-gate))
    silu = gate * sigmoid
    hidden = (silu * up).astype(LOW)
    grad_gate = (grad_hidden * up * sigmoid * (1.0 + gate * (1.0 - sigmoid))).astype(LOW)
    grad_up = (grad_hidden * silu).astype(LOW)
    hidden_ref[0] = hidden
    grads_ref[0] = grad_gate
    grads_ref[1] = grad_up
    feed_acc[...] += matmul(hidden, down_ref[...], 1, 1)
    norm_acc[...] += matmul(grad_gate, gate_ref[...], 1, 1) + matmul(grad_up, up_ref[...], 1, 1)

    @pl.when(step == pl.num_programs(0) - 1)
    def _():
        half = feed_own_ref.shape[0]
        feed_own_ref[...] = feed_acc[:half, :]
        feed_other_ref[...] = feed_acc[half:, :].astype(LOW)
        norm_own_ref[...] = norm_acc[:half, :]
        norm_other_ref[...] = norm_acc[half:, :].astype(LOW)


def feed_forward(normed, grads, weights, columns, tile):
    rows, width = normed.shape
    tiles = columns // tile
    own = jax.ShapeDtypeStruct((rows // 2, width), FLOAT)
    other = jax.ShapeDtypeStruct((rows // 2, width), LOW)
    return pl.pallas_call(
        feed_kernel,
        grid=(tiles,),
        in_specs=[whole(normed.shape), whole(grads.shape)]
        + [
            pl.BlockSpec((width, tile), lambda i, part=part: (0, part * tiles + i))
            for part in range(3)
        ],
        out_specs=[
            pl.BlockSpec((1, rows, tile), lambda i: (0, 0, i)),
            pl.BlockSpec((2, rows, tile), lambda i: (0, 0, i)),
        ]
        + [whole(own.shape)] * 4,
        out_shape=[
            jax.ShapeDtypeStruct((1, rows, columns), LOW),
            jax.ShapeDtypeStruct((2, rows, columns), LOW),
            own,
            other,
            own,
            other,
        ],
        scratch_shapes=[pltpu.VMEM((rows, width), FLOAT)] * 2,
        compiler_params=pltpu.CompilerParams(vmem_limit_bytes=48 * MIB),
        cost_estimate=SMALL,
    )(normed, grads, weights, weights, weights)


def dot_float(left, right):
    return jnp.dot(left, right, preferred_element_type=FLOAT)


def dot_turned(left, right):
    return matmul(left, right, 1, 1)


def norm_rows(values, gains):
    return values * lax.rsqrt(jnp.mean(values * values, axis=-1, keepdims=True) + EPS) * gains


def modulated(values, gains, shifts, scales):
    return norm_rows(values, gains) * (1.0 + scales) + shifts


def swapped(values):
    return lax.ppermute(values, "tensor", [(0, 1), (1, 0)])


def both_rows(values):
    return jnp.concatenate([values, swapped(values)], axis=0)


def own_rows(partial):
    rows = partial.shape[0] // 2
    return partial[:rows] + swapped(partial[rows:].astype(LOW)).astype(FLOAT)


def shards(
    inputs,
    clip_ids,
    positions,
    text_tokens,
    conditioning,
    ada_weight,
    ada_bias,
    first_norm_gain,
    query_gain,
    key_gain,
    text_key_gain,
    head_gate,
    qkv_weight,
    out_weight,
    text_kv_weight,
    second_norm_gain,
    gate_up_weight,
    down_weight,
    grad_output,
):
    dp = lax.axis_size("dp")
    near = dp // SPLIT
    bits = [near >> (step + 1) for step in range(near.bit_length() - 1)]
    tensor_index = lax.axis_index("tensor")
    dp_index = lax.axis_index("dp")
    far_index, near_index = dp_index // near, dp_index % near
    row_count, width = inputs.shape
    token_count = clip_ids.shape[0]
    head_size = query_gain.shape[0]
    local_width = qkv_weight.shape[2]
    heads = local_width // head_size
    each = heads // SPLIT
    part_width = each * head_size
    clip_count = conditioning.shape[0]
    hidden_count = gate_up_weight.shape[2]
    weight_rows = qkv_weight.shape[1]

    def flip(values, bit):
        return lax.ppermute(values, "dp", [(j, j ^ bit) for j in range(dp)])

    def shift(values, steps):
        pairs = [(j, ((j // near + steps) % SPLIT) * near + j % near) for j in range(dp)]
        return lax.ppermute(values, "dp", pairs)

    def sum_dp(values):
        step = 1
        while step < dp:
            values = values + flip(values, step)
            step *= 2
        return values

    def spread(values):
        for bit in bits:
            values = jnp.concatenate([values, flip(values, bit)], axis=0)
        return values

    def spread_list(values):
        values = [values]
        for bit in bits[1:]:
            values = values + [flip(value, bit) for value in values]
        return values

    def collect(values):
        for bit in reversed(bits):
            half = values.shape[0] // 2
            values = values[:half].astype(FLOAT) + flip(
                values[half:].astype(LOW), bit
            ).astype(FLOAT)
        return values

    def pick(stacked, index):
        return lax.dynamic_index_in_dim(stacked, index, 0, keepdims=False)

    def send_parts(stacked):
        out = [pick(stacked, far_index)]
        for steps in range(1, SPLIT):
            out.append(shift(pick(stacked, (far_index + steps) % SPLIT), steps))
        return out

    def send_slots(slots):
        return [slots[0]] + [shift(slots[steps], steps) for steps in range(1, SPLIT)]

    def return_slots(slots):
        return [slots[0]] + [shift(slots[steps], -steps) for steps in range(1, SPLIT)]

    flips = []
    for order in range(near):
        mask = 0
        for place, bit in enumerate(bits):
            if order >> place & 1:
                mask |= bit
        flips.append(mask)

    core = dp_index % 2
    pair_order = []
    for column in range(near // 2):
        line = [group * (near // 2) + column for group in range(SPLIT)]
        pair_order += line if column % 2 == 0 else line[::-1]
    core_groups = [[2 * pair + first for pair in pair_order] for first in range(2)]

    core_at = core.astype(jnp.int32).reshape(1)

    def core_columns(values):
        own, other = split_columns(core_at, values, weight_rows, pair_order)
        return own, flip(other, 1)

    def scatter(values):
        return lax.psum_scatter(
            values, "dp", scatter_dimension=0, axis_index_groups=core_groups, tiled=True
        )

    qkv_full = lax.all_gather(
        qkv_weight.transpose(1, 0, 2).reshape(weight_rows, 3 * local_width),
        "dp",
        axis=0,
        tiled=True,
    )
    cond_float = conditioning.astype(FLOAT)
    silu_cond = jax.nn.silu(cond_float).astype(LOW)
    cond_rows = ada_weight.shape[0]
    silu_slice = lax.dynamic_slice_in_dim(silu_cond, dp_index * cond_rows, cond_rows, axis=1)
    first_rows = jnp.sum((clip_ids == 0).astype(FLOAT))
    spots = jnp.arange(ada_weight.shape[1], dtype=jnp.int32)
    early = 2 * width
    early_part = jnp.concatenate(
        [
            dot_float(silu_slice, ada_weight[:, :early]),
            jnp.where(spots[:early] == dp_index, first_rows, 0.0)[None],
        ],
        axis=0,
    )
    text_columns = lax.all_to_all(text_tokens, "dp", split_axis=1, concat_axis=0, tiled=True)
    early_part, text_columns = tie(early_part, text_columns)
    early_sum = sum_dp(early_part)
    bias = ada_bias.astype(FLOAT)
    early_mod = early_sum[:clip_count] + bias[:early]
    counts = early_sum[clip_count, :dp].astype(jnp.int32)

    own_ids = lax.dynamic_slice_in_dim(clip_ids, tensor_index * row_count, row_count)
    row_positions = jnp.where(
        tensor_index == 0, positions, jnp.roll(positions, row_count)
    )
    other_clip = jnp.max(clip_ids)
    first_clip = (own_ids == 0)[:, None]

    def mod_blocks(modulation):
        rows = jnp.where(
            first_clip,
            modulation[0:1],
            lax.dynamic_slice_in_dim(modulation, other_clip, 1, 0),
        )
        return jnp.split(rows, rows.shape[1] // width, axis=1)

    shift_one, scale_one = mod_blocks(early_mod)
    input_rows = inputs.astype(FLOAT)
    first_gain = first_norm_gain.astype(FLOAT)
    normed_one = modulated(input_rows, first_gain, shift_one, scale_one).astype(LOW)
    normed_all = both_rows(normed_one)
    late_sum = sum_dp(dot_float(silu_slice, ada_weight[:, early:]))

    half_size = head_size // 2
    frequency = 10000.0 ** (-(jnp.arange(half_size, dtype=FLOAT) * 2.0 / head_size))
    angles = row_positions.astype(FLOAT)[:, None] * frequency[None, :]
    cosine = jnp.cos(angles)
    sine = jnp.sin(angles)
    cosine = jnp.concatenate([cosine] * 4, axis=1)
    sine = jnp.concatenate([-sine, sine, -sine, sine], axis=1)
    gains = jnp.stack([jnp.tile(query_gain, 2), jnp.tile(key_gain, 2)]).astype(FLOAT)
    gains = jnp.concatenate([gains, jnp.zeros((6, 128), FLOAT)], axis=0)

    text_rows = text_tokens.shape[0]
    group_rows = text_rows * SPLIT
    text_groups = text_columns.reshape(near, group_rows, text_columns.shape[1])
    text_near = jnp.concatenate([pick(text_groups, near_index ^ mask) for mask in flips], axis=0)
    text_weight = (
        text_kv_weight.reshape(2, -1, SPLIT, each, head_size)
        .transpose(1, 2, 3, 0, 4)
        .reshape(-1, 2 * local_width)
    )
    far = far_index.astype(jnp.int32).reshape(1)
    text_sum = collect(dot_float(text_near, text_weight))
    part_shape = jax.ShapeDtypeStruct((group_rows, 2 * part_width), LOW)
    text_parts = small_call(text_split_kernel, (far, text_sum), [part_shape] * SPLIT, [])
    ky_gain = jnp.concatenate([text_key_gain.astype(FLOAT), jnp.zeros((128 - head_size,), FLOAT)])
    ky_gain = jnp.broadcast_to(ky_gain[None], (8, 128))

    lanes = jnp.arange(128, dtype=jnp.int32)[None, :]
    ordered = flips[0::2] + flips[1::2]
    text_groups_at = jnp.stack([near_index ^ mask for mask in ordered])
    text_clip = (
        text_groups_at[:, None] * group_rows + jnp.arange(group_rows, dtype=jnp.int32)[None, :]
    ).reshape(-1) // TXT
    text_features = (lanes == 64 + text_clip[:, None]).astype(LOW)
    block_at = jnp.stack(
        [
            ((far_index - steps) % SPLIT) * near + (near_index ^ mask)
            for mask in ordered
            for steps in range(SPLIT)
        ]
    )
    block_count = jnp.sum(
        jnp.where(block_at[:, None] == jnp.arange(dp, dtype=jnp.int32)[None, :], counts[None, :], 0),
        axis=1,
    )
    row_at = (jnp.arange(token_count, dtype=jnp.int32) + tensor_index * row_count) % token_count
    key_clip = jnp.where(
        row_at[None, :] < block_count[:, None], 0, 1 + block_at[:, None] // GROUP
    ).reshape(-1)
    key_features = (lanes == 64 + key_clip[:, None]).astype(LOW)
    group_tokens = SPLIT * token_count
    query_clip = key_clip[:group_tokens, None]
    query_features = jnp.where(
        (lanes >= 64) & (lanes < 64 + clip_count) & (lanes != 64 + query_clip), MASK, 0.0
    ).astype(LOW)
    gate_heads = jnp.tanh(
        lax.dynamic_slice_in_dim(
            head_gate.astype(FLOAT), tensor_index * heads + far_index * each, each
        )
    )
    gate_lanes = jnp.broadcast_to(gate_heads[:, None, None], (each, 8, 128))

    rest_weights, qkv_full, normed_all, text_parts, late_sum, key_features, query_features = tie(
        jnp.concatenate(
            [gate_up_weight[0], gate_up_weight[1], down_weight.T, out_weight.T], axis=1
        ),
        qkv_full,
        normed_all,
        text_parts,
        late_sum,
        key_features,
        query_features,
    )
    rest_full = lax.all_gather(rest_weights, "dp", axis=0, tiled=True)
    out_full = rest_full[:, 3 * hidden_count :]
    text_arrived = send_slots(text_parts)
    qkv_raw = dot_float(normed_all, qkv_full)
    head_slots = rope_forward(far, qkv_raw, cosine, sine, gains, heads)
    gate_one, shift_two, scale_two, gate_two = mod_blocks(late_sum + bias[early:])
    grad_two = grad_output.astype(FLOAT)
    grad_ffn = both_rows((gate_two * grad_two).astype(LOW))
    head_slots, text_arrived = tie(head_slots, text_arrived)
    text_raw, text_pairs = local_call(
        text_norm_kernel,
        (*text_arrived, ky_gain),
        [
            jax.ShapeDtypeStruct((group_rows, 2 * part_width), FLOAT),
            jax.ShapeDtypeStruct((each * group_rows, 128), LOW),
        ],
    )
    arrived = send_slots(head_slots)
    arrived, grad_ffn = tie(arrived, grad_ffn)
    own_pairs, queries = gather_slots(arrived, text_pairs, each)
    far_pairs = flip(own_pairs, bits[0])
    near_keys = spread_list(own_pairs)
    shared = (queries, query_features, key_features, text_features, gate_lanes)
    partial_sums = attention_forward(near_keys, *shared, ())
    far_pairs, partial_sums = tie(far_pairs, partial_sums)
    far_keys = spread_list(far_pairs)
    mixed_slots, head_outs, head_stats = attention_forward(far_keys, *shared, partial_sums)
    mixed = join_heads(far, return_slots(mixed_slots), heads)
    attn_rows = own_rows(dot_turned(mixed, out_full))
    after_attn = input_rows + gate_one * attn_rows
    second_gain = second_norm_gain.astype(FLOAT)
    normed_two_all = both_rows(modulated(after_attn, second_gain, shift_two, scale_two).astype(LOW))
    hidden_low, feed_grads, feed_own, feed_other, norm_own, norm_other = feed_forward(
        normed_two_all, grad_ffn, rest_full, hidden_count, 512
    )
    feed_weights_grad = outer_products(
        [*core_columns(normed_two_all), feed_grads, flip(feed_grads, 1)],
        [*core_columns(grad_ffn), hidden_low, flip(hidden_low, 1)],
        512,
    )
    norm_other = swapped(norm_other)
    grad_normed_two = norm_own + norm_other.astype(FLOAT)
    _, pull_two = jax.vjp(modulated, after_attn, second_gain, shift_two, scale_two)
    back_two, grad_second_gain, grad_shift_two, grad_scale_two = pull_two(grad_normed_two)
    grad_after = grad_two + back_two
    grad_attn, feed_other = tie(both_rows((gate_one * grad_after).astype(LOW)), feed_other)
    ffn_rows = feed_own + swapped(feed_other).astype(FLOAT)
    output = (after_attn + gate_two * ffn_rows).astype(LOW)
    grad_gate_two = grad_two * ffn_rows
    grad_gate_one = grad_after * attn_rows
    grad_slots = send_slots(split_heads(far, dot_float(grad_attn, out_full), heads))
    normed_core = core_columns(normed_all)
    last_left = [normed_core, core_columns(grad_attn)]
    mixed_right = mixed[None]
    mixed_other = flip(mixed_right, 1)
    grad_slots, feed_weights_grad, last_left, mixed_other = tie(
        grad_slots, feed_weights_grad, last_left, mixed_other
    )
    feed_low = scatter(feed_weights_grad)

    def total_rows(terms, first, last):
        return sum(term[:, first:last].astype(FLOAT) for term in terms).astype(LOW)

    def start_sums(keep, send, text_keep, text_send):
        return (
            [keep, flip(send, bits[-1])],
            [text_keep, flip(text_send, bits[-1])],
        )

    def next_send(state):
        terms, text_terms = state
        size, text_size = terms[-1].shape[1], text_terms[-1].shape[1]
        return jnp.concatenate(
            [
                total_rows(terms, size // 2, size),
                total_rows(text_terms, text_size // 2, text_size),
            ],
            axis=1,
        )

    def next_state(state, sent, bit):
        terms, text_terms = state
        size = terms[-1].shape[1] // 2
        other = flip(sent, bit)
        return terms + [other[:, :size]], text_terms + [other[:, size:]]

    def reduce_near(pieces):
        state = start_sums(*pieces)
        for bit in reversed(bits[1:-1]):
            state = next_state(state, next_send(state), bit)
        return state

    saved = (head_outs, head_stats)
    query_part, far_pieces = attention_backward(far_keys, *shared, grad_slots, *saved, ())
    far_terms, far_text = reduce_near(far_pieces)
    sent = jnp.concatenate(
        [
            total_rows(far_terms, 0, group_tokens),
            total_rows(far_text, 0, group_rows),
        ],
        axis=1,
    )
    grad_slots, sent = tie(grad_slots, sent)
    came = flip(sent, bits[0])
    (*folded, gate_parts), own_pieces = attention_backward(
        near_keys, *shared, grad_slots, *saved, query_part
    )
    pair_terms, text_terms = reduce_near(own_pieces)
    pair_terms = pair_terms + [came[:, :group_tokens]]
    text_terms = text_terms + [came[:, group_tokens:]]
    back_slots = pack_slots(pair_terms, folded)
    clip_at = jnp.arange(clip_count, dtype=jnp.int32)[:, None]

    def clip_sums(values):
        first_sum = jnp.sum(jnp.where(first_clip, values, 0.0), axis=0)[None]
        other_sum = jnp.sum(jnp.where(first_clip, 0.0, values), axis=0)[None]
        return jnp.where(clip_at == 0, first_sum, jnp.where(clip_at == other_clip, other_sum, 0.0))

    def pair_sums(blocks, gains_row):
        wide = jnp.concatenate([clip_sums(values) for values in blocks], axis=1)
        gains_row = jnp.concatenate(
            [gains_row, jnp.zeros((wide.shape[1] - gains_row.shape[0],), FLOAT)]
        )
        wide = jnp.concatenate([wide, gains_row[None]], axis=0)
        return wide + swapped(wide)

    back_parts = return_slots(back_slots)
    text_low, ky_sums = local_call(
        functools.partial(text_back_kernel, len(text_terms)),
        (*text_terms, text_raw, ky_gain),
        [part_shape, jax.ShapeDtypeStruct((8, 128), FLOAT)],
    )
    qkv_grad, gain_sums = rope_backward(far, back_parts, qkv_raw, cosine, sine, gains, heads)
    qkv_grad, text_low = tie(qkv_grad, text_low)
    normed_part = dot_turned(qkv_grad, qkv_full)
    qkv_right = qkv_grad[None]
    last_grads = outer_products(
        [*last_left[0], qkv_right, flip(qkv_right, 1)],
        [*last_left[1], mixed_right, mixed_other],
        local_width,
    )
    text_arrived = return_slots([text_low] * SPLIT)
    normed_part, last_grads, text_arrived = tie(normed_part, last_grads, text_arrived)
    last_grads, feed_low = tie(last_grads, feed_low)
    last_low = scatter(last_grads)
    grad_normed_one = own_rows(normed_part)
    _, pull_one = jax.vjp(modulated, input_rows, first_gain, shift_one, scale_one)
    back_one, grad_first_gain, grad_shift_one, grad_scale_one = pull_one(grad_normed_one)
    grad_inputs = grad_after + back_one
    head_sums = (1.0 - gate_heads * gate_heads) * jnp.sum(gate_parts, axis=(1, 2))
    head_row = lax.dynamic_update_slice_in_dim(
        jnp.zeros((head_gate.shape[0],), FLOAT),
        head_sums,
        tensor_index * heads + far_index * each,
        0,
    )
    gain_halves = gain_sums[:2, :head_size] + gain_sums[:2, head_size:]
    all_pairs = pair_sums(
        (
            grad_shift_one,
            grad_scale_one,
            grad_gate_one,
            grad_shift_two,
            grad_scale_two,
            grad_gate_two,
        ),
        jnp.concatenate(
            [
                grad_first_gain,
                grad_second_gain,
                gain_halves.reshape(-1),
                ky_sums[0, :head_size],
                head_row,
            ]
        ),
    )
    text_wide = small_call(
        text_join_kernel,
        (far, *text_arrived),
        [jax.ShapeDtypeStruct((group_rows, 2 * local_width), LOW)],
        [],
    )[0]
    text_all = spread(text_wide)
    all_pairs, text_all = tie(all_pairs, text_all)
    grad_sums = sum_dp(all_pairs)
    grad_mod_low, sums = grad_sums[:clip_count].astype(LOW), grad_sums[clip_count]
    first_gain_sum = sums[:width]
    second_gain_sum = sums[width : 2 * width]
    at = 2 * width
    q_gain_sum = sums[at : at + head_size]
    k_gain_sum = sums[at + head_size : at + 2 * head_size]
    ky_gain_sum = sums[at + 2 * head_size : at + 3 * head_size]
    gate_sum = sums[at + 3 * head_size : at + 3 * head_size + head_gate.shape[0]]
    grad_text_kv = (
        matmul(text_near, text_all, 0, 0)
        .reshape(-1, SPLIT, each, 2, head_size)
        .transpose(3, 0, 1, 2, 4)
        .reshape(2, -1, local_width)
    )
    grad_text_part = dot_turned(text_all, text_weight).astype(LOW)
    grad_text_pair = grad_text_part.astype(FLOAT) + swapped(grad_text_part).astype(FLOAT)
    grad_text_groups = grad_text_pair.astype(LOW).reshape(near, group_rows, -1)
    orders = jnp.arange(near, dtype=jnp.int32)
    flip_at = jnp.array(flips, jnp.int32)
    grad_text_rows = jnp.concatenate(
        [
            pick(grad_text_groups, jnp.sum(jnp.where(flip_at == near_index ^ group, orders, 0)))
            for group in range(near)
        ],
        axis=0,
    )
    grad_text_all = lax.all_to_all(grad_text_rows, "dp", split_axis=0, concat_axis=1, tiled=True)
    half_text = text_tokens.shape[1] // 2
    grad_text = lax.dynamic_slice_in_dim(
        grad_text_all, tensor_index * half_text, half_text, 1
    ).astype(FLOAT)
    grad_ada_bias = jnp.sum(grad_mod_low.astype(FLOAT), axis=0)
    grad_ada = matmul(silu_slice, grad_mod_low, 0, 0)
    cond_part = lax.dynamic_update_slice_in_dim(
        jnp.zeros(cond_float.shape, FLOAT),
        dot_turned(grad_mod_low, ada_weight),
        dp_index * cond_rows,
        1,
    )
    cond_sigmoid = jax.nn.sigmoid(cond_float)
    grad_conditioning = (
        sum_dp(cond_part) * cond_sigmoid * (1.0 + cond_float * (1.0 - cond_sigmoid))
    )
    last_shard = last_low.astype(FLOAT)
    qkv_shard = last_shard[:, : 3 * local_width].reshape(weight_rows, 3, local_width).transpose(1, 0, 2)
    feed_shard = feed_low.astype(FLOAT)
    gate_up_shard = jnp.stack(
        [feed_shard[:, :hidden_count], feed_shard[:, hidden_count : 2 * hidden_count]]
    )
    out_shard = last_shard[:, 3 * local_width :]
    down_shard = feed_shard[:, 2 * hidden_count : 3 * hidden_count]
    return (
        output,
        grad_inputs,
        grad_text,
        grad_conditioning,
        grad_ada,
        grad_ada_bias,
        first_gain_sum,
        q_gain_sum,
        k_gain_sum,
        ky_gain_sum,
        gate_sum,
        qkv_shard,
        out_shard.T,
        grad_text_kv,
        second_gain_sum,
        gate_up_shard,
        down_shard.T,
    )


def solution(mesh):
    placed = (
        P(("dp", "tensor"), None),
        P("dp"),
        P("dp"),
        P("dp", None),
        P(),
        P("dp", None),
        P(),
        P(),
        P(),
        P(),
        P(),
        P(),
        P(None, "dp", "tensor"),
        P("tensor", "dp"),
        P(None, "dp", "tensor"),
        P(),
        P(None, "dp", "tensor"),
        P("tensor", "dp"),
        P(("dp", "tensor"), None),
    )
    return jax.shard_map(
        shards,
        mesh=mesh,
        in_specs=placed,
        out_specs=(
            P(("dp", "tensor"), None),
            P(("dp", "tensor"), None),
            P("dp", "tensor"),
            P(),
            P("dp", None),
            P(),
            P(),
            P(),
            P(),
            P(),
            P(),
            P(None, "dp", "tensor"),
            P("tensor", "dp"),
            P(None, "dp", "tensor"),
            P(),
            P(None, "dp", "tensor"),
            P("tensor", "dp"),
        ),
        check_vma=False,
    )
```
